32 devices in a mesh: item: 4 (over y, x), lat: 8 (over z, core).
Axes of the slice: x: 2, y: 2, z: 4, core: 2. Of those that a mesh axis runs over, the one named last changes fastest.
Arguments:
- noisy_state: float32 [4, 83, 8192], P('item', None, 'lat'), may hold values from -6 to 6
- target_state: float32 [4, 83, 8192], P('item', None, 'lat'), may hold values from -6 to 6
- sigmas: float32 [4], P('item'), may hold values from 0.5 to 8
- sh_basis: float32 [64, 8192], P(None, 'lat'), may hold values from -0.0625 to 0.0625
- lengths: int32 [4, 16], P('item'), may hold values from 1 to 4096, 8192 in all within a row
- grid_edges: int32 [8192, 4], P('lat'), may hold values from 0 to 1023
- mesh_edges: int32 [8192, 16], P('lat'), may hold values from 0 to 3071
- dec_edges: int32 [8192, 3], P('lat'), may hold values from 0 to 3071
- tables_copy: bfloat16 [2, 83, 512], replicated, may hold values from -0.625 to 0.625
- tables_master: float32 [2, 83, 512], P(None, None, 'lat'), may hold values from -0.625 to 0.625
- tables_first: float32 [2, 83, 512], P(None, None, 'lat'), may hold values from -1 to 1, as said below
- tables_second: float32 [2, 83, 512], P(None, None, 'lat'), may hold values from 0 to 1, as said below
- tables_ema: float32 [2, 83, 512], P(None, None, 'lat'), may hold values from -0.625 to 0.625
- attn_copy: bfloat16 [512, 2048], replicated, may hold values from -0.25 to 0.25
- attn_master: float32 [512, 2048], P('lat'), may hold values from -0.25 to 0.25
- attn_first: float32 [512, 2048], P('lat'), may hold values from -1 to 1, as said below
- attn_second: float32 [512, 2048], P('lat'), may hold values from 0 to 1, as said below
- attn_ema: float32 [512, 2048], P('lat'), may hold values from -0.25 to 0.25
- mlp_copy: bfloat16 [3, 512, 4096], replicated, may hold values from -0.25 to 0.25
- mlp_master: float32 [3, 512, 4096], P(None, 'lat'), may hold values from -0.25 to 0.25
- mlp_first: float32 [3, 512, 4096], P(None, 'lat'), may hold values from -1 to 1, as said below
- mlp_second: float32 [3, 512, 4096], P(None, 'lat'), may hold values from 0 to 1, as said below
- mlp_ema: float32 [3, 512, 4096], P(None, 'lat'), may hold values from -0.25 to 0.25
- gains_copy: bfloat16 [5, 512], replicated, may hold values from 0.5 to 6, as said below
- gains_master: float32 [5, 512], P(None, 'lat'), may hold values from 0.5 to 6, as said below
- gains_first: float32 [5, 512], P(None, 'lat'), may hold values from -1 to 1, as said below
- gains_second: float32 [5, 512], P(None, 'lat'), may hold values from 0 to 1, as said below
- gains_ema: float32 [5, 512], P(None, 'lat'), may hold values from 0.2 to 6, as said below
Outputs:
- loss_sum: float32 [], replicated
- grad_norm: float32 [], replicated
- tables_first_new: float32 [2, 83, 512], P(None, None, 'lat')
- tables_second_new: float32 [2, 83, 512], P(None, None, 'lat')
- tables_master_new: float32 [2, 83, 512], P(None, None, 'lat')
- tables_ema_new: float32 [2, 83, 512], P(None, None, 'lat')
- tables_copy_new: bfloat16 [2, 83, 512], P(None, None, 'lat')
- attn_first_new: float32 [512, 2048], P('lat')
- attn_second_new: float32 [512, 2048], P('lat')
- attn_master_new: float32 [512, 2048], P('lat')
- attn_ema_new: float32 [512, 2048], P('lat')
- attn_copy_new: bfloat16 [512, 2048], P('lat')
- mlp_first_new: float32 [3, 512, 4096], P(None, 'lat')
- mlp_second_new: float32 [3, 512, 4096], P(None, 'lat')
- mlp_master_new: float32 [3, 512, 4096], P(None, 'lat')
- mlp_ema_new: float32 [3, 512, 4096], P(None, 'lat')
- mlp_copy_new: bfloat16 [3, 512, 4096], P(None, 'lat')
- gains_first_new: float32 [5, 512], P(None, 'lat')
- gains_second_new: float32 [5, 512], P(None, 'lat')
- gains_master_new: float32 [5, 512], P(None, 'lat')
- gains_ema_new: float32 [5, 512], P(None, 'lat')
- gains_copy_new: bfloat16 [5, 512], P(None, 'lat')
The draws below stay inside these ranges and needn't reach their ends.
Inputs may be any that keep to these rules, and one draw needn't show every extreme that they name: The lengths of an item sum to 8192. `tables_first`: first moments of both signs. `tables_second`: Positive. `attn_first`: first moments of both signs. `attn_second`: Positive. `mlp_first`: first moments of both signs. `mlp_second`: Positive. `gains_first`: first moments of both signs. `gains_second`: Positive. `gains_copy`: Positive. `gains_master`: Positive. `gains_ema`: Positive.
All inputs are finite; a program needn't handle non-finite values.
Results may differ from the reference program's by a relative error of at most 0.0076.
Values may be sent and summed in bfloat16 or wider, within the bound.
No kernel may reach another device: no remote copies, remote signals or barrier semaphores. Data moves between devices by JAX's collectives and lax.ppermute only.
A program may use at most 512 MiB of HBM per device.

```python
import math
import jax
import jax.numpy as jnp
import numpy as np
from jax import lax

C = 83
LATENT_WIDTH = 512
HEADS = 4
HEAD_SIZE = 128
FF = 2048
M_DEV = 1024
G_DEV = 1024
NB = 16
EG = 4
EM = 3
CROPS = 16
STEP = 10
ITEMS = 4
NMESH = 8192
GRID = 8192
KSH = 64
NPARAM = 7427584


CLIP_LEVEL = 1.0


GAIN_FACTOR = 2.0


def entry_size(scale_factor):
    return scale_factor * CLIP_LEVEL / NPARAM ** 0.5


def first_moment(key, shape, scale_factor):
    return jax.random.normal(key, shape, jnp.float32) * (entry_size(scale_factor) * 0.1 / 0.9)


def second_moment(key, shape, scale_factor):
    spread = jnp.exp(jax.random.uniform(key, shape, jnp.float32, math.log(0.5), math.log(8.0)))
    size = entry_size(scale_factor)
    return spread * (size * size * 0.001 / 0.999)


def gain_rows(key, rise, low_end, high_end):
    place = jnp.arange(LATENT_WIDTH, dtype=jnp.float32) / (LATENT_WIDTH - 1.0)
    noise = jax.random.uniform(key, (5, LATENT_WIDTH), jnp.float32, low_end, high_end)
    return (1.0 + rise * place)[None, :] * noise


def draw_gains_copy(key, part):
    key = jax.random.fold_in(key, 11)
    return gain_rows(key, 2.0, 0.85, 1.15).astype(jnp.bfloat16)


def draw_gains_master(key, part):
    key = jax.random.fold_in(key, 12)
    return gain_rows(key, 2.0, 0.85, 1.15)


def draw_gains_ema(key, part):
    key = jax.random.fold_in(key, 13)
    return gain_rows(key, 2.0, 0.3, 0.7)


def draw_tables_first(key, part):
    key = jax.random.fold_in(key, 21)
    return first_moment(key, (2, C, LATENT_WIDTH), 1.0)


def draw_tables_second(key, part):
    key = jax.random.fold_in(key, 22)
    return second_moment(key, (2, C, LATENT_WIDTH), 1.0)


def draw_attn_first(key, part):
    key = jax.random.fold_in(key, 23)
    return first_moment(key, (LATENT_WIDTH, 4 * LATENT_WIDTH), 1.0)


def draw_attn_second(key, part):
    key = jax.random.fold_in(key, 24)
    return second_moment(key, (LATENT_WIDTH, 4 * LATENT_WIDTH), 1.0)


def draw_mlp_first(key, part):
    key = jax.random.fold_in(key, 25)
    return first_moment(key, (3, LATENT_WIDTH, 2 * FF), 1.0)


def draw_mlp_second(key, part):
    key = jax.random.fold_in(key, 26)
    return second_moment(key, (3, LATENT_WIDTH, 2 * FF), 1.0)


def draw_gains_first(key, part):
    key = jax.random.fold_in(key, 27)
    return first_moment(key, (5, LATENT_WIDTH), GAIN_FACTOR)


def draw_gains_second(key, part):
    key = jax.random.fold_in(key, 28)
    return second_moment(key, (5, LATENT_WIDTH), GAIN_FACTOR)


def touch_ends(result, key, smallest, top_value):
    index_at = [jax.random.randint(jax.random.fold_in(key, axis), (), 0, length) for axis, length in enumerate(result.shape)]
    main_axis = result.shape.index(max(result.shape))
    neighbour = index_at[:main_axis] + [(index_at[main_axis] + 1) % result.shape[main_axis]] + index_at[main_axis + 1:]
    return result.at[tuple(index_at)].set(smallest).at[tuple(neighbour)].set(top_value)


def levels(key, shape, cuts, least, largest):
    gain, own = 1.0, jax.random.fold_in(key, 6)
    for axis_at, parts in cuts:
        draws = jnp.exp(jax.random.uniform(jax.random.fold_in(own, axis_at), (parts,), jnp.float32, least / len(cuts), largest / len(cuts)))
        gain = gain * jnp.repeat(draws, shape[axis_at] // parts).reshape([-1 if axis == axis_at else 1 for axis in range(len(shape))])
    return gain


def split_up(amount, total, bound, skew):
    weights = [(1 << 20) // math.isqrt(rank ** skew) + 1 for rank in range(2, amount + 1)]
    spare, given = total - bound - (amount - 1), [1] * (amount - 1)
    while spare > 0:
        candidates = [i for i in range(amount - 1) if given[i] < bound]
        pool, left = sum([weights[i] for i in candidates]), spare
        for i in candidates:
            addition = min(bound - given[i], max(1, left * weights[i] // pool), spare)
            given[i] = given[i] + addition
            spare = spare - addition
    return np.array([bound] + given)


def ragged_sizes(stream_key, amount, total, limit, skew):
    if amount == 2:
        one = jax.random.randint(stream_key, (), max(1, total - limit), min(limit, total - 1) + 1)
        return jnp.stack([one, total - one])
    tallies = jnp.asarray(split_up(amount, total, limit, skew), jnp.int32)
    pairs = (amount - 1) // 2
    donor, taker = tallies[1:1 + 2 * pairs:2], tallies[2:2 + 2 * pairs:2]
    room = jnp.minimum(donor - 1, limit - taker)
    moved = jax.random.randint(jax.random.fold_in(stream_key, 1), (pairs,), 0, 1 << 20) % (room + 1)
    tallies = tallies.at[1:1 + 2 * pairs:2].set(donor - moved).at[2:2 + 2 * pairs:2].set(taker + moved)
    return tallies[jax.random.permutation(jax.random.fold_in(stream_key, 2), amount)]


def centred(stream_key, dims, scale, limit, cuts=(), kind=jnp.bfloat16):
    gain = levels(stream_key, dims, cuts, -0.22, 0.18) if cuts else 1.0
    values = jax.random.normal(stream_key, dims, jnp.float32) * scale * gain
    return jnp.minimum(jnp.maximum(values, -limit), limit).astype(kind)


def setup_inputs(seed: int = 0) -> dict:
    key_of = jax.random.split(jax.random.key(seed), 29)
    noisy_state = centred(key_of[0], (ITEMS, C, GRID), 1.0, 6.0, ((0, 4), (2, 8)), jnp.float32)
    target_state = centred(key_of[1], (ITEMS, C, GRID), 1.0, 6.0, ((0, 4), (2, 8)), jnp.float32)
    sigmas = jnp.clip(jnp.exp(math.log(8.0) - 2.7725887 * jax.random.uniform(key_of[2], (ITEMS,), jnp.float32) ** levels(key_of[2], (ITEMS,), ((0, 4),), -0.2, 0.2)), 0.5, 8.0)
    sh_basis = centred(key_of[3], (KSH, GRID), GRID ** -0.5, 0.0625, ((1, 8),), jnp.float32)
    lengths = jax.vmap(lambda own: ragged_sizes(own, CROPS, NMESH, NMESH // 2, 2))(jax.random.split(key_of[4], ITEMS)).reshape((ITEMS, CROPS)).astype(jnp.int32)
    grid_edges = touch_ends(jax.random.randint(key_of[5], (NMESH, EG), 0, G_DEV), jax.random.fold_in(key_of[5], 1), 0, G_DEV - 1).astype(jnp.int32)
    mesh_edges = touch_ends(jax.random.randint(key_of[6], (NMESH, NB), 0, 3 * M_DEV), jax.random.fold_in(key_of[6], 1), 0, (3 * M_DEV) - 1).astype(jnp.int32)
    dec_edges = touch_ends(jax.random.randint(key_of[7], (GRID, EM), 0, 3 * M_DEV), jax.random.fold_in(key_of[7], 1), 0, (3 * M_DEV) - 1).astype(jnp.int32)
    tables_copy = centred(key_of[8], (2, C, LATENT_WIDTH), C ** -0.5, 0.625)
    tables_master = centred(key_of[9], (2, C, LATENT_WIDTH), C ** -0.5, 0.625, ((2, 8),), jnp.float32)
    tables_first = draw_tables_first(jax.random.fold_in(key_of[28], 71), 0)
    tables_second = draw_tables_second(jax.random.fold_in(key_of[28], 71), 0)
    tables_ema = centred(key_of[12], (2, C, LATENT_WIDTH), C ** -0.5, 0.625, ((2, 8),), jnp.float32)
    attn_copy = centred(key_of[13], (LATENT_WIDTH, 4 * LATENT_WIDTH), LATENT_WIDTH ** -0.5, 0.25)
    attn_master = centred(key_of[14], (LATENT_WIDTH, 4 * LATENT_WIDTH), LATENT_WIDTH ** -0.5, 0.25, ((0, 8),), jnp.float32)
    attn_first = draw_attn_first(jax.random.fold_in(key_of[28], 71), 0)
    attn_second = draw_attn_second(jax.random.fold_in(key_of[28], 71), 0)
    attn_ema = centred(key_of[17], (LATENT_WIDTH, 4 * LATENT_WIDTH), LATENT_WIDTH ** -0.5, 0.25, ((0, 8),), jnp.float32)
    mlp_copy = centred(key_of[18], (3, LATENT_WIDTH, 2 * FF), LATENT_WIDTH ** -0.5, 0.25)
    mlp_master = centred(key_of[19], (3, LATENT_WIDTH, 2 * FF), LATENT_WIDTH ** -0.5, 0.25, ((1, 8),), jnp.float32)
    mlp_first = draw_mlp_first(jax.random.fold_in(key_of[28], 71), 0)
    mlp_second = draw_mlp_second(jax.random.fold_in(key_of[28], 71), 0)
    mlp_ema = centred(key_of[22], (3, LATENT_WIDTH, 2 * FF), LATENT_WIDTH ** -0.5, 0.25, ((1, 8),), jnp.float32)
    gains_copy = draw_gains_copy(jax.random.fold_in(key_of[28], 71), 0)
    gains_master = draw_gains_master(jax.random.fold_in(key_of[28], 71), 0)
    gains_first = draw_gains_first(jax.random.fold_in(key_of[28], 71), 0)
    gains_second = draw_gains_second(jax.random.fold_in(key_of[28], 71), 0)
    gains_ema = draw_gains_ema(jax.random.fold_in(key_of[28], 71), 0)
    return {"noisy_state": noisy_state, "target_state": target_state, "sigmas": sigmas, "sh_basis": sh_basis, "lengths": lengths, "grid_edges": grid_edges, "mesh_edges": mesh_edges, "dec_edges": dec_edges, "tables_copy": tables_copy, "tables_master": tables_master, "tables_first": tables_first, "tables_second": tables_second, "tables_ema": tables_ema, "attn_copy": attn_copy, "attn_master": attn_master, "attn_first": attn_first, "attn_second": attn_second, "attn_ema": attn_ema, "mlp_copy": mlp_copy, "mlp_master": mlp_master, "mlp_first": mlp_first, "mlp_second": mlp_second, "mlp_ema": mlp_ema, "gains_copy": gains_copy, "gains_master": gains_master, "gains_first": gains_first, "gains_second": gains_second, "gains_ema": gains_ema}


@jax.custom_vjp
def low(v):
    return lax.optimization_barrier(v.astype(jnp.bfloat16)).astype(jnp.float32)

@jax.custom_vjp
def low_back(v):
    return v

def low_keep(v):
    return (low(v), None)

def low_pass(kept, grad):
    return (grad,)

def back_keep(v):
    return (v, None)

def back_low(kept, grad):
    return (low(grad),)
low.defvjp(low_keep, low_pass)
low_back.defvjp(back_keep, back_low)
EPS_NORM = 1e-05
CLIP_LEVEL = 1.0
BETA_ONE = 0.9
BETA_TWO = 0.999
ADAM_EPS = 1e-08
EMA_DECAY = 0.9
RATE_MATRIX = 0.05
RATE_GAIN = 0.3
WEIGHT_DECAY = 0.1
HIGH_PRECISION = lax.Precision.HIGHEST

def product(left, right):
    return jnp.matmul(left, right, precision=HIGH_PRECISION)

def layer_norm(values, gain_row):
    center = values - lax.optimization_barrier(jnp.mean(values, axis=-1, keepdims=True))
    spread = lax.optimization_barrier(jnp.mean(center * center, axis=-1, keepdims=True))
    return center * lax.rsqrt(spread + EPS_NORM) * gain_row

def feed_forward(values, gain_row, weights):
    normed = low(layer_norm(values, gain_row))
    before = low_back(product(normed, weights[:, :FF]))
    active = low(jax.nn.gelu(before))
    return values + low_back(product(active, weights[:, FF:].T))

def crop_of(crop_ends, nodes):
    return lax.optimization_barrier(jnp.sum((crop_ends <= nodes[..., None]).astype(jnp.int32), axis=-1))

def item_loss(params, noisy_field, target_field, noise_level, item_lengths, grid_edges, mesh_edges, dec_edges, sh_basis):
    tables, attn, mlp, gains = params
    node_count = mesh_edges.shape[0]
    grid_count = noisy_field.shape[1]
    square = noise_level * noise_level
    scale_in = lax.rsqrt(square + 1.0)
    scale_skip = 1.0 / (square + 1.0)
    scale_out = noise_level * scale_in
    weight_loss = (square + 1.0) / square
    inputs = low(scale_in * noisy_field)
    embedded = low_back(product(inputs.T, tables[0]))
    node_ids = jnp.arange(node_count)
    band_ids = node_ids // M_DEV
    grid_ids = band_ids[:, None] * G_DEV + grid_edges
    pooled = lax.optimization_barrier(jnp.mean(embedded[grid_ids], axis=1))
    encoded = feed_forward(pooled, gains[0], mlp[0])
    project = low(low_back(product(low(layer_norm(encoded, gains[1])), attn[:, :3 * LATENT_WIDTH])))
    queries = project[:, :LATENT_WIDTH]
    key_all = project[:, LATENT_WIDTH:2 * LATENT_WIDTH]
    value_all = project[:, 2 * LATENT_WIDTH:]
    crop_ends = jnp.cumsum(item_lengths)
    global_ids = (band_ids[:, None] - 1) * M_DEV + mesh_edges
    inside = (global_ids >= 0) & (global_ids < node_count)
    safe_ids = jnp.clip(global_ids, 0, node_count - 1)
    allowed = inside & (crop_of(crop_ends, safe_ids) == crop_of(crop_ends, node_ids)[:, None])
    blocks = node_count // M_DEV

    def block_attend(pieces):
        query_blk, key_blk, value_blk, ids_blk, ok_blk = pieces
        input_rows = query_blk.shape[0]
        key_near = jnp.concatenate([key_blk[:, None], key_all[ids_blk]], axis=1)
        value_near = jnp.concatenate([value_blk[:, None], value_all[ids_blk]], axis=1)
        usable = jnp.concatenate([jnp.ones((input_rows, 1), jnp.bool_), ok_blk], axis=1)
        split_query_heads = query_blk.reshape(input_rows, HEADS, HEAD_SIZE)
        key_head_rows = key_near.reshape(input_rows, -1, HEADS, HEAD_SIZE)
        value_head_rows = value_near.reshape(input_rows, -1, HEADS, HEAD_SIZE)
        score_matrix = low_back(jnp.einsum('yza,yvza->yzv', split_query_heads, key_head_rows, precision=HIGH_PRECISION) * HEAD_SIZE ** (-0.5))
        score_matrix = jnp.where(usable[:, None, :], score_matrix, -1e+30)
        attention_probabilities = low(jax.nn.softmax(score_matrix, axis=-1))
        return jnp.einsum('piv,pviu->piu', attention_probabilities, value_head_rows, precision=HIGH_PRECISION).reshape(input_rows, LATENT_WIDTH)
    attended_values = lax.map(jax.checkpoint(block_attend), (queries.reshape(blocks, M_DEV, LATENT_WIDTH), key_all.reshape(blocks, M_DEV, LATENT_WIDTH), value_all.reshape(blocks, M_DEV, LATENT_WIDTH), safe_ids.reshape(blocks, M_DEV, -1), allowed.reshape(blocks, M_DEV, -1)))
    attended_values = low(low_back(attended_values.reshape(node_count, LATENT_WIDTH)))
    residual = encoded + low_back(product(attended_values, attn[:, 3 * LATENT_WIDTH:]))
    latent = feed_forward(residual, gains[2], mlp[1])
    sent = low(latent)
    grid_band = jnp.arange(grid_count) // G_DEV
    mesh_ids = (grid_band[:, None] - 1) * M_DEV + dec_edges
    mesh_inside = (mesh_ids >= 0) & (mesh_ids < node_count)
    terms = jnp.where(mesh_inside[:, :, None], sent[jnp.clip(mesh_ids, 0, node_count - 1)], 0.0)
    gathered = lax.optimization_barrier(jnp.mean(terms, axis=1))
    decoded = feed_forward(embedded + gathered, gains[3], mlp[2])
    output = low_back(product(tables[1], low(layer_norm(decoded, gains[4])).T))
    error_field = scale_skip * noisy_field + scale_out * output - target_field
    coeffs = product(error_field, sh_basis.T)
    return weight_loss * jnp.sum(coeffs * coeffs)

def adam_update(gradient, master, moment_one, moment_two, average, step_rate, decay_rate):
    one_new = BETA_ONE * moment_one + (1.0 - BETA_ONE) * gradient
    two_new = BETA_TWO * moment_two + (1.0 - BETA_TWO) * gradient * gradient
    one_hat = one_new / (1.0 - BETA_ONE ** STEP)
    two_hat = two_new / (1.0 - BETA_TWO ** STEP)
    master_new = master - step_rate * (one_hat / (jnp.sqrt(two_hat) + ADAM_EPS) + decay_rate * master)
    average_new = EMA_DECAY * average + (1.0 - EMA_DECAY) * master_new
    return (one_new, two_new, master_new, average_new, master_new.astype(jnp.bfloat16))

def reference(noisy_state, target_state, sigmas, sh_basis, lengths, grid_edges, mesh_edges, dec_edges, tables_copy, tables_master, tables_first, tables_second, tables_ema, attn_copy, attn_master, attn_first, attn_second, attn_ema, mlp_copy, mlp_master, mlp_first, mlp_second, mlp_ema, gains_copy, gains_master, gains_first, gains_second, gains_ema):
    weights = (tables_copy.astype(jnp.float32), attn_copy.astype(jnp.float32), mlp_copy.astype(jnp.float32), gains_copy.astype(jnp.float32))

    def total(params):
        loss_total = jnp.zeros((), jnp.float32)
        for item_index in range(ITEMS):
            loss_total = loss_total + jax.checkpoint(item_loss)(params, noisy_state[item_index], target_state[item_index], sigmas[item_index], lengths[item_index], grid_edges, mesh_edges, dec_edges, sh_basis)
        return loss_total
    loss_sum, pull_back = jax.vjp(total, weights)
    gradients = pull_back(jnp.ones_like(loss_sum))[0]
    grad_norm = jnp.sqrt(sum((jnp.sum(grad_part * grad_part) for grad_part in gradients)))
    scale_factor = CLIP_LEVEL / jnp.maximum(grad_norm, CLIP_LEVEL)
    tab = adam_update(scale_factor * gradients[0], tables_master, tables_first, tables_second, tables_ema, RATE_MATRIX, WEIGHT_DECAY)
    att = adam_update(scale_factor * gradients[1], attn_master, attn_first, attn_second, attn_ema, RATE_MATRIX, WEIGHT_DECAY)
    mlps = adam_update(scale_factor * gradients[2], mlp_master, mlp_first, mlp_second, mlp_ema, RATE_MATRIX, WEIGHT_DECAY)
    gns = adam_update(scale_factor * gradients[3], gains_master, gains_first, gains_second, gains_ema, RATE_GAIN, 0.0)
    return (loss_sum, grad_norm, tab[0], tab[1], tab[2], tab[3], tab[4], att[0], att[1], att[2], att[3], att[4], mlps[0], mlps[1], mlps[2], mlps[3], mlps[4], gns[0], gns[1], gns[2], gns[3], gns[4])
```

```python
import functools

import jax
import jax.numpy as jnp
from jax import lax
from jax.experimental import pallas as pl
from jax.experimental.pallas import tpu as pltpu
from jax.sharding import PartitionSpec as P

HEADS = 4
STEP = 10

EPS_NORM = 1e-05
CLIP_LEVEL = 1.0
BETA_ONE = 0.9
BETA_TWO = 0.999
ADAM_EPS = 1e-08
EMA_DECAY = 0.9
RATE_MATRIX = 0.05
RATE_GAIN = 0.3
WEIGHT_DECAY = 0.1
HIGH_PRECISION = lax.Precision.HIGHEST

F32 = jnp.float32
BF16 = jnp.bfloat16
LOG2E = 1.4426950408889634
CHANNEL_PAD = 128
ROWS = 256
VMEM_BYTES = 60 * 1024 * 1024


def dot(left, right, left_dim, right_dim):
    return lax.dot_general(
        left, right, (((left_dim,), (right_dim,)), ((), ())), preferred_element_type=F32
    )


def call(kernel, grid, outs, in_specs, out_specs, operands, scratch=(), flops=0, moved=0):
    return pl.pallas_call(
        kernel,
        grid=grid,
        out_shape=outs,
        in_specs=in_specs,
        out_specs=out_specs,
        scratch_shapes=list(scratch),
        cost_estimate=pl.CostEstimate(flops=flops, bytes_accessed=moved, transcendentals=0),
        compiler_params=pltpu.CompilerParams(vmem_limit_bytes=VMEM_BYTES),
    )(*operands)


def whole(shape):
    return pl.BlockSpec(shape, lambda *_: (0,) * len(shape))


def rows_of(width, rows=ROWS):
    return pl.BlockSpec((rows, width), lambda i: (i, 0))


def lanes_of(height, lanes=ROWS):
    return pl.BlockSpec((height, lanes), lambda i: (0, i))


def shape(dims, kind):
    return jax.ShapeDtypeStruct(dims, kind)


def norm_parts(values):
    center = values - jnp.mean(values, axis=-1, keepdims=True)
    spread = jnp.mean(center * center, axis=-1, keepdims=True)
    inverse = lax.rsqrt(spread + EPS_NORM)
    return center * inverse, inverse


def norm_back(upstream, values, gain_row):
    unit, inverse = norm_parts(values)
    scaled = upstream * gain_row
    along = jnp.mean(scaled * unit, axis=-1, keepdims=True)
    grad = inverse * (scaled - jnp.mean(scaled, axis=-1, keepdims=True) - unit * along)
    gain_grad = jnp.sum(upstream * unit, axis=0, keepdims=True)
    return grad, gain_grad


def gelu_parts(u):
    root = 0.7978845608028654
    cubic = 0.044715
    square = u * u
    t = jnp.tanh(root * u * (1.0 + cubic * square))
    half = 0.5 * (1.0 + t)
    slope = half + 0.5 * u * (1.0 - t * t) * (root + (3.0 * root * cubic) * square)
    return u * half, slope


def mlp_forward(values, gain_row, w_ref, normed_ref, slope_ref, active_ref, step=512):
    hidden = w_ref.shape[-1] // 2
    normed = (norm_parts(values)[0] * gain_row).astype(BF16)
    normed_ref[...] = normed
    result = jnp.zeros(values.shape, F32)
    for start in range(0, hidden, step):
        part = slice(start, start + step)
        before = dot(normed, w_ref[0, :, part], 1, 0)
        active, slope = gelu_parts(before)
        active = active.astype(BF16)
        slope_ref[:, part] = slope
        active_ref[:, part] = active
        result = result + dot(active, w_ref[0, :, hidden + start : hidden + start + step], 1, 1)
    return values + result


def mlp_backward(upstream, values, gain_row, w_ref, slope_ref, rounded_ref, before_ref, step=512):
    hidden = w_ref.shape[-1] // 2
    rounded = upstream.astype(BF16)
    rounded_ref[...] = rounded
    grad_normed = jnp.zeros(values.shape, F32)
    for start in range(0, hidden, step):
        part = slice(start, start + step)
        grad_active = dot(rounded, w_ref[0, :, hidden + start : hidden + start + step], 1, 0)
        grad_before = (grad_active * slope_ref[:, part]).astype(BF16)
        before_ref[:, part] = grad_before
        grad_normed = grad_normed + dot(grad_before, w_ref[0, :, part], 1, 1)
    grad, gain_grad = norm_back(grad_normed, values, gain_row)
    return upstream + grad, gain_grad


def two_parts(values):
    high = values.astype(BF16)
    return high, (values - high.astype(F32)).astype(BF16)


def add_up(ref, value):
    step = pl.program_id(0)

    @pl.when(step == 0)
    def _():
        ref[...] = value

    @pl.when(step > 0)
    def _():
        ref[...] += value


def encoder_kernel(
    edges, x, table, gains, mlp, attn,
    pin_ref, pooled_ref, encoded_ref, normed_ref, slope_ref, active_ref, normed_attn_ref, q_ref, kv_ref,
):
    rows, count = edges.shape
    width = attn.shape[0]
    lanes = lax.broadcasted_iota(jnp.int32, (rows, x.shape[1]), 1)
    tally = jnp.zeros(lanes.shape, F32)
    for j in range(count):
        tally = tally + jnp.where(edges[:, j : j + 1] == lanes, 1.0, 0.0)
    pin = dot(tally.astype(BF16), x[...], 1, 1) / count
    high, low = two_parts(pin)
    pin_ref[...] = jnp.concatenate([high, low], axis=1)
    pooled = dot(high, table[0], 1, 0) + dot(low, table[0], 1, 0)
    pooled_ref[...] = pooled
    encoded = mlp_forward(pooled, gains[0:1], mlp, normed_ref, slope_ref, active_ref)
    encoded_ref[...] = encoded
    normed_attn = (norm_parts(encoded)[0] * gains[1:2]).astype(BF16)
    normed_attn_ref[...] = normed_attn
    q_ref[...] = dot(attn[:, :width], normed_attn, 0, 1).astype(BF16)
    kv_ref[...] = dot(normed_attn, attn[:, width : 3 * width], 1, 0).astype(BF16)


def bias_kernel(places, ends, edges, bias_ref, *, crops):
    count, lanes = edges.shape
    rows = bias_ref.shape[1]
    window = bias_ref.shape[0] * rows
    col = pl.program_id(0)
    nodes = col * lanes + lax.broadcasted_iota(jnp.int32, (1, lanes), 1)
    first = places[0] * rows
    low = jnp.zeros((1, lanes), jnp.int32)
    high = jnp.full((1, lanes), places[1] * rows, jnp.int32)
    for c in range(crops - 1, -1, -1):
        high = jnp.where(ends[c] > first + nodes, ends[c], high)
    for c in range(crops):
        low = jnp.where(ends[c] <= first + nodes, ends[c], low)
    near = edges[...] + (first - rows)
    place = jnp.where((near >= low) & (near < high), edges[...], -1)
    place = jnp.concatenate([place, rows + nodes], axis=0)
    tile = 128
    tiles = window // tile
    each = 6
    fine = jnp.where(place < 0, -1, place % tile)
    coarse = place // tile
    sub = lax.broadcasted_iota(jnp.int32, (tile, lanes), 0)
    for start in range(0, tiles, each):
        here = (coarse >= start) & (coarse < start + each)
        amount = jnp.where(here, jnp.left_shift(1, 5 * jnp.where(here, coarse - start, 0)), 0)
        total = jnp.zeros((tile, lanes), jnp.int32)
        for j in range(count + 1):
            total = total + jnp.where(sub == fine[j : j + 1], amount[j : j + 1], 0)
        for t in range(start, min(tiles, start + each)):
            tally = jnp.bitwise_and(jnp.right_shift(total, 5 * (t - start)), 31)
            value = jnp.where(tally == 0, -1e30, jnp.log2(jnp.maximum(tally, 1).astype(F32)))
            at = t * tile
            bias_ref[at // rows, at % rows : at % rows + tile, :] = value


def attend_kernel(q_ref, k0, k1, k2, v0, v1, v2, bias, o_ref, l_ref, scores, *, chunk):
    depth, lanes = q_ref.shape
    rows = k0.shape[0]
    factor = depth**-0.5 * LOG2E
    q = q_ref[...]
    top = jnp.full((8, lanes), -3e38, F32)
    for w, keys in enumerate((k0, k1, k2)):
        for start in range(0, rows, chunk):
            part = slice(start, start + chunk)
            score = dot(keys[part, :], q, 1, 0) * factor + bias[w, part, :]
            scores[w, part, :] = score
            top = jnp.maximum(top, jnp.max(score.reshape(chunk // 8, 8, lanes), axis=0))
    top = jnp.max(top, axis=0, keepdims=True)
    total = jnp.zeros((8, lanes), F32)
    result = jnp.zeros((depth, lanes), F32)
    for w, values in enumerate((v0, v1, v2)):
        for start in range(0, rows, chunk):
            part = slice(start, start + chunk)
            e = jnp.exp2(scores[w, part, :] - top)
            total = total + jnp.sum(e.reshape(chunk // 8, 8, lanes), axis=0)
            result = result + dot(values[part, :], e.astype(BF16), 0, 0)
    total = jnp.sum(total, axis=0, keepdims=True)
    o_ref[...] = result * (1.0 / total)
    l_ref[...] = jnp.broadcast_to((top + jnp.log2(total))[None], l_ref.shape)


def processor_kernel(
    o_ref, encoded, gains, mlp, attn,
    attended_ref, residual_ref, normed_ref, slope_ref, active_ref, sent_ref,
):
    width = encoded.shape[1]
    attended = o_ref[...].astype(BF16)
    attended_ref[...] = attended
    residual = encoded[...] + dot(attended, attn[:, 3 * width :], 0, 0)
    residual_ref[...] = residual
    latent = mlp_forward(residual, gains[2:3], mlp, normed_ref, slope_ref, active_ref)
    sent_ref[...] = latent.astype(BF16)


def decoder_kernel(
    edges, s0, s1, s2, x, tables, gains, mlp,
    joined_ref, normed_ref, slope_ref, active_ref, decoded_ref, final_ref, output_ref,
):
    lanes_total = s0.shape[0]
    rows, count = edges.shape
    gathered = jnp.zeros(joined_ref.shape, F32)
    lanes = lax.broadcasted_iota(jnp.int32, (rows, lanes_total), 1)
    for w, sent in enumerate((s0, s1, s2)):
        tally = jnp.zeros((rows, lanes_total), F32)
        for j in range(count):
            tally = tally + jnp.where(edges[:, j : j + 1] - w * lanes_total == lanes, 1.0, 0.0)
        gathered = gathered + dot(tally.astype(BF16), sent[...], 1, 0)
    joined = dot(x[...], tables[0], 0, 0) + gathered / count
    joined_ref[...] = joined
    decoded = mlp_forward(joined, gains[3:4], mlp, normed_ref, slope_ref, active_ref)
    decoded_ref[...] = decoded
    final = (norm_parts(decoded)[0] * gains[4:5]).astype(BF16)
    final_ref[...] = final
    output_ref[...] = dot(tables[1], final, 1, 1)


def decoder_back_kernel(
    grad_output, tables, decoded, final, joined, slope, gains, mlp,
    grad_join_ref, rounded_ref, before_ref, table_ref, gain_ref,
):
    grad_final = dot(grad_output[...], tables[1], 0, 0)
    add_up(table_ref, dot(final[...], grad_output[...], 0, 1))
    grad_decoded, gain_final = norm_back(grad_final, decoded[...], gains[4:5])
    grad_join, gain_dec = mlp_backward(
        grad_decoded, joined[...], gains[3:4], mlp, slope, rounded_ref, before_ref
    )
    grad_join_ref[...] = grad_join
    add_up(gain_ref, jnp.concatenate([gain_dec, gain_final], axis=0))


def scatter_kernel(edges, grad, out0, out1, out2, high_ref, low_ref):
    rows = out0.shape[0]
    count = edges.shape[0]
    step = pl.program_id(0)

    @pl.when(step == 0)
    def _():
        high, low = two_parts(grad[...])
        high_ref[...] = high
        low_ref[...] = low

    total = grad.shape[0]
    for w, out in enumerate((out0, out1, out2)):
        sub = lax.broadcasted_iota(jnp.int32, (rows, total), 0) + (step * rows + w * total)
        tally = jnp.zeros((rows, total), F32)
        for j in range(count):
            tally = tally + jnp.where(edges[j : j + 1, :] == sub, 1.0, 0.0)
        tally = tally.astype(BF16)
        value = dot(tally, high_ref[...], 1, 0) + dot(tally, low_ref[...], 1, 0)
        out[...] = (value / count).astype(out.dtype)


def processor_back_kernel(
    g0, g1, g2, residual, slope, gains, mlp, attn, o_ref,
    grad_residual_ref, rounded_ref, before_ref, gain_ref, branch_ref, grad_o_ref, delta_ref,
):
    width = residual.shape[1]
    upstream = g1[...] + g0[...].astype(F32) + g2[...].astype(F32)
    grad, gain = mlp_backward(
        upstream, residual[...], gains[2:3], mlp, slope, rounded_ref, before_ref
    )
    add_up(gain_ref, gain)
    grad_residual_ref[...] = grad
    branch = grad.astype(BF16)
    branch_ref[...] = branch
    grad_o = dot(attn[:, 3 * width :], branch, 1, 1).astype(BF16)
    grad_o_ref[...] = grad_o
    depth = width // HEADS
    together = grad_o.astype(F32) * o_ref[...]
    for h in range(HEADS):
        row = jnp.sum(together[h * depth : (h + 1) * depth], axis=0, keepdims=True)
        delta_ref[h] = jnp.broadcast_to(row, delta_ref.shape[1:])


def attend_back_kernel(
    q_ref, do_ref, lse_ref, delta_ref, k0, k1, k2, v0, v1, v2, bias,
    dq_ref, out0, out1, out2, p_ref, ds_ref, *, chunk,
):
    block, depth = k0.shape
    scale = depth**-0.5
    factor = scale * LOG2E
    step, h = pl.program_id(0), pl.program_id(1)
    here = pl.ds(pl.multiple_of(h * depth, depth), depth)
    q = q_ref[here, :]
    do = do_ref[here, :]
    lse = lse_ref[h, 0:1, :]
    delta = delta_ref[h, 0:1, :]
    total = jnp.zeros(q.shape, F32)
    for w, (keys, values, out) in enumerate(((k0, v0, out0), (k1, v1, out1), (k2, v2, out2))):
        for start in range(0, block, chunk):
            part = slice(start, start + chunk)
            p = jnp.exp2(dot(keys[part, :], q, 1, 0) * factor + bias[w, part, :] - lse)
            ds = p * (dot(values[part, :], do, 1, 0) - delta)
            p_ref[part, :] = p.astype(BF16)
            ds_ref[part, :] = ds.astype(BF16)
            out[0, :, part] = (dot(q, ds_ref[part, :], 1, 1) * scale).astype(out.dtype)
            out[1, :, part] = dot(do, p_ref[part, :], 1, 1).astype(out.dtype)
            total = total + dot(keys[part, :], ds_ref[part, :], 0, 0)

    @pl.when(step == 0)
    def _():
        dq_ref[here, :] = total * scale

    @pl.when(step > 0)
    def _():
        dq_ref[here, :] += total * scale


def hand_out(core, value, keep_ref, send_ref, columns):
    bands, rows = keep_ref.shape[1:3]
    for parity in range(2):

        @pl.when(core == parity)
        def _(parity=parity):
            for band in range(bands):
                for side, ref in ((parity, keep_ref), (1 - parity, send_ref)):
                    at = (2 * band + side) * rows
                    ref[0, band, :, columns] = value[at : at + rows].astype(ref.dtype)


def weights_kernel(places, normed, rounded, before, active, keep_ref, send_ref):
    quarter = pl.program_id(0)
    columns = slice(0, before.shape[1])

    @pl.when(quarter < 2)
    def _():
        hand_out(places[2], dot(normed[...], before[...], 0, 0), keep_ref, send_ref, columns)

    @pl.when(quarter >= 2)
    def _():
        hand_out(places[2], dot(rounded[...], active[...], 0, 0), keep_ref, send_ref, columns)


def last_weights_kernel(
    places, normed, rounded, before, active, normed_attn, project, attended, branch, table_in, table_out, gain,
    keep_ref, send_ref,
):
    quarter = pl.program_id(0)
    weights_kernel(places, normed, rounded, before, active, keep_ref, send_ref)
    start = before.shape[1]
    width = normed_attn.shape[1]
    columns = slice(start, start + width)

    @pl.when(quarter < 3)
    def _():
        hand_out(places[2], dot(normed_attn[...], project[...], 0, 1), keep_ref, send_ref, columns)

    @pl.when(quarter == 3)
    def _():
        hand_out(places[2], dot(attended[...], branch[...], 1, 0), keep_ref, send_ref, columns)

    columns = slice(start + width, start + width + table_in.shape[1])
    for index, ref in enumerate((table_in, table_out, gain)):

        @pl.when(quarter == index)
        def _(ref=ref):
            hand_out(places[2], ref[...], keep_ref, send_ref, columns)

    @pl.when(quarter == 3)
    def _():
        hand_out(places[2], jnp.zeros(table_in.shape, F32), keep_ref, send_ref, columns)


def item_kernel(places, *refs, pairs, exact):
    ins, outs = refs[: 2 * pairs], refs[2 * pairs :]
    step = pl.program_id(0)
    for index, out in enumerate(outs):

        @pl.when(step == index)
        def _(index=index, out=out):
            start = 0
            for pair in range(pairs):
                keep, came = ins[2 * pair : 2 * pair + 2]
                value = keep[0] + came[0]
                size = value.shape[-1]
                out[:, :, start : start + size] = value.astype(out.dtype)
                if index > 0 and exact and pair == pairs - 1:
                    part = value[:, :, size - exact :]
                    rest = part - part.astype(out.dtype).astype(F32)
                    out[:, :, start + size : start + size + exact] = rest.astype(out.dtype)
                start += size


def band_kernel(places, own, *refs, count, exact):
    came, outs = refs[:count], refs[count:]
    step = pl.program_id(0)
    size = own.shape[-1]
    total = own[0]
    for ref in came:
        total = total + ref[0, :, :size].astype(F32)
    if exact:
        rest = sum(ref[0, :, size:].astype(F32) for ref in came)
    for index, out in enumerate(outs):

        @pl.when(step == index)
        def _(index=index, out=out):
            out[:, :size] = total.astype(out.dtype)
            if exact:
                part = total[:, size - exact :] + rest
                if index == 0:
                    out[:, size - exact :] = part
                else:
                    high = part.astype(out.dtype)
                    out[:, size - exact : size] = high
                    out[:, size:] = (part - high.astype(F32)).astype(out.dtype)


def exchange(value, axis, distance):
    size = lax.axis_size(axis)
    return lax.ppermute(value, axis, [(i, i ^ distance) for i in range(size)])


def prefetched(kernel, grid, outs, in_specs, out_specs, places, operands, moved):
    return pl.pallas_call(
        kernel,
        grid_spec=pltpu.PrefetchScalarGridSpec(
            num_scalar_prefetch=1, grid=grid, in_specs=in_specs, out_specs=out_specs
        ),
        out_shape=outs,
        cost_estimate=pl.CostEstimate(flops=moved, bytes_accessed=moved, transcendentals=0),
        compiler_params=pltpu.CompilerParams(vmem_limit_bytes=VMEM_BYTES),
    )(places, *operands)


def sort_shares(keeps, sends, places, exact=0):
    items = lax.axis_size("item")
    came = [exchange(send, "lat", 1) for send in sends]
    quarters, bands, rows, _ = keeps[0].shape
    size = sum(keep.shape[-1] for keep in keeps)
    wide = size + exact
    operands = [x for pair in zip(keeps, came) for x in pair]
    return prefetched(
        functools.partial(item_kernel, pairs=len(keeps), exact=exact),
        (items,),
        [shape((bands, rows, size), F32)] + [shape((bands, rows, wide), BF16)] * (items - 1),
        [pl.BlockSpec((1,) + x.shape[1:], lambda j, s: (s[3] ^ j, 0, 0, 0)) for x in operands],
        [pl.BlockSpec((bands, rows, size), lambda j, s: (0, 0, 0))]
        + [pl.BlockSpec((bands, rows, wide), lambda j, s: (0, 0, 0))] * (items - 1),
        places,
        operands,
        moved=14 * bands * rows * size * items,
    )


def sum_shares(sorted_shares, places, exact=0):
    items = lax.axis_size("item")
    own, *others = sorted_shares
    bands, rows, size = own.shape
    wide = size + exact
    came = [exchange(x, "item", k + 1) for k, x in enumerate(others)]
    own, *others = prefetched(
        functools.partial(band_kernel, count=items - 1, exact=exact),
        (bands,),
        [shape((rows, size), F32)] + [shape((rows, wide), BF16)] * (bands - 1),
        [pl.BlockSpec((1, rows, size), lambda j, s: (s[4] ^ j, 0, 0))]
        + [pl.BlockSpec((1, rows, wide), lambda j, s: (s[4] ^ j, 0, 0))] * (items - 1),
        [pl.BlockSpec((rows, size), lambda j, s: (0, 0))]
        + [pl.BlockSpec((rows, wide), lambda j, s: (0, 0))] * (bands - 1),
        places,
        (own, *came),
        moved=14 * bands * rows * size,
    )
    came = [exchange(x, "lat", 2 * (k + 1)) for k, x in enumerate(others)]
    total = own
    for x in came:
        total = total + x[:, :size].astype(F32)
    if exact:
        rest = sum(x[:, size:].astype(F32) for x in came)
        total = jnp.concatenate([total[:, : size - exact], total[:, size - exact :] + rest], axis=1)
    return total


def after(value, *others):
    return lax.optimization_barrier((value, *others))[0]


def all_items(value):
    return [value] + [exchange(value, "item", k) for k in range(1, lax.axis_size("item"))]


def sum_over(value, axis):
    distance = 1
    while distance < lax.axis_size(axis):
        value = value + exchange(value, axis, distance)
        distance *= 2
    return value


def adam_kernel(places, factor, *refs):
    first, second = refs[:4], refs[4:8]
    mlp, attn = refs[8:12], refs[12:16]
    mlp_out, attn_out = refs[16:21], refs[21:26]
    block = mlp[0].shape[-1]
    width = attn[0].shape[-1]
    step = pl.program_id(0)
    for index in range(4):

        @pl.when(step == index)
        def _(index=index):
            scale = factor[0]
            shares = (
                second[index][:, :block], first[index][:, block : 2 * block], first[index][:, :block]
            )
            for layer, share in enumerate(shares):
                new = adam_update(scale * share, *(ref[layer] for ref in mlp), RATE_MATRIX, WEIGHT_DECAY)
                for ref, value in zip(mlp_out, new):
                    ref[layer] = value
            share = second[index][:, block : block + width]
            new = adam_update(scale * share, *(ref[...] for ref in attn), RATE_MATRIX, WEIGHT_DECAY)
            for ref, value in zip(attn_out, new):
                ref[...] = value


def encoder_back_kernel(
    dq, g0, g1, g2, grad_residual, encoded, pooled, slope, gains, mlp, attn, x, pin, grad_join,
    rounded_ref, before_ref, project_ref, table_ref, gain_ref,
):
    width = encoded.shape[1]
    pairs = g1[...] + g0[...].astype(F32) + g2[...].astype(F32)
    project = jnp.concatenate([dq[...], pairs], axis=0).astype(BF16)
    project_ref[...] = project
    grad_normed = dot(project, attn[:, : 3 * width], 0, 1)
    grad_encoded, gain_attn = norm_back(grad_normed, encoded[...], gains[1:2])
    grad_pooled, gain_enc = mlp_backward(
        grad_residual[...] + grad_encoded, pooled[...], gains[0:1], mlp, slope, rounded_ref, before_ref
    )
    add_up(gain_ref, jnp.concatenate([gain_enc, gain_attn], axis=0))
    high, low = two_parts(grad_pooled)
    both = dot(high, pin[...], 0, 0) + dot(low, pin[...], 0, 0)
    channels = x.shape[0]
    high, low = two_parts(grad_join[...])
    direct = dot(high, x[...], 0, 1) + dot(low, x[...], 0, 1)
    add_up(table_ref, direct + both[:, :channels] + both[:, channels:])


def weights(normed, rounded, before, active, places, last=()):
    rows, width = normed.shape
    hidden = before.shape[1]
    bands = lax.axis_size("lat") // 2
    block = hidden // 2
    columns = block + (width + CHANNEL_PAD if last else 0)
    out = shape((4, bands, width // (2 * bands), columns), F32)
    out_spec = pl.BlockSpec((1,) + out.shape[1:], lambda i: (i, 0, 0, 0))
    specs = [
        pl.BlockSpec(memory_space=pltpu.SMEM),
        whole((rows, width)),
        whole((rows, width)),
        pl.BlockSpec((rows, block), lambda i: (0, jnp.minimum(i, 1))),
        pl.BlockSpec((rows, block), lambda i: (0, jnp.maximum(i - 2, 0))),
    ]
    if last:
        specs += [whole((rows, width)), pl.BlockSpec((width, rows), lambda i: (jnp.minimum(i, 2), 0))]
        specs += [whole(x.shape) for x in last[2:]]
    return call(
        last_weights_kernel if last else weights_kernel,
        (4,),
        [out, out],
        specs,
        [out_spec, out_spec],
        (places, normed, rounded, before, active, *last),
        flops=4 * rows * width * hidden,
        moved=4 * rows * hidden + 8 * width * hidden,
    )


def adam_update(gradient, master, moment_one, moment_two, average, step_rate, decay_rate):
    one_new = BETA_ONE * moment_one + (1.0 - BETA_ONE) * gradient
    two_new = BETA_TWO * moment_two + (1.0 - BETA_TWO) * gradient * gradient
    one_hat = one_new / (1.0 - BETA_ONE**STEP)
    two_hat = two_new / (1.0 - BETA_TWO**STEP)
    master_new = master - step_rate * (
        one_hat / (jnp.sqrt(two_hat) + ADAM_EPS) + decay_rate * master
    )
    average_new = EMA_DECAY * average + (1.0 - EMA_DECAY) * master_new
    return (one_new, two_new, master_new, average_new, master_new.astype(jnp.bfloat16))


def from_sides(to_left, to_right):
    size = lax.axis_size("lat")
    up = [(i, (i + 1) % size) for i in range(size - 1)]
    down = [(j, i) for i, j in up]
    return lax.ppermute(to_right, "lat", up), lax.ppermute(to_left, "lat", down)


def shards(
    noisy_state,
    target_state,
    sigmas,
    sh_basis,
    lengths,
    grid_edges,
    mesh_edges,
    dec_edges,
    tables_copy,
    tables_master,
    tables_first,
    tables_second,
    tables_ema,
    attn_copy,
    attn_master,
    attn_first,
    attn_second,
    attn_ema,
    mlp_copy,
    mlp_master,
    mlp_first,
    mlp_second,
    mlp_ema,
    gains_copy,
    gains_master,
    gains_first,
    gains_second,
    gains_ema,
):
    band_index = lax.axis_index("lat")
    bands = lax.axis_size("lat")
    item_index = lax.axis_index("item")
    places = jnp.stack([band_index, bands, band_index % 2, item_index, band_index // 2]).astype(jnp.int32)
    rows = mesh_edges.shape[0]
    grid_rows = noisy_state.shape[2]
    width = attn_copy.shape[0]
    channels = noisy_state.shape[1]
    padded = CHANNEL_PAD
    hidden = mlp_copy.shape[2] // 2
    depth = width // HEADS
    gains = gains_copy.astype(F32)
    gain_rows = gains.shape[0]
    noise_level = sigmas[0]
    square = noise_level * noise_level
    scale_in = lax.rsqrt(square + 1.0)
    scale_skip = 1.0 / (square + 1.0)
    scale_out = noise_level * scale_in
    weight_loss = (square + 1.0) / square
    noisy_field = noisy_state[0]
    target_field = target_state[0]
    extra = padded - channels
    inputs = jnp.pad((scale_in * noisy_field).astype(BF16), ((0, extra), (0, 0)))
    tables = jnp.pad(tables_copy, ((0, 0), (0, extra), (0, 0)))

    def weights_spec(index):
        return pl.BlockSpec((1, width, 2 * hidden), lambda *_: (index, 0, 0))

    attn_spec = whole(attn_copy.shape)
    gains_spec = whole(gains.shape)
    tables_spec = whole(tables.shape)
    steps = rows // ROWS
    kept_shapes = [shape((rows, width), BF16), shape((rows, hidden), F32), shape((rows, hidden), BF16)]
    kept_specs = [rows_of(width), rows_of(hidden), rows_of(hidden)]
    mlp_flops = 4 * rows * width * hidden

    pin, pooled, encoded, normed_enc, slope_enc, active_enc, normed_attn, queries, pairs = call(
        encoder_kernel,
        (steps,),
        [shape((rows, 2 * padded), BF16), shape((rows, width), F32), shape((rows, width), F32)]
        + kept_shapes
        + [shape((rows, width), BF16), shape((width, rows), BF16), shape((rows, 2 * width), BF16)],
        [
            rows_of(grid_edges.shape[1]), whole((padded, grid_rows)), tables_spec, gains_spec,
            weights_spec(0), attn_spec,
        ],
        [rows_of(2 * padded), rows_of(width), rows_of(width)]
        + kept_specs
        + [rows_of(width), lanes_of(width), rows_of(2 * width)],
        (grid_edges, inputs, tables, gains, mlp_copy, attn_copy),
        flops=mlp_flops + 6 * rows * width * width,
        moved=30 * rows * width,
    )

    before_pairs, after_pairs = from_sides(pairs, pairs)

    crops = lengths.shape[1]
    smem = pl.BlockSpec(memory_space=pltpu.SMEM)
    bias_lanes = 128
    bias = call(
        functools.partial(bias_kernel, crops=crops),
        (rows // bias_lanes,),
        shape((3, rows, rows), F32),
        [smem, smem, lanes_of(mesh_edges.shape[1], bias_lanes)],
        pl.BlockSpec((3, rows, bias_lanes), lambda i: (0, 0, i)),
        (places, jnp.cumsum(lengths[0]), mesh_edges.T),
        flops=2 * 10**9,
        moved=12 * rows * rows,
    )

    lanes = 512
    window = [before_pairs, pairs, after_pairs]
    attended, lse = call(
        functools.partial(attend_kernel, chunk=256),
        (rows // lanes, HEADS),
        [shape((width, rows), F32), shape((HEADS, 8, rows), F32)],
        [pl.BlockSpec((depth, lanes), lambda i, h: (h, i))]
        + [pl.BlockSpec((rows, depth), lambda i, h: (0, h))] * 3
        + [pl.BlockSpec((rows, depth), lambda i, h: (0, HEADS + h))] * 3
        + [pl.BlockSpec((3, rows, lanes), lambda i, h: (0, 0, i))],
        [
            pl.BlockSpec((depth, lanes), lambda i, h: (h, i)),
            pl.BlockSpec((1, 8, lanes), lambda i, h: (h, 0, i)),
        ],
        (queries, *window, *window, bias),
        scratch=[pltpu.VMEM((3, rows, lanes), F32)],
        flops=24 * rows * rows * width,
        moved=12 * rows * rows,
    )

    rounded_o, residual, normed_proc, slope_proc, active_proc, sent = call(
        processor_kernel,
        (steps,),
        [shape((width, rows), BF16), shape((rows, width), F32)] + kept_shapes + [shape((rows, width), BF16)],
        [lanes_of(width), rows_of(width), gains_spec, weights_spec(1), attn_spec],
        [lanes_of(width), rows_of(width)] + kept_specs + [rows_of(width)],
        (attended, encoded, gains, mlp_copy, attn_copy),
        flops=mlp_flops + 2 * rows * width * width,
        moved=24 * rows * width,
    )

    before_sent, after_sent = from_sides(sent, sent)

    joined, normed_dec, slope_dec, active_dec, decoded, final, output = call(
        decoder_kernel,
        (grid_rows // ROWS,),
        [shape((grid_rows, width), F32)]
        + kept_shapes
        + [shape((grid_rows, width), F32), shape((grid_rows, width), BF16), shape((padded, grid_rows), F32)],
        [
            rows_of(dec_edges.shape[1]), whole((rows, width)), whole((rows, width)), whole((rows, width)),
            lanes_of(padded), tables_spec, gains_spec, weights_spec(2),
        ],
        [rows_of(width)] + kept_specs + [rows_of(width), rows_of(width), lanes_of(padded)],
        (dec_edges, before_sent, sent, after_sent, inputs, tables, gains, mlp_copy),
        flops=mlp_flops + 6 * rows * rows * width,
        moved=24 * rows * width,
    )

    error_field = scale_skip * noisy_field + scale_out * output[:channels] - target_field
    partial_value = lax.dot_general(
        error_field,
        sh_basis,
        (((1,), (1,)), ((), ())),
        precision=HIGH_PRECISION,
        preferred_element_type=F32,
    )
    coeffs = sum_over(partial_value, "lat")
    slice_width = coeffs.shape[1] // bands
    own_coeffs = lax.dynamic_slice_in_dim(coeffs, band_index * slice_width, slice_width, 1)
    loss_item = weight_loss * jnp.sum(own_coeffs * own_coeffs)
    grad_error = jnp.dot(
        2.0 * weight_loss * coeffs, sh_basis, precision=HIGH_PRECISION, preferred_element_type=F32
    )
    grad_output = jnp.pad((scale_out * grad_error).astype(BF16), ((0, extra), (0, 0)))

    grad_join, rounded_dec, before_dec, table_out, gain_dec = call(
        decoder_back_kernel,
        (grid_rows // ROWS,),
        [
            shape((grid_rows, width), F32), shape((grid_rows, width), BF16), shape((grid_rows, hidden), BF16),
            shape((width, padded), F32), shape((2, width), F32),
        ],
        [
            lanes_of(padded), tables_spec, rows_of(width), rows_of(width), rows_of(width), rows_of(hidden),
            gains_spec, weights_spec(2),
        ],
        [rows_of(width), rows_of(width), rows_of(hidden), whole((width, padded)), whole((2, width))],
        (grad_output, tables, decoded, final, joined, slope_dec, gains, mlp_copy),
        flops=mlp_flops,
        moved=24 * rows * width,
    )

    to_left, grad_own, to_right = call(
        scatter_kernel,
        (steps,),
        [shape((rows, width), BF16), shape((rows, width), F32), shape((rows, width), BF16)],
        [whole((dec_edges.shape[1], grid_rows)), whole((grid_rows, width))],
        [rows_of(width)] * 3,
        (dec_edges.T, grad_join),
        scratch=[pltpu.VMEM((grid_rows, width), BF16), pltpu.VMEM((grid_rows, width), BF16)],
        flops=12 * rows * grid_rows * width,
        moved=12 * rows * width,
    )
    from_left, from_right = from_sides(to_left, to_right)
    keep_dec, send_dec = weights(normed_dec, rounded_dec, before_dec, active_dec, places)

    grad_residual, rounded_proc, before_proc, gain_proc, branch, grad_o, delta = call(
        processor_back_kernel,
        (steps,),
        [
            shape((rows, width), F32), shape((rows, width), BF16), shape((rows, hidden), BF16),
            shape((1, width), F32), shape((rows, width), BF16), shape((width, rows), BF16),
            shape((HEADS, 8, rows), F32),
        ],
        [rows_of(width)] * 4 + [rows_of(hidden), gains_spec, weights_spec(1), attn_spec, lanes_of(width)],
        [
            rows_of(width), rows_of(width), rows_of(hidden), whole((1, width)), rows_of(width), lanes_of(width),
            pl.BlockSpec((HEADS, 8, ROWS), lambda i: (0, 0, i)),
        ],
        (from_left, after(grad_own, keep_dec, send_dec), from_right, residual, slope_proc, gains, mlp_copy, attn_copy, attended),
        flops=mlp_flops + 2 * rows * width * width,
        moved=24 * rows * width,
    )

    block = 512
    side = pl.BlockSpec((2, depth, block), lambda i, h: (0, h, i))
    grad_queries, pairs_left, pairs_own, pairs_right = call(
        functools.partial(attend_back_kernel, chunk=256),
        (rows // block, HEADS),
        [
            shape((width, rows), F32), shape((2, width, rows), BF16), shape((2, width, rows), F32),
            shape((2, width, rows), BF16),
        ],
        [whole((width, rows)), whole((width, rows)), whole((HEADS, 8, rows)), whole((HEADS, 8, rows))]
        + [pl.BlockSpec((block, depth), lambda i, h: (i, h))] * 3
        + [pl.BlockSpec((block, depth), lambda i, h: (i, HEADS + h))] * 3
        + [pl.BlockSpec((3, block, rows), lambda i, h: (0, i, 0))],
        [whole((width, rows)), side, side, side],
        (queries, grad_o, lse, delta, *window, *window, bias),
        scratch=[pltpu.VMEM((block, rows), BF16), pltpu.VMEM((block, rows), BF16)],
        flops=60 * rows * rows * width,
        moved=12 * rows * rows,
    )
    before_grad, after_grad = from_sides(
        pairs_left.reshape(2 * width, rows), pairs_right.reshape(2 * width, rows)
    )
    keep_proc, send_proc = weights(normed_proc, rounded_proc, before_proc, active_proc, places)
    first_sorted = sort_shares([keep_dec, keep_proc], [send_dec, send_proc], places)
    first_total = sum_shares(first_sorted, places)
    first_all = all_items(first_total)

    rounded_enc, before_enc, project, table_in, gain_enc = call(
        encoder_back_kernel,
        (steps,),
        [
            shape((rows, width), BF16), shape((rows, hidden), BF16), shape((3 * width, rows), BF16),
            shape((width, padded), F32), shape((2, width), F32),
        ],
        [lanes_of(width)] + [lanes_of(2 * width)] * 3 + [rows_of(width)] * 3
        + [rows_of(hidden), gains_spec, weights_spec(0), attn_spec, lanes_of(padded), rows_of(2 * padded), rows_of(width)],
        [rows_of(width), rows_of(hidden), lanes_of(3 * width), whole((width, padded)), whole((2, width))],
        (
            grad_queries, before_grad, pairs_own.reshape(2 * width, rows), after_grad,
            after(grad_residual, *first_sorted), encoded,
            pooled, slope_enc, gains, mlp_copy, attn_copy, inputs, pin, grad_join,
        ),
        flops=mlp_flops + 6 * rows * width * width,
        moved=24 * rows * width,
    )
    grad_gains = jnp.concatenate([gain_enc, gain_proc, gain_dec], axis=0)
    gain_columns = jnp.pad(grad_gains.T, ((0, 0), (0, padded - gain_rows)))
    keep_last, send_last = weights(
        normed_enc, rounded_enc, before_enc, active_enc, places,
        (normed_attn, project, rounded_o, branch, table_in, table_out, gain_columns),
    )
    last_total = sum_shares(
        sort_shares([keep_last], [send_last], places, exact=padded), places, exact=padded
    )
    squares = jnp.sum(first_total * first_total) + jnp.sum(last_total * last_total)
    scalars = sum_over(sum_over(jnp.stack([squares, loss_item])[None], "lat"), "item")
    last_all = all_items(last_total)
    loss_sum = scalars[0, 1]
    grad_norm = jnp.sqrt(scalars[0, 0])
    scale_factor = CLIP_LEVEL / jnp.maximum(grad_norm, CLIP_LEVEL)

    shard_rows = attn_master.shape[0]
    quarter = hidden // 2
    mlp_spec = pl.BlockSpec((mlp_master.shape[0], shard_rows, quarter), lambda j, s: (0, 0, s[3] ^ j))
    attn_part = pl.BlockSpec((shard_rows, width), lambda j, s: (0, s[3] ^ j))
    kinds = [F32, F32, F32, F32, BF16]
    updated = prefetched(
        adam_kernel,
        (4,),
        [shape(mlp_master.shape, kind) for kind in kinds] + [shape(attn_master.shape, kind) for kind in kinds],
        [smem]
        + [pl.BlockSpec(x.shape, lambda j, s: (0, 0)) for x in (*first_all, *last_all)]
        + [mlp_spec] * 4
        + [attn_part] * 4,
        [mlp_spec] * 5 + [attn_part] * 5,
        places,
        (
            scale_factor[None], *first_all, *last_all, mlp_master, mlp_first, mlp_second, mlp_ema,
            attn_master, attn_first, attn_second, attn_ema,
        ),
        moved=34 * (mlp_master.size + attn_master.size),
    )
    mlps, att = updated[:5], updated[5:]
    small = jnp.stack([x[:, quarter + width :] for x in last_all])
    tab_sum = jnp.stack(
        [lax.dynamic_index_in_dim(small, item_index ^ q, 0, False)[:, :channels].T for q in range(2)]
    )
    gain_sum = lax.dynamic_index_in_dim(small, item_index ^ 2, 0, False)[:, :gain_rows].T
    tab = adam_update(
        scale_factor * tab_sum, tables_master, tables_first, tables_second, tables_ema, RATE_MATRIX, WEIGHT_DECAY
    )
    gns = adam_update(
        scale_factor * gain_sum, gains_master, gains_first, gains_second, gains_ema, RATE_GAIN, 0.0
    )
    return (loss_sum, grad_norm, *tab, *att, *mlps, *gns)


def solution(mesh):
    table = P(None, None, "lat")
    attn = P("lat", None)
    mlp = P(None, "lat", None)
    gain = P(None, "lat")
    placed = (
        P("item", None, "lat"),
        P("item", None, "lat"),
        P("item"),
        P(None, "lat"),
        P("item", None),
        P("lat", None),
        P("lat", None),
        P("lat", None),
        P(), table, table, table, table,
        P(), attn, attn, attn, attn,
        P(), mlp, mlp, mlp, mlp,
        P(), gain, gain, gain, gain,
    )
    return jax.shard_map(
        shards,
        mesh=mesh,
        in_specs=placed,
        out_specs=(P(), P(), *([table] * 5), *([attn] * 5), *([mlp] * 5), *([gain] * 5)),
        check_vma=False,
    )
```

```python
import functools

import jax
import jax.numpy as jnp
from jax import lax
from jax.experimental import pallas as pl
from jax.experimental.pallas import tpu as pltpu
from jax.sharding import PartitionSpec as P

HEADS = 4
GROUPS = 2
WEIGH = 30
LARGE = 1 << 20
STEP = 10

EPS_NORM = 1e-05
CLIP_LEVEL = 1.0
BETA_ONE = 0.9
BETA_TWO = 0.999
ADAM_EPS = 1e-08
EMA_DECAY = 0.9
RATE_MATRIX = 0.05
RATE_GAIN = 0.3
WEIGHT_DECAY = 0.1
HIGH_PRECISION = lax.Precision.HIGHEST

F32 = jnp.float32
BF16 = jnp.bfloat16
LOG2E = 1.4426950408889634
CHANNEL_PAD = 128
ROWS = 256
VMEM_BYTES = 36 * 1024 * 1024


def dot(left, right, left_dim, right_dim):
    return lax.dot_general(
        left, right, (((left_dim,), (right_dim,)), ((), ())), preferred_element_type=F32
    )


FAR = []


def is_far(value):
    return any(value is x for x in FAR)


def far(value):
    return pltpu.with_memory_space_constraint(value, pltpu.HBM) if is_far(value) else value


def call(kernel, grid, outs, in_specs, out_specs, operands, scratch=(), flops=0, moved=0, near=False):
    single = not isinstance(outs, list)
    kinds = [outs] if single else outs
    large = [not near and x.size * x.dtype.itemsize >= LARGE for x in kinds]
    kinds = [pltpu.HBM(x.shape, x.dtype) if flag else x for x, flag in zip(kinds, large)]
    results = pl.pallas_call(
        kernel,
        grid=grid,
        out_shape=kinds[0] if single else kinds,
        in_specs=in_specs,
        out_specs=out_specs,
        scratch_shapes=list(scratch),
        cost_estimate=pl.CostEstimate(flops=flops * WEIGH, bytes_accessed=moved * WEIGH, transcendentals=0),
        compiler_params=pltpu.CompilerParams(vmem_limit_bytes=VMEM_BYTES),
    )(*[far(x) for x in operands])
    FAR.extend(x for x, flag in zip([results] if single else results, large) if flag)
    return results


def whole(shape):
    return pl.BlockSpec(shape, lambda *_: (0,) * len(shape))


def rows_of(width, rows=ROWS):
    return pl.BlockSpec((rows, width), lambda i: (i, 0))


def lanes_of(height, lanes=ROWS):
    return pl.BlockSpec((height, lanes), lambda i: (0, i))


def shape(dims, kind):
    return jax.ShapeDtypeStruct(dims, kind)


def norm_parts(values):
    center = values - jnp.mean(values, axis=-1, keepdims=True)
    spread = jnp.mean(center * center, axis=-1, keepdims=True)
    inverse = lax.rsqrt(spread + EPS_NORM)
    return center * inverse, inverse


def norm_back(upstream, values, gain_row):
    unit, inverse = norm_parts(values)
    scaled = upstream * gain_row
    along = jnp.mean(scaled * unit, axis=-1, keepdims=True)
    grad = inverse * (scaled - jnp.mean(scaled, axis=-1, keepdims=True) - unit * along)
    gain_grad = jnp.sum(upstream * unit, axis=0, keepdims=True)
    return grad, gain_grad


def gelu_parts(u):
    root = 0.7978845608028654
    cubic = 0.044715
    square = u * u
    inner = u * (root + (root * cubic) * square)
    half = 0.5 + 0.5 * jnp.tanh(inner)
    slope = half * (1.0 + (1.0 - half) * (6.0 * inner - (4.0 * root) * u))
    return u * half, slope


def mlp_forward(values, gain_row, w_ref, normed_ref, slope_ref, active_ref, step=512):
    hidden = w_ref.shape[-1] // 2
    normed = (norm_parts(values)[0] * gain_row).astype(BF16)
    normed_ref[...] = normed
    result = jnp.zeros(values.shape, F32)
    starts = range(0, hidden, step)
    befores = [dot(normed, w_ref[0, :, :step], 1, 0)]
    for start in starts:
        part = slice(start, start + step)
        if start + step < hidden:
            befores.append(dot(normed, w_ref[0, :, start + step : start + 2 * step], 1, 0))
        active, slope = gelu_parts(befores.pop(0))
        active = active.astype(BF16)
        slope_ref[:, part] = slope
        active_ref[:, part] = active
        result = result + dot(active, w_ref[0, :, hidden + start : hidden + start + step], 1, 1)
    return values + result


def mlp_backward(upstream, values, gain_row, w_ref, slope_ref, rounded_ref, before_ref, step=512):
    hidden = w_ref.shape[-1] // 2
    rounded = upstream.astype(BF16)
    rounded_ref[...] = rounded
    grad_normed = jnp.zeros(values.shape, F32)
    for start in range(0, hidden, step):
        part = slice(start, start + step)
        grad_active = dot(rounded, w_ref[0, :, hidden + start : hidden + start + step], 1, 0)
        grad_before = (grad_active * slope_ref[:, part]).astype(BF16)
        before_ref[:, part] = grad_before
        grad_normed = grad_normed + dot(grad_before, w_ref[0, :, part], 1, 1)
    grad, gain_grad = norm_back(grad_normed, values, gain_row)
    return upstream + grad, gain_grad


def two_parts(values):
    high = values.astype(BF16)
    return high, (values - high.astype(F32)).astype(BF16)


def named(edges, places):
    tally = jnp.zeros(places.shape, F32)
    for j in range(edges.shape[0]):
        tally = tally + jnp.where(edges[j : j + 1, :] == places, 1.0, 0.0)
    return tally.astype(BF16)


def add_up(ref, value):
    step = pl.program_id(0)

    @pl.when(step == 0)
    def _():
        ref[...] = value

    @pl.when(step > 0)
    def _():
        ref[...] += value


def encoder_kernel(
    edges, x, table, gains, mlp, attn,
    pin_ref, pooled_ref, encoded_ref, normed_ref, slope_ref, active_ref, normed_attn_ref, q_ref, *pair_refs,
):
    count, rows = edges.shape
    width = attn.shape[0]
    places = lax.broadcasted_iota(jnp.int32, (x.shape[1], rows), 0)
    pin = dot(named(edges, places), x[...], 0, 1) / count
    high, low = two_parts(pin)
    pin_ref[...] = jnp.concatenate([high, low], axis=1)
    pooled = dot(high, table[0], 1, 0) + dot(low, table[0], 1, 0)
    pooled_ref[...] = pooled
    encoded = mlp_forward(pooled, gains[0:1], mlp, normed_ref, slope_ref, active_ref)
    encoded_ref[...] = encoded
    normed_attn = (norm_parts(encoded)[0] * gains[1:2]).astype(BF16)
    normed_attn_ref[...] = normed_attn
    q_ref[...] = dot(attn[:, :width], normed_attn, 0, 1).astype(BF16)
    part = width // len(pair_refs)
    for g, ref in enumerate(pair_refs):
        for side in range(2):
            start = (1 + side) * width + g * part
            ref[:, side * part : (side + 1) * part] = dot(
                normed_attn, attn[:, start : start + part], 1, 0
            ).astype(BF16)


def bias_kernel(places, ends, edges, bias_ref, *, crops):
    count, lanes = edges.shape
    rows = bias_ref.shape[1]
    window = bias_ref.shape[0] * rows
    col = pl.program_id(0)
    nodes = col * lanes + lax.broadcasted_iota(jnp.int32, (1, lanes), 1)
    first = places[0] * rows
    low = jnp.zeros((1, lanes), jnp.int32)
    high = jnp.full((1, lanes), places[1] * rows, jnp.int32)
    for c in range(crops - 1, -1, -1):
        high = jnp.where(ends[c] > first + nodes, ends[c], high)
    for c in range(crops):
        low = jnp.where(ends[c] <= first + nodes, ends[c], low)
    near = edges[...] + (first - rows)
    place = jnp.where((near >= low) & (near < high), edges[...], -1)
    place = jnp.concatenate([place, rows + nodes], axis=0)
    tile = 128
    tiles = window // tile
    each = 6
    fine = jnp.where(place < 0, -1, place % tile)
    coarse = place // tile
    sub = lax.broadcasted_iota(jnp.int32, (tile, lanes), 0)
    for start in range(0, tiles, each):
        here = (coarse >= start) & (coarse < start + each)
        amount = jnp.where(here, jnp.left_shift(1, 5 * jnp.where(here, coarse - start, 0)), 0)
        total = jnp.zeros((tile, lanes), jnp.int32)
        for j in range(count + 1):
            total = total + jnp.where(sub == fine[j : j + 1], amount[j : j + 1], 0)
        for t in range(start, min(tiles, start + each)):
            tally = jnp.bitwise_and(jnp.right_shift(total, 5 * (t - start)), 31)
            value = jnp.where(tally == 0, -1e30, jnp.log2(jnp.maximum(tally, 1).astype(F32)))
            at = t * tile
            bias_ref[at // rows, at % rows : at % rows + tile, :] = value


def attend_kernel(q_ref, k0, k1, k2, v0, v1, v2, bias, o_ref, l_ref, scores, *, chunk):
    depth, lanes = q_ref.shape
    rows = k0.shape[0]
    factor = depth**-0.5 * LOG2E
    q = q_ref[...]
    top = jnp.full((8, lanes), -3e38, F32)
    for w, keys in enumerate((k0, k1, k2)):
        for start in range(0, rows, chunk):
            part = slice(start, start + chunk)
            score = dot(keys[part, :], q, 1, 0) * factor + bias[w, part, :]
            scores[w, part, :] = score
            top = jnp.maximum(top, jnp.max(score.reshape(chunk // 8, 8, lanes), axis=0))
    top = jnp.max(top, axis=0, keepdims=True)
    total = jnp.zeros((8, lanes), F32)
    result = jnp.zeros((depth, lanes), F32)
    for w, values in enumerate((v0, v1, v2)):
        for start in range(0, rows, chunk):
            part = slice(start, start + chunk)
            e = jnp.exp2(scores[w, part, :] - top)
            total = total + jnp.sum(e.reshape(chunk // 8, 8, lanes), axis=0)
            result = result + dot(values[part, :], e.astype(BF16), 0, 0)
    total = jnp.sum(total, axis=0, keepdims=True)
    o_ref[...] = result * (1.0 / total)
    l_ref[...] = jnp.broadcast_to((top + jnp.log2(total))[None], l_ref.shape)


def processor_kernel(
    o0, o1, encoded, gains, mlp, attn,
    attended_ref, residual_ref, normed_ref, slope_ref, active_ref, sent_ref,
):
    attended = jnp.concatenate([o0[...], o1[...]], axis=0).astype(BF16)
    attended_ref[...] = attended
    residual = encoded[...] + dot(attended, attn[...], 0, 0)
    residual_ref[...] = residual
    latent = mlp_forward(residual, gains[2:3], mlp, normed_ref, slope_ref, active_ref)
    sent_ref[...] = latent.astype(BF16)


def decoder_kernel(
    edges, s0, s1, s2, x, tables, gains, mlp,
    joined_ref, normed_ref, slope_ref, active_ref, decoded_ref, final_ref, output_ref,
):
    count, rows = edges.shape
    band = s0.shape[0]
    gathered = jnp.zeros(joined_ref.shape, F32)
    places = lax.broadcasted_iota(jnp.int32, (band, rows), 0)
    for w, sent in enumerate((s0, s1, s2)):
        gathered = gathered + dot(named(edges, places + w * band), sent[...], 0, 0)
    joined = dot(x[...], tables[0], 0, 0) + gathered / count
    joined_ref[...] = joined
    decoded = mlp_forward(joined, gains[3:4], mlp, normed_ref, slope_ref, active_ref)
    decoded_ref[...] = decoded
    final = (norm_parts(decoded)[0] * gains[4:5]).astype(BF16)
    final_ref[...] = final
    output_ref[...] = dot(tables[1], final, 1, 1)


def decoder_back_kernel(
    grad_output, tables, decoded, final, joined, slope, gains, mlp,
    grad_join_ref, rounded_ref, before_ref, table_ref, gain_ref,
):
    grad_final = dot(grad_output[...], tables[1], 0, 0)
    add_up(table_ref, dot(final[...], grad_output[...], 0, 1))
    grad_decoded, gain_final = norm_back(grad_final, decoded[...], gains[4:5])
    grad_join, gain_dec = mlp_backward(
        grad_decoded, joined[...], gains[3:4], mlp, slope, rounded_ref, before_ref
    )
    grad_join_ref[...] = grad_join
    add_up(gain_ref, jnp.concatenate([gain_dec, gain_final], axis=0))


def scatter_kernel(edges, grad, out0, out1, out2, high_ref, low_ref):
    rows = out0.shape[0]
    count = edges.shape[0]
    step = pl.program_id(0)

    @pl.when(step == 0)
    def _():
        high, low = two_parts(grad[...])
        high_ref[...] = high
        low_ref[...] = low

    total = grad.shape[0]
    for w, out in enumerate((out0, out1, out2)):
        sub = lax.broadcasted_iota(jnp.int32, (rows, total), 0) + (step * rows + w * total)
        tally = named(edges, sub)
        value = dot(tally, high_ref[...], 1, 0) + dot(tally, low_ref[...], 1, 0)
        out[...] = (value / count).astype(out.dtype)


def processor_back_kernel(
    g0, g1, g2, residual, slope, gains, mlp, attn, o0, o1,
    grad_residual_ref, rounded_ref, before_ref, gain_ref, branch_ref, grad_o_ref, delta_ref,
):
    width = residual.shape[1]
    upstream = g1[...] + g0[...].astype(F32) + g2[...].astype(F32)
    grad, gain = mlp_backward(
        upstream, residual[...], gains[2:3], mlp, slope, rounded_ref, before_ref
    )
    add_up(gain_ref, gain)
    grad_residual_ref[...] = grad
    branch = grad.astype(BF16)
    branch_ref[...] = branch
    grad_o = dot(attn[...], branch, 1, 1).astype(BF16)
    grad_o_ref[...] = grad_o
    depth = width // HEADS
    attended = jnp.concatenate([o0[...], o1[...]], axis=0)
    together = grad_o.astype(F32) * attended
    for h in range(HEADS):
        row = jnp.sum(together[h * depth : (h + 1) * depth], axis=0, keepdims=True)
        delta_ref[h] = jnp.broadcast_to(row, delta_ref.shape[1:])


def attend_back_kernel(
    q_ref, do_ref, lse_ref, delta_ref, k0, k1, k2, v0, v1, v2, bias,
    dq_ref, out0, out1, out2, p_ref, ds_ref, *, chunk,
):
    block, depth = k0.shape
    scale = depth**-0.5
    factor = scale * LOG2E
    step, h = pl.program_id(0), pl.program_id(1)
    here = pl.ds(pl.multiple_of(h * depth, depth), depth)
    q = q_ref[here, :]
    do = do_ref[here, :]
    lse = lse_ref[h, 0:1, :]
    delta = delta_ref[h, 0:1, :]
    total = jnp.zeros(q.shape, F32)
    for w, (keys, values, out) in enumerate(((k0, v0, out0), (k1, v1, out1), (k2, v2, out2))):
        for start in range(0, block, chunk):
            part = slice(start, start + chunk)
            p = jnp.exp2(dot(keys[part, :], q, 1, 0) * factor + bias[w, part, :] - lse)
            ds = p * (dot(values[part, :], do, 1, 0) - delta)
            p_ref[part, :] = p.astype(BF16)
            ds_ref[part, :] = ds.astype(BF16)
            out[0, :, part] = (dot(q, ds_ref[part, :], 1, 1) * scale).astype(out.dtype)
            out[1, :, part] = dot(do, p_ref[part, :], 1, 1).astype(out.dtype)
            total = total + dot(keys[part, :], ds_ref[part, :], 0, 0)

    @pl.when(step == 0)
    def _():
        dq_ref[here, :] = total * scale

    @pl.when(step > 0)
    def _():
        dq_ref[here, :] += total * scale


def hand_out(core, value, keep_ref, send_ref, columns):
    bands, rows = keep_ref.shape[1:3]
    for parity in range(2):

        @pl.when(core == parity)
        def _(parity=parity):
            for band in range(bands):
                for side, ref in ((parity, keep_ref), (1 - parity, send_ref)):
                    at = (2 * band + side) * rows
                    ref[0, band, :, columns] = value[at : at + rows].astype(ref.dtype)


def turn(pairs):
    @pl.when(pl.program_id(0) == 0)
    def _():
        for ref, kept in pairs:
            kept[...] = ref[...].T


def weights_kernel(places, normed, rounded, before, active, keep_ref, send_ref, normed_turned, rounded_turned):
    size = before.shape[1]
    turn(((normed, normed_turned), (rounded, rounded_turned)))
    hand_out(places[2], dot(normed_turned[...], before[...], 1, 0), keep_ref, send_ref, slice(0, size))
    hand_out(places[2], dot(rounded_turned[...], active[...], 1, 0), keep_ref, send_ref, slice(size, 2 * size))


def down_weights_kernel(
    places, rounded, active, normed_attn, project, attended, branch, keep_ref, send_ref, rounded_turned, normed_turned
):
    quarter = pl.program_id(0)
    size = active.shape[1]
    turn(((rounded, rounded_turned), (normed_attn, normed_turned)))
    hand_out(places[2], dot(rounded_turned[...], active[...], 1, 0), keep_ref, send_ref, slice(0, size))
    columns = slice(size, size + normed_attn.shape[1])

    @pl.when(quarter < 3)
    def _():
        hand_out(places[2], dot(normed_turned[...], project[...], 1, 1), keep_ref, send_ref, columns)

    @pl.when(quarter == 3)
    def _():
        hand_out(places[2], dot(attended[...], branch[...], 1, 0), keep_ref, send_ref, columns)


def up_weights_kernel(places, normed, before, table_in, table_out, gain, keep_ref, send_ref, normed_turned):
    quarter = pl.program_id(0)
    size = before.shape[1]
    turn(((normed, normed_turned),))
    hand_out(places[2], dot(normed_turned[...], before[...], 1, 0), keep_ref, send_ref, slice(0, size))
    columns = slice(size, size + table_in.shape[1])
    for index, ref in enumerate((table_in, table_out, gain)):

        @pl.when(quarter == index)
        def _(ref=ref):
            hand_out(places[2], ref[...], keep_ref, send_ref, columns)

    @pl.when(quarter == 3)
    def _():
        hand_out(places[2], jnp.zeros(table_in.shape, F32), keep_ref, send_ref, columns)


def item_kernel(places, *refs, pairs, exact):
    ins, outs = refs[: 2 * pairs], refs[2 * pairs :]
    step = pl.program_id(0)
    for index, out in enumerate(outs):

        @pl.when(step == index)
        def _(index=index, out=out):
            start = 0
            for pair in range(pairs):
                keep, came = ins[2 * pair : 2 * pair + 2]
                value = keep[0] + came[0]
                size = value.shape[-1]
                out[:, :, start : start + size] = value.astype(out.dtype)
                if index > 0 and exact and pair == pairs - 1:
                    part = value[:, :, size - exact :]
                    rest = part - part.astype(out.dtype).astype(F32)
                    out[:, :, start + size : start + size + exact] = rest.astype(out.dtype)
                start += size


def band_kernel(places, *refs, groups, count, exact):
    ins, outs = refs[: groups * (1 + count)], refs[groups * (1 + count) :]
    step = pl.program_id(0)
    start = 0
    for group in range(groups):
        own, *came = ins[group * (1 + count) : (group + 1) * (1 + count)]
        size = own.shape[-1]
        total = own[0]
        for ref in came:
            total = total + ref[0, :, :size].astype(F32)
        last = exact and group == groups - 1
        if last:
            part = total[:, size - exact :] + sum(ref[0, :, size:].astype(F32) for ref in came)
            high = part.astype(BF16)
            rest = (part - high.astype(F32)).astype(BF16)
        for index, out in enumerate(outs):

            @pl.when(step == index)
            def _(index=index, out=out):
                out[:, start : start + size] = total.astype(out.dtype)
                if last and index == 0:
                    out[:, start + size - exact : start + size] = part
                elif last:
                    out[:, start + size - exact : start + size] = high
                    out[:, start + size : start + size + exact] = rest

        start += size


def exchange(value, axis, distance):
    size = lax.axis_size(axis)
    return lax.ppermute(value, axis, [(i, i ^ distance) for i in range(size)])


def prefetched(kernel, grid, outs, in_specs, out_specs, places, operands, moved, weight=1):
    return pl.pallas_call(
        kernel,
        grid_spec=pltpu.PrefetchScalarGridSpec(
            num_scalar_prefetch=1, grid=grid, in_specs=in_specs, out_specs=out_specs
        ),
        out_shape=outs,
        cost_estimate=pl.CostEstimate(flops=moved * WEIGH * weight, bytes_accessed=moved * WEIGH, transcendentals=0),
        compiler_params=pltpu.CompilerParams(vmem_limit_bytes=VMEM_BYTES),
    )(places, *[far(x) for x in operands])


def sort_shares(keeps, sends, places, exact=0, late=()):
    items = lax.axis_size("item")
    came = [exchange(send, "lat", 1) for send in sends]
    quarters, bands, rows, _ = keeps[0].shape
    size = sum(keep.shape[-1] for keep in keeps)
    wide = size + exact
    operands = [after(x, *late) for pair in zip(keeps, came) for x in pair]
    return prefetched(
        functools.partial(item_kernel, pairs=len(keeps), exact=exact),
        (items,),
        [shape((bands, rows, size), F32)] + [shape((bands, rows, wide), BF16)] * (items - 1),
        [pl.BlockSpec((1,) + x.shape[1:], lambda j, s: (s[3] ^ j, 0, 0, 0)) for x in operands],
        [pl.BlockSpec((bands, rows, size), lambda j, s: (0, 0, 0))]
        + [pl.BlockSpec((bands, rows, wide), lambda j, s: (0, 0, 0))] * (items - 1),
        places,
        operands,
        moved=14 * bands * rows * size * items,
    )


def swap_items(sorted_shares):
    own, *others = sorted_shares
    return [own] + [exchange(x, "item", k + 1) for k, x in enumerate(others)]


def sum_items(groups, places, exact=0):
    items = len(groups[0])
    bands, rows, _ = groups[0][0].shape
    operands = [x for group in groups for x in group]
    size = sum(group[0].shape[-1] for group in groups)
    wide = size + exact
    return prefetched(
        functools.partial(band_kernel, groups=len(groups), count=items - 1, exact=exact),
        (bands,),
        [shape((rows, size), F32)] + [shape((rows, wide), BF16)] * (bands - 1),
        [pl.BlockSpec((1,) + x.shape[1:], lambda j, s: (s[4] ^ j, 0, 0)) for x in operands],
        [pl.BlockSpec((rows, size), lambda j, s: (0, 0))]
        + [pl.BlockSpec((rows, wide), lambda j, s: (0, 0))] * (bands - 1),
        places,
        operands,
        moved=14 * bands * rows * size,
        weight=10000,
    )


def sum_bands(parts, exact=0, late=()):
    own, *others = parts
    size = own.shape[-1]
    came = [exchange(x, "lat", 2 * (k + 1)) for k, x in enumerate(others)]
    total = after(own, *late) if late else own
    for x in came:
        total = total + x[:, :size].astype(F32)
    if exact:
        rest = sum(x[:, size:].astype(F32) for x in came)
        total = jnp.concatenate([total[:, : size - exact], total[:, size - exact :] + rest], axis=1)
    return total


def after(value, *others):
    result = lax.optimization_barrier((value, *others))[0]
    if is_far(value):
        FAR.append(result)
    return result


def total_kernel(own, *refs):
    *came, out = refs
    total = own[...]
    for ref in came:
        total = total + ref[...].astype(F32)
    out[...] = total.astype(out.dtype)


def add_bands(parts, late):
    own, *others = parts
    came = [exchange(x, "lat", 2 * (k + 1)) for k, x in enumerate(others)]
    return call(
        total_kernel,
        (1,),
        shape(own.shape, BF16),
        [whole(own.shape)] * len(parts),
        whole(own.shape),
        (after(own, *late), *came),
        flops=10**11,
        moved=16 * own.size,
        near=True,
    )


def all_items(value):
    return [value] + [exchange(value, "item", k) for k in range(1, lax.axis_size("item"))]


def sum_over(value, axis):
    distance = 1
    while distance < lax.axis_size(axis):
        value = value + exchange(value, axis, distance)
        distance *= 2
    return value


def adam_kernel(places, factor, *refs):
    first, down, up = refs[:4], refs[4:8], refs[8:12]
    mlp, attn = refs[12:16], refs[16:20]
    mlp_out, attn_out = refs[20:25], refs[25:30]
    size = mlp[0].shape[-1]
    part = attn[0].shape[-1]
    half = pl.program_id(1)
    for index in range(4):
        for side in range(2):

            @pl.when((pl.program_id(0) == index) & (half == side))
            def _(index=index, side=side):
                scale = factor[0]
                here = slice(side * size, (side + 1) * size)
                there = slice((2 + side) * size, (3 + side) * size)
                shares = ((down if side else up)[index][:, :size], first[index][:, there], first[index][:, here])
                for layer, share in enumerate(shares):
                    new = adam_update(
                        scale * share.astype(F32), *(ref[layer] for ref in mlp), RATE_MATRIX, WEIGHT_DECAY
                    )
                    for ref, value in zip(mlp_out, new):
                        ref[layer] = value
                share = down[index][:, size + side * part : size + (side + 1) * part]
                new = adam_update(scale * share, *(ref[...] for ref in attn), RATE_MATRIX, WEIGHT_DECAY)
                for ref, value in zip(attn_out, new):
                    ref[...] = value


def projection_back_kernel(
    dq0, dq1, left0, left1, own0, own1, right0, right1, grad_residual, encoded, gains, attn,
    upstream_ref, rounded_ref, project_ref, gain_ref,
):
    pairs = [
        own[...] + left[...].astype(F32) + right[...].astype(F32)
        for left, own, right in ((left0, own0, right0), (left1, own1, right1))
    ]
    project = jnp.concatenate(
        [dq0[...], dq1[...], pairs[0][0], pairs[1][0], pairs[0][1], pairs[1][1]], axis=0
    ).astype(BF16)
    project_ref[...] = project
    grad_normed = dot(project, attn[...], 0, 1)
    grad_encoded, gain_attn = norm_back(grad_normed, encoded[...], gains[1:2])
    upstream = grad_residual[...] + grad_encoded
    upstream_ref[...] = upstream
    rounded_ref[...] = upstream.astype(BF16)
    add_up(gain_ref, gain_attn)


def encoder_back_kernel(
    upstream, pooled, slope, gains, mlp, x, pin, grad_join, before_ref, table_ref, gain_ref, rounded_ref
):
    grad_pooled, gain_enc = mlp_backward(
        upstream[...], pooled[...], gains[0:1], mlp, slope, rounded_ref, before_ref
    )
    add_up(gain_ref, gain_enc)
    high, low = two_parts(grad_pooled)
    both = dot(high, pin[...], 0, 0) + dot(low, pin[...], 0, 0)
    channels = x.shape[0]
    high, low = two_parts(grad_join[...])
    direct = dot(high, x[...], 0, 1) + dot(low, x[...], 0, 1)
    add_up(table_ref, direct + both[:, :channels] + both[:, channels:])


def weights(kernel, places, operands, specs, columns, flops, turned):
    rows, width = operands[0].shape
    bands = lax.axis_size("lat") // 2
    out = shape((4, bands, width // (2 * bands), columns), F32)
    out_spec = pl.BlockSpec((1,) + out.shape[1:], lambda i: (i, 0, 0, 0))
    return call(
        kernel,
        (4,),
        [out, out],
        [pl.BlockSpec(memory_space=pltpu.SMEM)] + specs,
        [out_spec, out_spec],
        (places, *operands),
        flops=flops,
        moved=8 * width * columns * 4,
        scratch=[pltpu.VMEM((width, rows), BF16)] * turned,
        near=True,
    )


def adam_update(gradient, master, moment_one, moment_two, average, step_rate, decay_rate):
    one_new = BETA_ONE * moment_one + (1.0 - BETA_ONE) * gradient
    two_new = BETA_TWO * moment_two + (1.0 - BETA_TWO) * gradient * gradient
    one_hat = one_new / (1.0 - BETA_ONE**STEP)
    two_hat = two_new / (1.0 - BETA_TWO**STEP)
    master_new = master - step_rate * (
        one_hat / (jnp.sqrt(two_hat) + ADAM_EPS) + decay_rate * master
    )
    average_new = EMA_DECAY * average + (1.0 - EMA_DECAY) * master_new
    return (one_new, two_new, master_new, average_new, master_new.astype(jnp.bfloat16))


def from_sides(to_left, to_right):
    size = lax.axis_size("lat")
    up = [(i, (i + 1) % size) for i in range(size - 1)]
    down = [(j, i) for i, j in up]
    return lax.ppermute(to_right, "lat", up), lax.ppermute(to_left, "lat", down)


def shards(
    noisy_state,
    target_state,
    sigmas,
    sh_basis,
    lengths,
    grid_edges,
    mesh_edges,
    dec_edges,
    tables_copy,
    tables_master,
    tables_first,
    tables_second,
    tables_ema,
    attn_copy,
    attn_master,
    attn_first,
    attn_second,
    attn_ema,
    mlp_copy,
    mlp_master,
    mlp_first,
    mlp_second,
    mlp_ema,
    gains_copy,
    gains_master,
    gains_first,
    gains_second,
    gains_ema,
):
    FAR.clear()
    band_index = lax.axis_index("lat")
    bands = lax.axis_size("lat")
    item_index = lax.axis_index("item")
    places = jnp.stack([band_index, bands, band_index % 2, item_index, band_index // 2]).astype(jnp.int32)
    rows = mesh_edges.shape[0]
    grid_rows = noisy_state.shape[2]
    width = attn_copy.shape[0]
    channels = noisy_state.shape[1]
    padded = CHANNEL_PAD
    hidden = mlp_copy.shape[2] // 2
    depth = width // HEADS
    FAR.extend([mlp_copy, attn_copy, mlp_master, mlp_first, mlp_second, mlp_ema])
    FAR.extend([attn_master, attn_first, attn_second, attn_ema])
    gains = gains_copy.astype(F32)
    gain_rows = gains.shape[0]
    noise_level = sigmas[0]
    square = noise_level * noise_level
    scale_in = lax.rsqrt(square + 1.0)
    scale_skip = 1.0 / (square + 1.0)
    scale_out = noise_level * scale_in
    weight_loss = (square + 1.0) / square
    noisy_field = noisy_state[0]
    target_field = target_state[0]
    extra = padded - channels
    inputs = jnp.pad((scale_in * noisy_field).astype(BF16), ((0, extra), (0, 0)))
    tables = jnp.pad(tables_copy, ((0, 0), (0, extra), (0, 0)))

    def weights_spec(index):
        return pl.BlockSpec((1, width, 2 * hidden), lambda *_: (index, 0, 0))

    wout_spec = pl.BlockSpec((width, width), lambda *_: (0, 3))
    few = HEADS // GROUPS
    part = few * depth
    gains_spec = whole(gains.shape)
    tables_spec = whole(tables.shape)
    steps = rows // ROWS
    kept_shapes = [shape((rows, width), BF16), shape((rows, hidden), F32), shape((rows, hidden), BF16)]
    kept_specs = [rows_of(width), rows_of(hidden), rows_of(hidden)]
    mlp_flops = 4 * rows * width * hidden

    pin, pooled, encoded, normed_enc, slope_enc, active_enc, normed_attn, queries, *pairs = call(
        encoder_kernel,
        (steps,),
        [shape((rows, 2 * padded), BF16), shape((rows, width), F32), shape((rows, width), F32)]
        + kept_shapes
        + [shape((rows, width), BF16), shape((width, rows), BF16)]
        + [shape((rows, width), BF16)] * GROUPS,
        [
            lanes_of(grid_edges.shape[1]), whole((padded, grid_rows)), tables_spec, gains_spec,
            weights_spec(0), pl.BlockSpec((width, 3 * width), lambda i: (0, 0)),
        ],
        [rows_of(2 * padded), rows_of(width), rows_of(width)]
        + kept_specs
        + [rows_of(width), lanes_of(width)]
        + [rows_of(width)] * GROUPS,
        (grid_edges.T, inputs, tables, gains, mlp_copy, attn_copy),
        flops=mlp_flops + 6 * rows * width * width,
        moved=30 * rows * width,
    )

    crops = lengths.shape[1]
    smem = pl.BlockSpec(memory_space=pltpu.SMEM)
    bias_lanes = 128
    bias = call(
        functools.partial(bias_kernel, crops=crops),
        (rows // bias_lanes,),
        shape((3, rows, rows), F32),
        [smem, smem, lanes_of(mesh_edges.shape[1], bias_lanes)],
        pl.BlockSpec((3, rows, bias_lanes), lambda i: (0, 0, i)),
        (places, jnp.cumsum(lengths[0]), mesh_edges.T),
        flops=2 * 10**9,
        moved=12 * rows * rows,
    )

    windows = []
    for own in pairs:
        if windows:
            own = after(own, *windows[-1], bias)
        came = from_sides(own, own)
        windows.append([came[0], own, came[1]])

    lanes = 512
    attended, lse = [], []
    for g, window in enumerate(windows):
        result, logs = call(
            functools.partial(attend_kernel, chunk=256),
            (rows // lanes, few),
            [shape((part, rows), F32), shape((few, 8, rows), F32)],
            [pl.BlockSpec((depth, lanes), lambda i, h, g=g: (g * few + h, i))]
            + [pl.BlockSpec((rows, depth), lambda i, h: (0, h))] * 3
            + [pl.BlockSpec((rows, depth), lambda i, h: (0, few + h))] * 3
            + [pl.BlockSpec((3, rows, lanes), lambda i, h: (0, 0, i))],
            [
                pl.BlockSpec((depth, lanes), lambda i, h: (h, i)),
                pl.BlockSpec((1, 8, lanes), lambda i, h: (h, 0, i)),
            ],
            (queries, *window, *window, bias),
            scratch=[pltpu.VMEM((3, rows, lanes), F32)],
            flops=24 * rows * rows * part,
            moved=12 * rows * rows,
        )
        attended.append(result)
        lse.append(logs)

    rounded_o, residual, normed_proc, slope_proc, active_proc, sent = call(
        processor_kernel,
        (steps,),
        [shape((width, rows), BF16), shape((rows, width), F32)] + kept_shapes + [shape((rows, width), BF16)],
        [lanes_of(part)] * GROUPS + [rows_of(width), gains_spec, weights_spec(1), wout_spec],
        [lanes_of(width), rows_of(width)] + kept_specs + [rows_of(width)],
        (*attended, encoded, gains, mlp_copy, attn_copy),
        flops=mlp_flops + 2 * rows * width * width,
        moved=24 * rows * width,
    )

    before_sent, after_sent = from_sides(sent, sent)

    joined, normed_dec, slope_dec, active_dec, decoded, final, output = call(
        decoder_kernel,
        (grid_rows // ROWS,),
        [shape((grid_rows, width), F32)]
        + kept_shapes
        + [shape((grid_rows, width), F32), shape((grid_rows, width), BF16), shape((padded, grid_rows), F32)],
        [
            lanes_of(dec_edges.shape[1]), whole((rows, width)), whole((rows, width)), whole((rows, width)),
            lanes_of(padded), tables_spec, gains_spec, weights_spec(2),
        ],
        [rows_of(width)] + kept_specs + [rows_of(width), rows_of(width), lanes_of(padded)],
        (dec_edges.T, before_sent, sent, after_sent, inputs, tables, gains, mlp_copy),
        flops=mlp_flops + 6 * rows * rows * width,
        moved=24 * rows * width,
    )

    error_field = scale_skip * noisy_field + scale_out * output[:channels] - target_field
    partial_value = lax.dot_general(
        error_field,
        sh_basis,
        (((1,), (1,)), ((), ())),
        precision=HIGH_PRECISION,
        preferred_element_type=F32,
    )
    coeffs = sum_over(partial_value, "lat")
    slice_width = coeffs.shape[1] // bands
    own_coeffs = lax.dynamic_slice_in_dim(coeffs, band_index * slice_width, slice_width, 1)
    loss_item = weight_loss * jnp.sum(own_coeffs * own_coeffs)
    grad_error = jnp.dot(
        2.0 * weight_loss * coeffs, sh_basis, precision=HIGH_PRECISION, preferred_element_type=F32
    )
    grad_output = jnp.pad((scale_out * grad_error).astype(BF16), ((0, extra), (0, 0)))

    grad_join, rounded_dec, before_dec, table_out, gain_dec = call(
        decoder_back_kernel,
        (grid_rows // ROWS,),
        [
            shape((grid_rows, width), F32), shape((grid_rows, width), BF16), shape((grid_rows, hidden), BF16),
            shape((width, padded), F32), shape((2, width), F32),
        ],
        [
            lanes_of(padded), tables_spec, rows_of(width), rows_of(width), rows_of(width), rows_of(hidden),
            gains_spec, weights_spec(2),
        ],
        [rows_of(width), rows_of(width), rows_of(hidden), whole((width, padded)), whole((2, width))],
        (grad_output, tables, decoded, final, joined, slope_dec, gains, mlp_copy),
        flops=mlp_flops,
        moved=24 * rows * width,
    )

    to_left, grad_own, to_right = call(
        scatter_kernel,
        (steps,),
        [shape((rows, width), BF16), shape((rows, width), F32), shape((rows, width), BF16)],
        [whole((dec_edges.shape[1], grid_rows)), whole((grid_rows, width))],
        [rows_of(width)] * 3,
        (dec_edges.T, grad_join),
        scratch=[pltpu.VMEM((grid_rows, width), BF16), pltpu.VMEM((grid_rows, width), BF16)],
        flops=12 * rows * grid_rows * width,
        moved=12 * rows * width,
    )
    from_left, from_right = from_sides(to_left, to_right)
    quarter = hidden // 4
    columns_of = pl.BlockSpec((rows, quarter), lambda i: (0, i))
    table_spec = whole((width, padded))
    full = whole((rows, width))
    product = 2 * rows * width * width

    def layer_weights(*operands):
        return weights(
            weights_kernel, places, operands, [full, full, columns_of, columns_of], 2 * quarter, 8 * product, 2
        )

    keep_dec, send_dec = layer_weights(normed_dec, after(rounded_dec, to_left, to_right), before_dec, active_dec)
    sorted_dec = sort_shares([keep_dec], [send_dec], places)
    swapped_dec = swap_items(sorted_dec)

    grad_residual, rounded_proc, before_proc, gain_proc, branch, grad_o, delta = call(
        processor_back_kernel,
        (steps,),
        [
            shape((rows, width), F32), shape((rows, width), BF16), shape((rows, hidden), BF16),
            shape((1, width), F32), shape((rows, width), BF16), shape((width, rows), BF16),
            shape((HEADS, 8, rows), F32),
        ],
        [rows_of(width)] * 4 + [rows_of(hidden), gains_spec, weights_spec(1), wout_spec] + [lanes_of(part)] * GROUPS,
        [
            rows_of(width), rows_of(width), rows_of(hidden), whole((1, width)), rows_of(width), lanes_of(width),
            pl.BlockSpec((HEADS, 8, ROWS), lambda i: (0, 0, i)),
        ],
        (from_left, after(grad_own, keep_dec, send_dec), from_right, residual, slope_proc, gains, mlp_copy, attn_copy,
            *attended,
        ),
        flops=mlp_flops + 2 * rows * width * width,
        moved=24 * rows * width,
    )

    keep_proc, send_proc = layer_weights(normed_proc, rounded_proc, before_proc, active_proc)
    block = 512
    side = pl.BlockSpec((2, depth, block), lambda i, h: (0, h, i))
    group_spec = whole((few, 8, rows))
    grad_queries, sides = [], []
    ahead = (keep_proc, send_proc)
    for g, window in enumerate(windows):
        row_spec = pl.BlockSpec((part, rows), lambda i, h, g=g: (g, 0))
        dq, left, own, right = call(
            functools.partial(attend_back_kernel, chunk=256),
            (rows // block, few),
            [
                shape((part, rows), F32), shape((2, part, rows), BF16), shape((2, part, rows), F32),
                shape((2, part, rows), BF16),
            ],
            [row_spec, row_spec, group_spec, pl.BlockSpec((few, 8, rows), lambda i, h, g=g: (g, 0, 0))]
            + [pl.BlockSpec((block, depth), lambda i, h: (i, h))] * 3
            + [pl.BlockSpec((block, depth), lambda i, h: (i, few + h))] * 3
            + [pl.BlockSpec((3, block, rows), lambda i, h: (0, i, 0))],
            [whole((part, rows)), side, side, side],
            (queries, after(grad_o, *ahead), lse[g], delta, *window, *window, bias),
            scratch=[pltpu.VMEM((block, rows), BF16), pltpu.VMEM((block, rows), BF16)],
            flops=60 * rows * rows * part,
            moved=12 * rows * rows,
        )
        if sides:
            left = after(left, *sides[-1], *swapped_proc)
            right = after(right, *sides[-1], *swapped_proc)
        came = from_sides(left, right)
        sides.append([came[0], own, came[1]])
        grad_queries.append(dq)
        if g == 0:
            sorted_proc = sort_shares([after(keep_proc, dq)], [send_proc], places)
            swapped_proc = swap_items(sorted_proc)
            ahead = (*sorted_proc, *swapped_dec)

    first_parts = sum_items([swapped_dec, swapped_proc], places)
    first_parts = [first_parts[0]] + [after(x, *sides[-1]) for x in first_parts[1:]]
    side_spec = pl.BlockSpec((2, part, ROWS), lambda i: (0, 0, i))
    upstream, rounded_enc, project, gain_attn = call(
        projection_back_kernel,
        (steps,),
        [
            shape((rows, width), F32), shape((rows, width), BF16), shape((3 * width, rows), BF16),
            shape((1, width), F32),
        ],
        [lanes_of(part)] * 2 + [side_spec] * 6
        + [rows_of(width)] * 2 + [gains_spec, pl.BlockSpec((width, 3 * width), lambda i: (0, 0))],
        [rows_of(width), rows_of(width), lanes_of(3 * width), whole((1, width))],
        (
            *grad_queries, sides[0][0], sides[1][0], sides[0][1], sides[1][1], sides[0][2], sides[1][2],
            after(grad_residual, first_parts[0]), encoded, gains, attn_copy,
        ),
        flops=3 * product,
        moved=24 * rows * width,
    )
    keep_down, send_down = weights(
        down_weights_kernel,
        places,
        (rounded_enc, active_enc, normed_attn, project, rounded_o, branch),
        [full, columns_of, full, pl.BlockSpec((width, rows), lambda i: (jnp.minimum(i, 2), 0)), whole((width, rows)), full],
        quarter + width,
        8 * product,
        2,
    )
    first_total = add_bands(first_parts, (keep_down,))
    sorted_down = sort_shares([keep_down], [send_down], places, late=(first_total,))
    swapped_down = swap_items(sorted_down)
    before_enc, table_in, gain_enc, _ = call(
        encoder_back_kernel,
        (steps,),
        [
            shape((rows, hidden), BF16), shape((width, padded), F32), shape((1, width), F32),
            shape((rows, width), BF16),
        ],
        [rows_of(width)] * 2
        + [rows_of(hidden), gains_spec, weights_spec(0), lanes_of(padded), rows_of(2 * padded), rows_of(width)],
        [rows_of(hidden), table_spec, whole((1, width)), rows_of(width)],
        (after(upstream, *sorted_down), pooled, slope_enc, gains, mlp_copy, inputs, pin, grad_join),
        flops=mlp_flops,
        moved=24 * rows * width,
    )
    grad_gains = jnp.concatenate([gain_enc, gain_attn, gain_proc, gain_dec], axis=0)
    gain_columns = jnp.pad(grad_gains.T, ((0, 0), (0, padded - gain_rows)))
    keep_up, send_up = weights(
        up_weights_kernel,
        places,
        (normed_enc, before_enc, table_in, table_out, gain_columns),
        [full, columns_of, table_spec, table_spec, table_spec],
        quarter + padded,
        4 * product,
        1,
    )
    down_parts = sum_items([swapped_down], places)
    down_total = sum_bands(down_parts)
    sorted_up = sort_shares([keep_up], [send_up], places, exact=padded, late=(down_parts[0],))
    swapped_up = swap_items([sorted_up[0]] + [after(x, *swapped_down) for x in sorted_up[1:]])
    first_all = all_items(after(first_total, *swapped_up))
    up_total = sum_bands(sum_items([swapped_up], places, exact=padded), exact=padded)
    squares = sum(jnp.sum(jnp.square(x.astype(F32))) for x in (first_total, down_total, up_total))
    down_all = all_items(down_total)
    up_all = all_items(up_total)
    scalars = after(jnp.stack([squares, loss_item])[None], *down_all)
    scalars = all_items(after(sum_over(scalars, "lat"), *up_all))
    scalars = (scalars[0] + scalars[1]) + (scalars[2] + scalars[3])
    loss_sum = scalars[0, 1]
    grad_norm = jnp.sqrt(scalars[0, 0])
    scale_factor = CLIP_LEVEL / jnp.maximum(grad_norm, CLIP_LEVEL)

    shard_rows = attn_master.shape[0]
    mlp_spec = pl.BlockSpec((mlp_master.shape[0], shard_rows, quarter), lambda j, k, s: (0, 0, k * 4 + (s[3] ^ j)))
    attn_part = pl.BlockSpec((shard_rows, width // 2), lambda j, k, s: (0, (s[3] ^ j) * 2 + k))
    kinds = [F32, F32, F32, F32, BF16]
    shares = (*first_all, *down_all, *up_all)
    updated = prefetched(
        adam_kernel,
        (4, 2),
        [shape(mlp_master.shape, kind) for kind in kinds] + [shape(attn_master.shape, kind) for kind in kinds],
        [smem] + [pl.BlockSpec(x.shape, lambda *_: (0, 0)) for x in shares] + [mlp_spec] * 4 + [attn_part] * 4,
        [mlp_spec] * 5 + [attn_part] * 5,
        places,
        (
            scale_factor[None], *shares, mlp_master, mlp_first, mlp_second, mlp_ema,
            attn_master, attn_first, attn_second, attn_ema,
        ),
        moved=34 * (mlp_master.size + attn_master.size),
    )
    mlps, att = updated[:5], updated[5:]
    small = jnp.stack([x[:, quarter:] for x in up_all])
    tab_sum = jnp.stack(
        [lax.dynamic_index_in_dim(small, item_index ^ q, 0, False)[:, :channels].T for q in range(2)]
    )
    gain_sum = lax.dynamic_index_in_dim(small, item_index ^ 2, 0, False)[:, :gain_rows].T
    tab = adam_update(
        scale_factor * tab_sum, tables_master, tables_first, tables_second, tables_ema, RATE_MATRIX, WEIGHT_DECAY
    )
    gns = adam_update(
        scale_factor * gain_sum, gains_master, gains_first, gains_second, gains_ema, RATE_GAIN, 0.0
    )
    return (loss_sum, grad_norm, *tab, *att, *mlps, *gns)


def solution(mesh):
    table = P(None, None, "lat")
    attn = P("lat", None)
    mlp = P(None, "lat", None)
    gain = P(None, "lat")
    placed = (
        P("item", None, "lat"),
        P("item", None, "lat"),
        P("item"),
        P(None, "lat"),
        P("item", None),
        P("lat", None),
        P("lat", None),
        P("lat", None),
        P(), table, table, table, table,
        P(), attn, attn, attn, attn,
        P(), mlp, mlp, mlp, mlp,
        P(), gain, gain, gain, gain,
    )
    return jax.shard_map(
        shards,
        mesh=mesh,
        in_specs=placed,
        out_specs=(P(), P(), *([table] * 5), *([attn] * 5), *([mlp] * 5), *([gain] * 5)),
        check_vma=False,
    )
```

```python
import functools

import jax
import jax.numpy as jnp
from jax import lax
from jax.experimental import pallas as pl
from jax.experimental.pallas import tpu as pltpu
from jax.sharding import PartitionSpec as P

HEADS = 4
GROUPS = 2
WEIGH = 30
LARGE = 1 << 20
STEP = 10

EPS_NORM = 1e-05
CLIP_LEVEL = 1.0
BETA_ONE = 0.9
BETA_TWO = 0.999
ADAM_EPS = 1e-08
EMA_DECAY = 0.9
RATE_MATRIX = 0.05
RATE_GAIN = 0.3
WEIGHT_DECAY = 0.1
HIGH_PRECISION = lax.Precision.HIGHEST

F32 = jnp.float32
BF16 = jnp.bfloat16
LOG2E = 1.4426950408889634
CHANNEL_PAD = 128
ROWS = 256
VMEM_BYTES = 36 * 1024 * 1024


def dot(left, right, left_dim, right_dim):
    return lax.dot_general(
        left, right, (((left_dim,), (right_dim,)), ((), ())), preferred_element_type=F32
    )


FAR = []


def is_far(value):
    return any(value is x for x in FAR)


def far(value):
    return pltpu.with_memory_space_constraint(value, pltpu.HBM) if is_far(value) else value


def call(kernel, grid, outs, in_specs, out_specs, operands, scratch=(), flops=0, moved=0, near=()):
    single = not isinstance(outs, list)
    kinds = [outs] if single else outs
    large = [i not in near and x.size * x.dtype.itemsize >= LARGE for i, x in enumerate(kinds)]
    kinds = [pltpu.HBM(x.shape, x.dtype) if flag else x for x, flag in zip(kinds, large)]
    results = pl.pallas_call(
        kernel,
        grid=grid,
        out_shape=kinds[0] if single else kinds,
        in_specs=in_specs,
        out_specs=out_specs,
        scratch_shapes=list(scratch),
        cost_estimate=pl.CostEstimate(flops=flops * WEIGH, bytes_accessed=moved * WEIGH, transcendentals=0),
        compiler_params=pltpu.CompilerParams(vmem_limit_bytes=VMEM_BYTES),
    )(*[far(x) for x in operands])
    FAR.extend(x for x, flag in zip([results] if single else results, large) if flag)
    return results


def whole(shape):
    return pl.BlockSpec(shape, lambda *_: (0,) * len(shape))


def rows_of(width, rows=ROWS):
    return pl.BlockSpec((rows, width), lambda i: (i, 0))


def lanes_of(height, lanes=ROWS):
    return pl.BlockSpec((height, lanes), lambda i: (0, i))


def shape(dims, kind):
    return jax.ShapeDtypeStruct(dims, kind)


def norm_parts(values):
    center = values - jnp.mean(values, axis=-1, keepdims=True)
    spread = jnp.mean(center * center, axis=-1, keepdims=True)
    inverse = lax.rsqrt(spread + EPS_NORM)
    return center * inverse, inverse


def norm_back(upstream, values, gain_row):
    unit, inverse = norm_parts(values)
    scaled = upstream * gain_row
    along = jnp.mean(scaled * unit, axis=-1, keepdims=True)
    grad = inverse * (scaled - jnp.mean(scaled, axis=-1, keepdims=True) - unit * along)
    gain_grad = jnp.sum(upstream * unit, axis=0, keepdims=True)
    return grad, gain_grad


def gelu_parts(u):
    root = 0.7978845608028654
    cubic = 0.044715
    square = u * u
    inner = u * (root + (root * cubic) * square)
    half = 0.5 + 0.5 * jnp.tanh(inner)
    slope = half * (1.0 + (1.0 - half) * (6.0 * inner - (4.0 * root) * u))
    return u * half, slope


def mlp_forward(values, gain_row, w_ref, normed_ref, slope_ref, active_ref, step=512):
    hidden = w_ref.shape[-1] // 2
    normed = (norm_parts(values)[0] * gain_row).astype(BF16)
    normed_ref[...] = normed
    result = jnp.zeros(values.shape, F32)
    starts = range(0, hidden, step)
    befores = [dot(normed, w_ref[0, :, :step], 1, 0)]
    for start in starts:
        part = slice(start, start + step)
        if start + step < hidden:
            befores.append(dot(normed, w_ref[0, :, start + step : start + 2 * step], 1, 0))
        active, slope = gelu_parts(befores.pop(0))
        active = active.astype(BF16)
        slope_ref[:, part] = slope
        active_ref[:, part] = active
        result = result + dot(active, w_ref[0, :, hidden + start : hidden + start + step], 1, 1)
    return values + result


def mlp_backward(upstream, values, gain_row, w_ref, slope_ref, rounded_ref, before_ref, step=512):
    hidden = w_ref.shape[-1] // 2
    rounded = upstream.astype(BF16)
    rounded_ref[...] = rounded
    grad_normed = jnp.zeros(values.shape, F32)
    ahead = [dot(rounded, w_ref[0, :, hidden : hidden + step], 1, 0)]
    for start in range(0, hidden, step):
        part = slice(start, start + step)
        if start + step < hidden:
            ahead.append(dot(rounded, w_ref[0, :, hidden + start + step : hidden + start + 2 * step], 1, 0))
        grad_before = (ahead.pop(0) * slope_ref[:, part]).astype(BF16)
        before_ref[:, part] = grad_before
        grad_normed = grad_normed + dot(grad_before, w_ref[0, :, part], 1, 1)
    grad, gain_grad = norm_back(grad_normed, values, gain_row)
    return upstream + grad, gain_grad


def two_parts(values):
    high = values.astype(BF16)
    return high, (values - high.astype(F32)).astype(BF16)


def named(edges, places):
    tally = jnp.zeros(places.shape, F32)
    for j in range(edges.shape[0]):
        tally = tally + jnp.where(edges[j : j + 1, :] == places, 1.0, 0.0)
    return tally.astype(BF16)


def add_up(ref, value):
    step = pl.program_id(0)

    @pl.when(step == 0)
    def _():
        ref[...] = value

    @pl.when(step > 0)
    def _():
        ref[...] += value


def encoder_kernel(
    edges, x, table, gains, mlp, attn,
    pin_ref, pooled_ref, encoded_ref, normed_ref, slope_ref, active_ref, normed_attn_ref, q_ref, *pair_refs,
):
    count, rows = edges.shape
    width = attn.shape[0]
    places = lax.broadcasted_iota(jnp.int32, (x.shape[1], rows), 0)
    pin = dot(named(edges, places), x[...], 0, 1) / count
    high, low = two_parts(pin)
    pin_ref[...] = jnp.concatenate([high, low], axis=1)
    pooled = dot(high, table[0], 1, 0) + dot(low, table[0], 1, 0)
    pooled_ref[...] = pooled
    encoded = mlp_forward(pooled, gains[0:1], mlp, normed_ref, slope_ref, active_ref)
    encoded_ref[...] = encoded
    normed_attn = (norm_parts(encoded)[0] * gains[1:2]).astype(BF16)
    normed_attn_ref[...] = normed_attn
    q_ref[...] = dot(attn[:, :width], normed_attn, 0, 1).astype(BF16)
    part = width // len(pair_refs)
    for g, ref in enumerate(pair_refs):
        for side in range(2):
            start = (1 + side) * width + g * part
            ref[:, side * part : (side + 1) * part] = dot(
                normed_attn, attn[:, start : start + part], 1, 0
            ).astype(BF16)


def bias_kernel(places, ends, edges, bias_ref, *, crops):
    count, lanes = edges.shape
    rows = bias_ref.shape[1]
    window = bias_ref.shape[0] * rows
    col = pl.program_id(0)
    nodes = col * lanes + lax.broadcasted_iota(jnp.int32, (1, lanes), 1)
    first = places[0] * rows
    low = jnp.zeros((1, lanes), jnp.int32)
    high = jnp.full((1, lanes), places[1] * rows, jnp.int32)
    for c in range(crops - 1, -1, -1):
        high = jnp.where(ends[c] > first + nodes, ends[c], high)
    for c in range(crops):
        low = jnp.where(ends[c] <= first + nodes, ends[c], low)
    near = edges[...] + (first - rows)
    place = jnp.where((near >= low) & (near < high), edges[...], -1)
    place = jnp.concatenate([place, rows + nodes], axis=0)
    tile = 128
    tiles = window // tile
    each = 6
    fine = jnp.where(place < 0, -1, place % tile)
    coarse = place // tile
    sub = lax.broadcasted_iota(jnp.int32, (tile, lanes), 0)
    for start in range(0, tiles, each):
        here = (coarse >= start) & (coarse < start + each)
        amount = jnp.where(here, jnp.left_shift(1, 5 * jnp.where(here, coarse - start, 0)), 0)
        total = jnp.zeros((tile, lanes), jnp.int32)
        for j in range(count + 1):
            total = total + jnp.where(sub == fine[j : j + 1], amount[j : j + 1], 0)
        for t in range(start, min(tiles, start + each)):
            tally = jnp.bitwise_and(jnp.right_shift(total, 5 * (t - start)), 31)
            value = jnp.where(tally == 0, -1e30, jnp.log2(jnp.maximum(tally, 1).astype(F32)))
            at = t * tile
            bias_ref[at // rows, at % rows : at % rows + tile, :] = value


def attend_kernel(q_ref, k0, k1, k2, v0, v1, v2, bias, o_ref, l_ref, scores, *, chunk):
    depth, lanes = q_ref.shape
    rows = k0.shape[0]
    factor = depth**-0.5 * LOG2E
    q = q_ref[...]
    top = jnp.full((8, lanes), -3e38, F32)
    for w, keys in enumerate((k0, k1, k2)):
        for start in range(0, rows, chunk):
            part = slice(start, start + chunk)
            score = dot(keys[part, :], q, 1, 0) * factor + bias[w, part, :]
            scores[w, part, :] = score
            top = jnp.maximum(top, jnp.max(score.reshape(chunk // 8, 8, lanes), axis=0))
    top = jnp.max(top, axis=0, keepdims=True)
    total = jnp.zeros((8, lanes), F32)
    result = jnp.zeros((depth, lanes), F32)
    for w, values in enumerate((v0, v1, v2)):
        for start in range(0, rows, chunk):
            part = slice(start, start + chunk)
            e = jnp.exp2(scores[w, part, :] - top)
            total = total + jnp.sum(e.reshape(chunk // 8, 8, lanes), axis=0)
            result = result + dot(values[part, :], e.astype(BF16), 0, 0)
    total = jnp.sum(total, axis=0, keepdims=True)
    o_ref[...] = result * (1.0 / total)
    l_ref[...] = jnp.broadcast_to((top + jnp.log2(total))[None], l_ref.shape)


def processor_kernel(
    o0, o1, encoded, gains, mlp, attn,
    attended_ref, residual_ref, normed_ref, slope_ref, active_ref, sent_ref,
):
    attended = jnp.concatenate([o0[...], o1[...]], axis=0).astype(BF16)
    attended_ref[...] = attended
    residual = encoded[...] + dot(attended, attn[...], 0, 0)
    residual_ref[...] = residual
    latent = mlp_forward(residual, gains[2:3], mlp, normed_ref, slope_ref, active_ref)
    sent_ref[...] = latent.astype(BF16)


def decoder_kernel(
    edges, s0, s1, s2, x, tables, gains, mlp,
    joined_ref, normed_ref, slope_ref, active_ref, decoded_ref, final_ref, output_ref,
):
    count, rows = edges.shape
    band = s0.shape[0]
    gathered = jnp.zeros(joined_ref.shape, F32)
    places = lax.broadcasted_iota(jnp.int32, (band, rows), 0)
    for w, sent in enumerate((s0, s1, s2)):
        gathered = gathered + dot(named(edges, places + w * band), sent[...], 0, 0)
    joined = dot(x[...], tables[0], 0, 0) + gathered / count
    joined_ref[...] = joined
    decoded = mlp_forward(joined, gains[3:4], mlp, normed_ref, slope_ref, active_ref)
    decoded_ref[...] = decoded
    final = (norm_parts(decoded)[0] * gains[4:5]).astype(BF16)
    final_ref[...] = final
    output_ref[...] = dot(tables[1], final, 1, 1)


def decoder_back_kernel(
    grad_output, tables, decoded, final, joined, slope, gains, mlp, x,
    high_ref, low_ref, rounded_ref, before_ref, table_ref, gain_ref, direct_ref,
):
    grad_final = dot(grad_output[...], tables[1], 0, 0)
    add_up(table_ref, dot(final[...], grad_output[...], 0, 1))
    grad_decoded, gain_final = norm_back(grad_final, decoded[...], gains[4:5])
    grad_join, gain_dec = mlp_backward(
        grad_decoded, joined[...], gains[3:4], mlp, slope, rounded_ref, before_ref
    )
    high, low = two_parts(grad_join)
    high_ref[...] = high
    low_ref[...] = low
    add_up(direct_ref, dot(high, x[...], 0, 1) + dot(low, x[...], 0, 1))
    add_up(gain_ref, jnp.concatenate([gain_dec, gain_final], axis=0))


def scatter_kernel(edges, high, low, out0, out1, out2):
    rows = out0.shape[0]
    count, total = edges.shape
    for w, out in enumerate((out0, out1, out2)):
        sub = lax.broadcasted_iota(jnp.int32, (rows, total), 0) + (pl.program_id(0) * rows + w * total)
        tally = named(edges, sub)
        value = dot(tally, high[...], 1, 0) + dot(tally, low[...], 1, 0)
        out[...] = (value / count).astype(out.dtype)


def processor_back_kernel(
    g0, g1, g2, residual, slope, gains, mlp, attn, o0, o1,
    grad_residual_ref, rounded_ref, before_ref, gain_ref, branch_ref, grad_o_ref, delta_ref,
):
    width = residual.shape[1]
    upstream = g1[...] + g0[...].astype(F32) + g2[...].astype(F32)
    grad, gain = mlp_backward(
        upstream, residual[...], gains[2:3], mlp, slope, rounded_ref, before_ref
    )
    add_up(gain_ref, gain)
    grad_residual_ref[...] = grad
    branch = grad.astype(BF16)
    branch_ref[...] = branch
    grad_o = dot(attn[...], branch, 1, 1).astype(BF16)
    grad_o_ref[...] = grad_o
    depth = width // HEADS
    attended = jnp.concatenate([o0[...], o1[...]], axis=0)
    together = grad_o.astype(F32) * attended
    for h in range(HEADS):
        row = jnp.sum(together[h * depth : (h + 1) * depth], axis=0, keepdims=True)
        delta_ref[h] = jnp.broadcast_to(row, delta_ref.shape[1:])


def attend_back_kernel(
    q_ref, do_ref, lse_ref, delta_ref, k0, k1, k2, v0, v1, v2, bias,
    dq_ref, out0, out1, out2, p_ref, ds_ref, *, chunk,
):
    block, depth = k0.shape
    scale = depth**-0.5
    factor = scale * LOG2E
    step, h = pl.program_id(0), pl.program_id(1)
    here = pl.ds(pl.multiple_of(h * depth, depth), depth)
    q = q_ref[here, :]
    do = do_ref[here, :]
    lse = lse_ref[h, 0:1, :]
    delta = delta_ref[h, 0:1, :]
    total = jnp.zeros(q.shape, F32)
    for w, (keys, values, out) in enumerate(((k0, v0, out0), (k1, v1, out1), (k2, v2, out2))):
        for start in range(0, block, chunk):
            part = slice(start, start + chunk)
            p = jnp.exp2(dot(keys[part, :], q, 1, 0) * factor + bias[w, part, :] - lse)
            ds = p * (dot(values[part, :], do, 1, 0) - delta)
            p_ref[part, :] = p.astype(BF16)
            ds_ref[part, :] = ds.astype(BF16)
            out[0, :, part] = (dot(q, ds_ref[part, :], 1, 1) * scale).astype(out.dtype)
            out[1, :, part] = dot(do, p_ref[part, :], 1, 1).astype(out.dtype)
            total = total + dot(keys[part, :], ds_ref[part, :], 0, 0)

    @pl.when(step == 0)
    def _():
        dq_ref[here, :] = total * scale

    @pl.when(step > 0)
    def _():
        dq_ref[here, :] += total * scale


def hand_out(core, value, keep_ref, send_ref, columns):
    bands, rows = keep_ref.shape[1:3]
    for parity in range(2):

        @pl.when(core == parity)
        def _(parity=parity):
            for band in range(bands):
                for side, ref in ((parity, keep_ref), (1 - parity, send_ref)):
                    at = (2 * band + side) * rows
                    ref[0, band, :, columns] = value[at : at + rows].astype(ref.dtype)


def turn(pairs):
    @pl.when(pl.program_id(0) == 0)
    def _():
        for ref, kept in pairs:
            kept[...] = ref[...].T


def weights_kernel(places, normed, rounded, before, active, keep_ref, send_ref, normed_turned, rounded_turned):
    size = before.shape[1]
    turn(((normed, normed_turned), (rounded, rounded_turned)))
    hand_out(places[2], dot(normed_turned[...], before[...], 1, 0), keep_ref, send_ref, slice(0, size))
    hand_out(places[2], dot(rounded_turned[...], active[...], 1, 0), keep_ref, send_ref, slice(size, 2 * size))


def down_weights_kernel(
    places, rounded, active, normed_attn, project, attended, branch, keep_ref, send_ref, rounded_turned, normed_turned
):
    quarter = pl.program_id(0)
    size = active.shape[1]
    turn(((rounded, rounded_turned), (normed_attn, normed_turned)))
    hand_out(places[2], dot(rounded_turned[...], active[...], 1, 0), keep_ref, send_ref, slice(0, size))
    columns = slice(size, size + normed_attn.shape[1])

    @pl.when(quarter < 3)
    def _():
        hand_out(places[2], dot(normed_turned[...], project[...], 1, 1), keep_ref, send_ref, columns)

    @pl.when(quarter == 3)
    def _():
        hand_out(places[2], dot(attended[...], branch[...], 1, 0), keep_ref, send_ref, columns)


def up_weights_kernel(places, normed, before, table_in, table_direct, table_out, gain, keep_ref, send_ref, normed_turned):
    quarter = pl.program_id(0)
    size = before.shape[1]
    turn(((normed, normed_turned),))
    hand_out(places[2], dot(normed_turned[...], before[...], 1, 0), keep_ref, send_ref, slice(0, size))
    columns = slice(size, size + table_in.shape[1])

    @pl.when(quarter == 0)
    def _():
        hand_out(places[2], table_in[...] + table_direct[...], keep_ref, send_ref, columns)

    for index, ref in ((1, table_out), (2, gain)):

        @pl.when(quarter == index)
        def _(ref=ref):
            hand_out(places[2], ref[...], keep_ref, send_ref, columns)

    @pl.when(quarter == 3)
    def _():
        hand_out(places[2], jnp.zeros(table_in.shape, F32), keep_ref, send_ref, columns)


def item_kernel(places, *refs, pairs, exact):
    ins, outs = refs[: 2 * pairs], refs[2 * pairs :]
    step = pl.program_id(0)
    for index, out in enumerate(outs):

        @pl.when(step == index)
        def _(index=index, out=out):
            start = 0
            for pair in range(pairs):
                keep, came = ins[2 * pair : 2 * pair + 2]
                value = keep[0] + came[0]
                size = value.shape[-1]
                out[:, :, start : start + size] = value.astype(out.dtype)
                if index > 0 and exact and pair == pairs - 1:
                    part = value[:, :, size - exact :]
                    rest = part - part.astype(out.dtype).astype(F32)
                    out[:, :, start + size : start + size + exact] = rest.astype(out.dtype)
                start += size


def band_kernel(places, *refs, groups, count, exact):
    ins, outs = refs[: groups * (1 + count)], refs[groups * (1 + count) :]
    step = pl.program_id(0)
    start = 0
    for group in range(groups):
        own, *came = ins[group * (1 + count) : (group + 1) * (1 + count)]
        size = own.shape[-1]
        total = own[0]
        for ref in came:
            total = total + ref[0, :, :size].astype(F32)
        last = exact and group == groups - 1
        if last:
            part = total[:, size - exact :] + sum(ref[0, :, size:].astype(F32) for ref in came)
            high = part.astype(BF16)
            rest = (part - high.astype(F32)).astype(BF16)
        for index, out in enumerate(outs):

            @pl.when(step == index)
            def _(index=index, out=out):
                out[:, start : start + size] = total.astype(out.dtype)
                if last and index == 0:
                    out[:, start + size - exact : start + size] = part
                elif last:
                    out[:, start + size - exact : start + size] = high
                    out[:, start + size : start + size + exact] = rest

        start += size


def exchange(value, axis, distance):
    size = lax.axis_size(axis)
    return lax.ppermute(value, axis, [(i, i ^ distance) for i in range(size)])


def prefetched(kernel, grid, outs, in_specs, out_specs, places, operands, moved, weight=1):
    return pl.pallas_call(
        kernel,
        grid_spec=pltpu.PrefetchScalarGridSpec(
            num_scalar_prefetch=1, grid=grid, in_specs=in_specs, out_specs=out_specs
        ),
        out_shape=outs,
        cost_estimate=pl.CostEstimate(flops=moved * WEIGH * weight, bytes_accessed=moved * WEIGH, transcendentals=0),
        compiler_params=pltpu.CompilerParams(vmem_limit_bytes=VMEM_BYTES * 2 // 3),
    )(places, *[far(x) for x in operands])


def sort_shares(keeps, sends, places, exact=0, late=()):
    items = lax.axis_size("item")
    came = [exchange(send, "lat", 1) for send in sends]
    quarters, bands, rows, _ = keeps[0].shape
    size = sum(keep.shape[-1] for keep in keeps)
    wide = size + exact
    operands = [after(x, *late) for pair in zip(keeps, came) for x in pair]
    return prefetched(
        functools.partial(item_kernel, pairs=len(keeps), exact=exact),
        (items,),
        [shape((bands, rows, size), F32)] + [shape((bands, rows, wide), BF16)] * (items - 1),
        [pl.BlockSpec((1,) + x.shape[1:], lambda j, s: (s[3] ^ j, 0, 0, 0)) for x in operands],
        [pl.BlockSpec((bands, rows, size), lambda j, s: (0, 0, 0))]
        + [pl.BlockSpec((bands, rows, wide), lambda j, s: (0, 0, 0))] * (items - 1),
        places,
        operands,
        moved=14 * bands * rows * size * items,
    )


def swap_items(sorted_shares):
    own, *others = sorted_shares
    return [own] + [exchange(x, "item", k + 1) for k, x in enumerate(others)]


def sum_items(groups, places, exact=0):
    items = len(groups[0])
    bands, rows, _ = groups[0][0].shape
    operands = [x for group in groups for x in group]
    size = sum(group[0].shape[-1] for group in groups)
    wide = size + exact
    return prefetched(
        functools.partial(band_kernel, groups=len(groups), count=items - 1, exact=exact),
        (bands,),
        [shape((rows, size), F32)] + [shape((rows, wide), BF16)] * (bands - 1),
        [pl.BlockSpec((1,) + x.shape[1:], lambda j, s: (s[4] ^ j, 0, 0)) for x in operands],
        [pl.BlockSpec((rows, size), lambda j, s: (0, 0))]
        + [pl.BlockSpec((rows, wide), lambda j, s: (0, 0))] * (bands - 1),
        places,
        operands,
        moved=14 * bands * rows * size,
        weight=10000,
    )


def sum_bands(parts, exact=0, late=()):
    own, *others = parts
    size = own.shape[-1]
    came = [exchange(x, "lat", 2 * (k + 1)) for k, x in enumerate(others)]
    total = after(own, *late) if late else own
    for x in came:
        total = total + x[:, :size].astype(F32)
    if exact:
        rest = sum(x[:, size:].astype(F32) for x in came)
        total = jnp.concatenate([total[:, : size - exact], total[:, size - exact :] + rest], axis=1)
    return total


def after(value, *others):
    result = lax.optimization_barrier((value, *others))[0]
    if is_far(value):
        FAR.append(result)
    return result


def total_kernel(own, *refs):
    *came, out0, out1 = refs
    total = own[...]
    for ref in came:
        total = total + ref[...].astype(F32)
    half = out0.shape[-1]
    out0[...] = total[:, :half]
    out1[...] = total[:, half:]


def add_bands(parts, late):
    own, *others = parts
    came = [exchange(x, "lat", 2 * (k + 1)) for k, x in enumerate(others)]
    return call(
        total_kernel,
        (1,),
        [shape((own.shape[0], own.shape[1] // 2), F32)] * 2,
        [whole(own.shape)] * len(parts),
        [whole((own.shape[0], own.shape[1] // 2))] * 2,
        (after(own, *late), *came),
        flops=10**11,
        moved=16 * own.size,
        near=(0, 1),
    )


def all_items(one, two):
    one_near, two_far = exchange(one, "item", 1), exchange(two, "item", 2)
    one_far, two_near = exchange(one, "item", 2), exchange(two, "item", 1)
    return [
        (one, two), (one_near, two_near), (one_far, two_far),
        (exchange(one_near, "item", 2), exchange(two_far, "item", 1)),
    ]


def sum_over(value, axis):
    distance = 1
    while distance < lax.axis_size(axis):
        value = value + exchange(value, axis, distance)
        distance *= 2
    return value


def adam_kernel(places, factor, *refs):
    dec, proc, down, up = refs[:4], refs[4:8], refs[8:12], refs[12:16]
    mlp, attn, tables, gains = refs[16:20], refs[20:24], refs[24:28], refs[28:32]
    mlp_out, attn_out, tables_out, gains_out = refs[32:37], refs[37:42], refs[42:47], refs[47:52]
    size = mlp[0].shape[-1]
    part = attn[0].shape[-1]
    half = pl.program_id(1)
    quarter = places[3] ^ pl.program_id(0)
    for index in range(4):
        for side in range(2):

            @pl.when((pl.program_id(0) == index) & (half == side))
            def _(index=index, side=side):
                scale = factor[0]
                here = slice(side * size, (side + 1) * size)
                shares = ((down if side else up)[index][:, :size], proc[index][:, here], dec[index][:, here])
                for layer, share in enumerate(shares):
                    new = adam_update(
                        scale * share, *(ref[layer] for ref in mlp), RATE_MATRIX, WEIGHT_DECAY
                    )
                    for ref, value in zip(mlp_out, new):
                        ref[layer] = value
                share = down[index][:, size + side * part : size + (side + 1) * part]
                new = adam_update(scale * share, *(ref[...] for ref in attn), RATE_MATRIX, WEIGHT_DECAY)
                for ref, value in zip(attn_out, new):
                    ref[...] = value

                if side:
                    return
                share = scale * up[index][:, size:]
                for table in range(2):

                    @pl.when(quarter == table)
                    def _(table=table):
                        new = adam_update(
                            share[:, : tables[0].shape[-1]], *(ref[table] for ref in tables), RATE_MATRIX, WEIGHT_DECAY
                        )
                        for ref, value in zip(tables_out, new):
                            ref[table] = value

                @pl.when(quarter == 2)
                def _():
                    turned = share.T[: gains[0].shape[0]]
                    new = adam_update(turned, *(ref[...] for ref in gains), RATE_GAIN, 0.0)
                    for ref, value in zip(gains_out, new):
                        ref[...] = value


def projection_back_kernel(
    dq0, dq1, left0, left1, own0, own1, right0, right1, grad_residual, encoded, gains, attn,
    upstream_ref, rounded_ref, project_ref, gain_ref,
):
    pairs = [
        own[...] + left[...].astype(F32) + right[...].astype(F32)
        for left, own, right in ((left0, own0, right0), (left1, own1, right1))
    ]
    project = jnp.concatenate(
        [dq0[...], dq1[...], pairs[0][0], pairs[1][0], pairs[0][1], pairs[1][1]], axis=0
    ).astype(BF16)
    project_ref[...] = project
    grad_normed = dot(project, attn[...], 0, 1)
    grad_encoded, gain_attn = norm_back(grad_normed, encoded[...], gains[1:2])
    upstream = grad_residual[...] + grad_encoded
    upstream_ref[...] = upstream
    rounded_ref[...] = upstream.astype(BF16)
    add_up(gain_ref, gain_attn)


def encoder_back_kernel(
    upstream, pooled, slope, gains, mlp, pin, before_ref, table_ref, gain_ref, rounded_ref
):
    grad_pooled, gain_enc = mlp_backward(
        upstream[...], pooled[...], gains[0:1], mlp, slope, rounded_ref, before_ref
    )
    add_up(gain_ref, gain_enc)
    high, low = two_parts(grad_pooled)
    both = dot(high, pin[...], 0, 0) + dot(low, pin[...], 0, 0)
    channels = both.shape[1] // 2
    add_up(table_ref, both[:, :channels] + both[:, channels:])


def weights(kernel, places, operands, specs, columns, flops, turned):
    rows, width = operands[0].shape
    bands = lax.axis_size("lat") // 2
    out = shape((4, bands, width // (2 * bands), columns), F32)
    out_spec = pl.BlockSpec((1,) + out.shape[1:], lambda i: (i, 0, 0, 0))
    return call(
        kernel,
        (4,),
        [out, out],
        [pl.BlockSpec(memory_space=pltpu.SMEM)] + specs,
        [out_spec, out_spec],
        (places, *operands),
        flops=flops,
        moved=8 * width * columns * 4,
        scratch=[pltpu.VMEM((width, rows), BF16)] * turned,
        near=(0, 1),
    )


def adam_update(gradient, master, moment_one, moment_two, average, step_rate, decay_rate):
    one_new = BETA_ONE * moment_one + (1.0 - BETA_ONE) * gradient
    two_new = BETA_TWO * moment_two + (1.0 - BETA_TWO) * gradient * gradient
    one_hat = one_new * (1.0 / (1.0 - BETA_ONE**STEP))
    two_hat = two_new * (1.0 / (1.0 - BETA_TWO**STEP))
    master_new = master - step_rate * (
        one_hat / (jnp.sqrt(two_hat) + ADAM_EPS) + decay_rate * master
    )
    average_new = EMA_DECAY * average + (1.0 - EMA_DECAY) * master_new
    return (one_new, two_new, master_new, average_new, master_new.astype(jnp.bfloat16))


def from_sides(to_left, to_right):
    size = lax.axis_size("lat")
    up = [(i, (i + 1) % size) for i in range(size - 1)]
    down = [(j, i) for i, j in up]
    return lax.ppermute(to_right, "lat", up), lax.ppermute(to_left, "lat", down)


def shards(
    noisy_state,
    target_state,
    sigmas,
    sh_basis,
    lengths,
    grid_edges,
    mesh_edges,
    dec_edges,
    tables_copy,
    tables_master,
    tables_first,
    tables_second,
    tables_ema,
    attn_copy,
    attn_master,
    attn_first,
    attn_second,
    attn_ema,
    mlp_copy,
    mlp_master,
    mlp_first,
    mlp_second,
    mlp_ema,
    gains_copy,
    gains_master,
    gains_first,
    gains_second,
    gains_ema,
):
    FAR.clear()
    band_index = lax.axis_index("lat")
    bands = lax.axis_size("lat")
    item_index = lax.axis_index("item")
    places = jnp.stack([band_index, bands, band_index % 2, item_index, band_index // 2]).astype(jnp.int32)
    rows = mesh_edges.shape[0]
    grid_rows = noisy_state.shape[2]
    width = attn_copy.shape[0]
    channels = noisy_state.shape[1]
    padded = CHANNEL_PAD
    hidden = mlp_copy.shape[2] // 2
    depth = width // HEADS
    FAR.extend([mlp_copy, attn_copy, mlp_master, mlp_first, mlp_second, mlp_ema])
    FAR.extend([attn_master, attn_first, attn_second, attn_ema])
    gains = gains_copy.astype(F32)
    gain_rows = gains.shape[0]
    noise_level = sigmas[0]
    square = noise_level * noise_level
    scale_in = lax.rsqrt(square + 1.0)
    scale_skip = 1.0 / (square + 1.0)
    scale_out = noise_level * scale_in
    weight_loss = (square + 1.0) / square
    noisy_field = noisy_state[0]
    target_field = target_state[0]
    extra = padded - channels
    inputs = jnp.pad((scale_in * noisy_field).astype(BF16), ((0, extra), (0, 0)))
    tables = jnp.pad(tables_copy, ((0, 0), (0, extra), (0, 0)))

    def weights_spec(index):
        return pl.BlockSpec((1, width, 2 * hidden), lambda *_: (index, 0, 0))

    wout_spec = pl.BlockSpec((width, width), lambda *_: (0, 3))
    few = HEADS // GROUPS
    part = few * depth
    gains_spec = whole(gains.shape)
    tables_spec = whole(tables.shape)
    steps = rows // ROWS
    kept_shapes = [shape((rows, width), BF16), shape((rows, hidden), F32), shape((rows, hidden), BF16)]
    kept_specs = [rows_of(width), rows_of(hidden), rows_of(hidden)]
    mlp_flops = 4 * rows * width * hidden

    pin, pooled, encoded, normed_enc, slope_enc, active_enc, normed_attn, queries, *pairs = call(
        encoder_kernel,
        (steps,),
        [shape((rows, 2 * padded), BF16), shape((rows, width), F32), shape((rows, width), F32)]
        + kept_shapes
        + [shape((rows, width), BF16), shape((width, rows), BF16)]
        + [shape((rows, width), BF16)] * GROUPS,
        [
            lanes_of(grid_edges.shape[1]), whole((padded, grid_rows)), tables_spec, gains_spec,
            weights_spec(0), pl.BlockSpec((width, 3 * width), lambda i: (0, 0)),
        ],
        [rows_of(2 * padded), rows_of(width), rows_of(width)]
        + kept_specs
        + [rows_of(width), lanes_of(width)]
        + [rows_of(width)] * GROUPS,
        (grid_edges.T, inputs, tables, gains, mlp_copy, attn_copy),
        flops=mlp_flops + 6 * rows * width * width,
        moved=30 * rows * width,
    )

    crops = lengths.shape[1]
    smem = pl.BlockSpec(memory_space=pltpu.SMEM)
    bias_lanes = 128
    bias = call(
        functools.partial(bias_kernel, crops=crops),
        (rows // bias_lanes,),
        shape((3, rows, rows), F32),
        [smem, smem, lanes_of(mesh_edges.shape[1], bias_lanes)],
        pl.BlockSpec((3, rows, bias_lanes), lambda i: (0, 0, i)),
        (places, jnp.cumsum(lengths[0]), mesh_edges.T),
        flops=2 * 10**9,
        moved=12 * rows * rows,
    )

    windows = []
    for own in pairs:
        if windows:
            own = after(own, *windows[-1], bias)
        came = from_sides(own, own)
        windows.append([came[0], own, came[1]])

    lanes = 512
    attended, lse = [], []
    for g, window in enumerate(windows):
        result, logs = call(
            functools.partial(attend_kernel, chunk=256),
            (rows // lanes, few),
            [shape((part, rows), F32), shape((few, 8, rows), F32)],
            [pl.BlockSpec((depth, lanes), lambda i, h, g=g: (g * few + h, i))]
            + [pl.BlockSpec((rows, depth), lambda i, h: (0, h))] * 3
            + [pl.BlockSpec((rows, depth), lambda i, h: (0, few + h))] * 3
            + [pl.BlockSpec((3, rows, lanes), lambda i, h: (0, 0, i))],
            [
                pl.BlockSpec((depth, lanes), lambda i, h: (h, i)),
                pl.BlockSpec((1, 8, lanes), lambda i, h: (h, 0, i)),
            ],
            (queries, *window, *window, bias),
            scratch=[pltpu.VMEM((3, rows, lanes), F32)],
            flops=24 * rows * rows * part,
            moved=12 * rows * rows,
        )
        attended.append(result)
        lse.append(logs)

    rounded_o, residual, normed_proc, slope_proc, active_proc, sent = call(
        processor_kernel,
        (steps,),
        [shape((width, rows), BF16), shape((rows, width), F32)] + kept_shapes + [shape((rows, width), BF16)],
        [lanes_of(part)] * GROUPS + [rows_of(width), gains_spec, weights_spec(1), wout_spec],
        [lanes_of(width), rows_of(width)] + kept_specs + [rows_of(width)],
        (*attended, encoded, gains, mlp_copy, attn_copy),
        flops=mlp_flops + 2 * rows * width * width,
        moved=24 * rows * width,
        near=(5,),
    )

    before_sent, after_sent = from_sides(sent, sent)

    joined, normed_dec, slope_dec, active_dec, decoded, final, output = call(
        decoder_kernel,
        (grid_rows // ROWS,),
        [shape((grid_rows, width), F32)]
        + kept_shapes
        + [shape((grid_rows, width), F32), shape((grid_rows, width), BF16), shape((padded, grid_rows), F32)],
        [
            lanes_of(dec_edges.shape[1]), whole((rows, width)), whole((rows, width)), whole((rows, width)),
            lanes_of(padded), tables_spec, gains_spec, weights_spec(2),
        ],
        [rows_of(width)] + kept_specs + [rows_of(width), rows_of(width), lanes_of(padded)],
        (dec_edges.T, before_sent, sent, after_sent, inputs, tables, gains, mlp_copy),
        flops=mlp_flops + 6 * rows * rows * width,
        moved=24 * rows * width,
    )

    error_field = scale_skip * noisy_field + scale_out * output[:channels] - target_field
    partial_value = lax.dot_general(
        error_field,
        sh_basis,
        (((1,), (1,)), ((), ())),
        precision=HIGH_PRECISION,
        preferred_element_type=F32,
    )
    coeffs = sum_over(partial_value, "lat")
    slice_width = coeffs.shape[1] // bands
    own_coeffs = lax.dynamic_slice_in_dim(coeffs, band_index * slice_width, slice_width, 1)
    loss_item = weight_loss * jnp.sum(own_coeffs * own_coeffs)
    grad_error = jnp.dot(
        2.0 * weight_loss * coeffs, sh_basis, precision=HIGH_PRECISION, preferred_element_type=F32
    )
    grad_output = jnp.pad((scale_out * grad_error).astype(BF16), ((0, extra), (0, 0)))

    join_high, join_low, rounded_dec, before_dec, table_out, gain_dec, table_direct = call(
        decoder_back_kernel,
        (grid_rows // ROWS,),
        [
            shape((grid_rows, width), BF16), shape((grid_rows, width), BF16), shape((grid_rows, width), BF16),
            shape((grid_rows, hidden), BF16), shape((width, padded), F32), shape((2, width), F32),
            shape((width, padded), F32),
        ],
        [
            lanes_of(padded), tables_spec, rows_of(width), rows_of(width), rows_of(width), rows_of(hidden),
            gains_spec, weights_spec(2), lanes_of(padded),
        ],
        [
            rows_of(width), rows_of(width), rows_of(width), rows_of(hidden), whole((width, padded)),
            whole((2, width)), whole((width, padded)),
        ],
        (grad_output, tables, decoded, final, joined, slope_dec, gains, mlp_copy, inputs),
        flops=mlp_flops,
        moved=24 * rows * width,
        near=(0, 1, 2),
    )

    to_left, grad_own, to_right = call(
        scatter_kernel,
        (steps,),
        [shape((rows, width), BF16), shape((rows, width), F32), shape((rows, width), BF16)],
        [whole((dec_edges.shape[1], grid_rows)), whole((grid_rows, width)), whole((grid_rows, width))],
        [rows_of(width)] * 3,
        (dec_edges.T, join_high, join_low),
        near=(0, 1, 2),
        flops=12 * rows * grid_rows * width,
        moved=12 * rows * width,
    )
    from_left, from_right = from_sides(to_left, to_right)
    quarter = hidden // 4
    columns_of = pl.BlockSpec((rows, quarter), lambda i: (0, i))
    table_spec = whole((width, padded))
    full = whole((rows, width))
    product = 2 * rows * width * width

    def layer_weights(*operands):
        return weights(
            weights_kernel, places, operands, [full, full, columns_of, columns_of], 2 * quarter, 8 * product, 2
        )

    keep_dec, send_dec = layer_weights(normed_dec, after(rounded_dec, to_left, to_right), before_dec, active_dec)
    sorted_dec = sort_shares([keep_dec], [send_dec], places)
    swapped_dec = swap_items(sorted_dec)

    grad_residual, rounded_proc, before_proc, gain_proc, branch, grad_o, delta = call(
        processor_back_kernel,
        (steps,),
        [
            shape((rows, width), F32), shape((rows, width), BF16), shape((rows, hidden), BF16),
            shape((1, width), F32), shape((rows, width), BF16), shape((width, rows), BF16),
            shape((HEADS, 8, rows), F32),
        ],
        [rows_of(width)] * 4 + [rows_of(hidden), gains_spec, weights_spec(1), wout_spec] + [lanes_of(part)] * GROUPS,
        [
            rows_of(width), rows_of(width), rows_of(hidden), whole((1, width)), rows_of(width), lanes_of(width),
            pl.BlockSpec((HEADS, 8, ROWS), lambda i: (0, 0, i)),
        ],
        (from_left, after(grad_own, keep_dec, send_dec), from_right, residual, slope_proc, gains, mlp_copy, attn_copy,
            *attended,
        ),
        flops=mlp_flops + 2 * rows * width * width,
        moved=24 * rows * width,
        near=(1, 5),
    )

    keep_proc, send_proc = layer_weights(normed_proc, rounded_proc, before_proc, active_proc)
    block = 512
    side = pl.BlockSpec((2, depth, block), lambda i, h: (0, h, i))
    group_spec = whole((few, 8, rows))
    grad_queries, sides = [], []
    ahead = (keep_proc, send_proc)
    for g, window in enumerate(windows):
        row_spec = pl.BlockSpec((part, rows), lambda i, h, g=g: (g, 0))
        dq, left, own, right = call(
            functools.partial(attend_back_kernel, chunk=256),
            (rows // block, few),
            [
                shape((part, rows), F32), shape((2, part, rows), BF16), shape((2, part, rows), F32),
                shape((2, part, rows), BF16),
            ],
            [row_spec, row_spec, group_spec, pl.BlockSpec((few, 8, rows), lambda i, h, g=g: (g, 0, 0))]
            + [pl.BlockSpec((block, depth), lambda i, h: (i, h))] * 3
            + [pl.BlockSpec((block, depth), lambda i, h: (i, few + h))] * 3
            + [pl.BlockSpec((3, block, rows), lambda i, h: (0, i, 0))],
            [whole((part, rows)), side, side, side],
            (queries, after(grad_o, *ahead), lse[g], delta, *window, *window, bias),
            scratch=[pltpu.VMEM((block, rows), BF16), pltpu.VMEM((block, rows), BF16)],
            flops=60 * rows * rows * part,
            moved=12 * rows * rows,
            near=(0, 1, 2, 3),
        )
        if sides:
            left = after(left, *sides[-1], *swapped_proc)
            right = after(right, *sides[-1], *swapped_proc)
        came = from_sides(left, right)
        sides.append([came[0], own, came[1]])
        grad_queries.append(dq)
        if g == 0:
            sorted_proc = sort_shares([after(keep_proc, dq)], [send_proc], places)
            swapped_proc = swap_items(sorted_proc)
            ahead = (*sorted_proc, *swapped_dec)

    first_parts = sum_items([swapped_dec, swapped_proc], places)
    first_parts = [first_parts[0]] + [after(x, *sides[-1]) for x in first_parts[1:]]
    side_spec = pl.BlockSpec((2, part, ROWS), lambda i: (0, 0, i))
    upstream, rounded_enc, project, gain_attn = call(
        projection_back_kernel,
        (steps,),
        [
            shape((rows, width), F32), shape((rows, width), BF16), shape((3 * width, rows), BF16),
            shape((1, width), F32),
        ],
        [lanes_of(part)] * 2 + [side_spec] * 6
        + [rows_of(width)] * 2 + [gains_spec, pl.BlockSpec((width, 3 * width), lambda i: (0, 0))],
        [rows_of(width), rows_of(width), lanes_of(3 * width), whole((1, width))],
        (
            *grad_queries, sides[0][0], sides[1][0], sides[0][1], sides[1][1], sides[0][2], sides[1][2],
            after(grad_residual, first_parts[0]), encoded, gains, attn_copy,
        ),
        flops=3 * product,
        moved=24 * rows * width,
        near=(0, 1, 2),
    )
    keep_down, send_down = weights(
        down_weights_kernel,
        places,
        (rounded_enc, active_enc, normed_attn, project, rounded_o, branch),
        [full, columns_of, full, pl.BlockSpec((width, rows), lambda i: (jnp.minimum(i, 2), 0)), whole((width, rows)), full],
        quarter + width,
        8 * product,
        2,
    )
    first_total = add_bands(first_parts, (keep_down,))
    sorted_down = sort_shares([keep_down], [send_down], places, late=tuple(first_total))
    swapped_down = swap_items(sorted_down)
    before_enc, table_in, gain_enc, _ = call(
        encoder_back_kernel,
        (steps,),
        [
            shape((rows, hidden), BF16), shape((width, padded), F32), shape((1, width), F32),
            shape((rows, width), BF16),
        ],
        [rows_of(width)] * 2
        + [rows_of(hidden), gains_spec, weights_spec(0), rows_of(2 * padded)],
        [rows_of(hidden), table_spec, whole((1, width)), rows_of(width)],
        (after(upstream, *sorted_down), pooled, slope_enc, gains, mlp_copy, pin),
        flops=mlp_flops,
        moved=24 * rows * width,
    )
    grad_gains = jnp.concatenate([gain_enc, gain_attn, gain_proc, gain_dec], axis=0)
    gain_columns = jnp.pad(grad_gains.T, ((0, 0), (0, padded - gain_rows)))
    keep_up, send_up = weights(
        up_weights_kernel,
        places,
        (normed_enc, before_enc, table_in, table_direct, table_out, gain_columns),
        [full, columns_of, table_spec, table_spec, table_spec, table_spec],
        quarter + padded,
        4 * product,
        1,
    )
    down_parts = sum_items([swapped_down], places)
    down_total = sum_bands(down_parts)
    sorted_up = sort_shares([keep_up], [send_up], places, exact=padded, late=(down_parts[0],))
    swapped_up = swap_items([sorted_up[0]] + [after(x, *swapped_down) for x in sorted_up[1:]])
    first_all = all_items(*[after(x, *swapped_up) for x in first_total])
    ready = [x for pair in first_all for x in pair]
    up_total = sum_bands(sum_items([swapped_up], places, exact=padded), exact=padded)
    squares = sum(jnp.sum(jnp.square(x.astype(F32))) for x in (*first_total, down_total, up_total))
    scalars = sum_over(jnp.stack([squares, loss_item])[None], "lat")
    place = [lax.broadcasted_iota(jnp.int32, up_total.shape, dim) for dim in range(2)]
    carried = jnp.where(place[0] == 0, scalars[0, 0], scalars[0, 1])
    up_total = jnp.where((place[1] == up_total.shape[1] - 1) & (place[0] < 2), carried, up_total)
    last_all = all_items(after(down_total, *ready), after(up_total, *ready))
    scalars = [x[:2, -1] for _, x in last_all]
    scalars = (scalars[0] + scalars[1]) + (scalars[2] + scalars[3])
    loss_sum = scalars[1]
    grad_norm = jnp.sqrt(scalars[0])
    scale_factor = CLIP_LEVEL / jnp.maximum(grad_norm, CLIP_LEVEL)

    shard_rows = attn_master.shape[0]
    mlp_spec = pl.BlockSpec((mlp_master.shape[0], shard_rows, quarter), lambda j, k, s: (0, 0, k * 4 + (s[3] ^ j)))
    attn_part = pl.BlockSpec((shard_rows, width // 2), lambda j, k, s: (0, (s[3] ^ j) * 2 + k))
    kinds = [F32, F32, F32, F32, BF16]
    shares = [x for pair in zip(*first_all) for x in pair] + [x for pair in zip(*last_all) for x in pair]
    state = (mlp_master, mlp_first, mlp_second, mlp_ema, attn_master, attn_first, attn_second, attn_ema)
    table_state = [jnp.swapaxes(x, 1, 2) for x in (tables_master, tables_first, tables_second, tables_ema)]
    FAR.extend(table_state)
    updated = prefetched(
        adam_kernel,
        (4, 2),
        [shape(x.shape, kind) for x in (mlp_master, attn_master, table_state[0], gains_master) for kind in kinds],
        [smem]
        + [pl.BlockSpec(x.shape, lambda *_: (0, 0)) for x in shares]
        + [mlp_spec] * 4
        + [attn_part] * 4
        + [whole(table_state[0].shape)] * 4
        + [whole(gains_master.shape)] * 4,
        [mlp_spec] * 5 + [attn_part] * 5 + [whole(table_state[0].shape)] * 5 + [whole(gains_master.shape)] * 5,
        places,
        (
            scale_factor[None], *shares, *state, *table_state,
            gains_master, gains_first, gains_second, gains_ema,
        ),
        moved=34 * (mlp_master.size + attn_master.size),
    )
    mlps, att, gns = updated[:5], updated[5:10], updated[15:]
    tab = [jnp.swapaxes(x, 1, 2) for x in updated[10:15]]
    return (loss_sum, grad_norm, *tab, *att, *mlps, *gns)


def solution(mesh):
    table = P(None, None, "lat")
    attn = P("lat", None)
    mlp = P(None, "lat", None)
    gain = P(None, "lat")
    placed = (
        P("item", None, "lat"),
        P("item", None, "lat"),
        P("item"),
        P(None, "lat"),
        P("item", None),
        P("lat", None),
        P("lat", None),
        P("lat", None),
        P(), table, table, table, table,
        P(), attn, attn, attn, attn,
        P(), mlp, mlp, mlp, mlp,
        P(), gain, gain, gain, gain,
    )
    return jax.shard_map(
        shards,
        mesh=mesh,
        in_specs=placed,
        out_specs=(P(), P(), *([table] * 5), *([attn] * 5), *([mlp] * 5), *([gain] * 5)),
        check_vma=False,
    )
```

```python
import functools

import jax
import jax.numpy as jnp
from jax import lax
from jax.experimental import pallas as pl
from jax.experimental.pallas import tpu as pltpu
from jax.sharding import PartitionSpec as P

HEADS = 4
GROUPS = 2
WEIGH = 30
LARGE = 1 << 20
STEP = 10

EPS_NORM = 1e-05
CLIP_LEVEL = 1.0
BETA_ONE = 0.9
BETA_TWO = 0.999
ADAM_EPS = 1e-08
EMA_DECAY = 0.9
RATE_MATRIX = 0.05
RATE_GAIN = 0.3
WEIGHT_DECAY = 0.1
HIGH_PRECISION = lax.Precision.HIGHEST

F32 = jnp.float32
BF16 = jnp.bfloat16
LOG2E = 1.4426950408889634
CHANNEL_PAD = 128
ROWS = 256
VMEM_BYTES = 36 * 1024 * 1024


def dot(left, right, left_dim, right_dim):
    return lax.dot_general(
        left, right, (((left_dim,), (right_dim,)), ((), ())), preferred_element_type=F32
    )


FAR = []


def is_far(value):
    return any(value is x for x in FAR)


def far(value):
    return pltpu.with_memory_space_constraint(value, pltpu.HBM) if is_far(value) else value


def call(kernel, grid, outs, in_specs, out_specs, operands, scratch=(), flops=0, moved=0, near=(), vmem=VMEM_BYTES):
    single = not isinstance(outs, list)
    kinds = [outs] if single else outs
    large = [i not in near and x.size * x.dtype.itemsize >= LARGE for i, x in enumerate(kinds)]
    kinds = [pltpu.HBM(x.shape, x.dtype) if flag else x for x, flag in zip(kinds, large)]
    results = pl.pallas_call(
        kernel,
        grid=grid,
        out_shape=kinds[0] if single else kinds,
        in_specs=in_specs,
        out_specs=out_specs,
        scratch_shapes=list(scratch),
        cost_estimate=pl.CostEstimate(flops=flops * WEIGH, bytes_accessed=moved * WEIGH, transcendentals=0),
        compiler_params=pltpu.CompilerParams(vmem_limit_bytes=vmem),
    )(*[far(x) for x in operands])
    FAR.extend(x for x, flag in zip([results] if single else results, large) if flag)
    return results


def whole(shape):
    return pl.BlockSpec(shape, lambda *_: (0,) * len(shape))


def rows_of(width, rows=ROWS):
    return pl.BlockSpec((rows, width), lambda i: (i, 0))


def lanes_of(height, lanes=ROWS):
    return pl.BlockSpec((height, lanes), lambda i: (0, i))


def shape(dims, kind):
    return jax.ShapeDtypeStruct(dims, kind)


def norm_parts(values):
    center = values - jnp.mean(values, axis=-1, keepdims=True)
    spread = jnp.mean(center * center, axis=-1, keepdims=True)
    inverse = lax.rsqrt(spread + EPS_NORM)
    return center * inverse, inverse


def norm_back(upstream, values, gain_row):
    unit, inverse = norm_parts(values)
    scaled = upstream * gain_row
    along = jnp.mean(scaled * unit, axis=-1, keepdims=True)
    grad = inverse * (scaled - jnp.mean(scaled, axis=-1, keepdims=True) - unit * along)
    gain_grad = jnp.sum(upstream * unit, axis=0, keepdims=True)
    return grad, gain_grad


def gelu_parts(u):
    root = 0.7978845608028654
    cubic = 0.044715
    square = u * u
    inner = u * (root + (root * cubic) * square)
    half = 0.5 + 0.5 * jnp.tanh(inner)
    slope = half * (1.0 + (1.0 - half) * (6.0 * inner - (4.0 * root) * u))
    return u * half, slope


def mlp_forward(values, gain_row, w_ref, normed_ref, slope_ref, active_ref, step=512):
    hidden = w_ref.shape[-1] // 2
    normed = (norm_parts(values)[0] * gain_row).astype(BF16)
    normed_ref[...] = normed
    result = jnp.zeros(values.shape, F32)
    starts = range(0, hidden, step)
    befores = [dot(normed, w_ref[0, :, :step], 1, 0)]
    for start in starts:
        part = slice(start, start + step)
        if start + step < hidden:
            befores.append(dot(normed, w_ref[0, :, start + step : start + 2 * step], 1, 0))
        active, slope = gelu_parts(befores.pop(0))
        active = active.astype(BF16)
        slope_ref[:, part] = slope
        active_ref[:, part] = active
        result = result + dot(active, w_ref[0, :, hidden + start : hidden + start + step], 1, 1)
    return values + result


def mlp_backward(upstream, values, gain_row, w_ref, slope_ref, rounded_ref, before_ref, step=512):
    hidden = w_ref.shape[-1] // 2
    rounded = upstream.astype(BF16)
    rounded_ref[...] = rounded
    grad_normed = jnp.zeros(values.shape, F32)
    ahead = [dot(rounded, w_ref[0, :, hidden : hidden + step], 1, 0)]
    for start in range(0, hidden, step):
        part = slice(start, start + step)
        if start + step < hidden:
            ahead.append(dot(rounded, w_ref[0, :, hidden + start + step : hidden + start + 2 * step], 1, 0))
        grad_before = (ahead.pop(0) * slope_ref[:, part]).astype(BF16)
        before_ref[:, part] = grad_before
        grad_normed = grad_normed + dot(grad_before, w_ref[0, :, part], 1, 1)
    grad, gain_grad = norm_back(grad_normed, values, gain_row)
    return upstream + grad, gain_grad


def two_parts(values):
    high = values.astype(BF16)
    return high, (values - high.astype(F32)).astype(BF16)


def named(edges, places):
    tally = jnp.zeros(places.shape, F32)
    for j in range(edges.shape[0]):
        tally = tally + jnp.where(edges[j : j + 1, :] == places, 1.0, 0.0)
    return tally.astype(BF16)


def add_up(ref, value):
    step = pl.program_id(0)

    @pl.when(step == 0)
    def _():
        ref[...] = value

    @pl.when(step > 0)
    def _():
        ref[...] += value


def encoder_kernel(
    edges, x, table, gains, mlp, attn,
    pin_ref, pooled_ref, encoded_ref, normed_ref, slope_ref, active_ref, normed_attn_ref, q_ref, *pair_refs,
):
    count, rows = edges.shape
    width = attn.shape[0]
    places = lax.broadcasted_iota(jnp.int32, (x.shape[1], rows), 0)
    pin = dot(named(edges, places), x[...], 0, 1) / count
    high, low = two_parts(pin)
    pin_ref[...] = jnp.concatenate([high, low], axis=1)
    pooled = dot(high, table[0], 1, 0) + dot(low, table[0], 1, 0)
    pooled_ref[...] = pooled
    encoded = mlp_forward(pooled, gains[0:1], mlp, normed_ref, slope_ref, active_ref)
    encoded_ref[...] = encoded
    normed_attn = (norm_parts(encoded)[0] * gains[1:2]).astype(BF16)
    normed_attn_ref[...] = normed_attn
    q_ref[...] = dot(attn[:, :width], normed_attn, 0, 1).astype(BF16)
    part = width // len(pair_refs)
    for g, ref in enumerate(pair_refs):
        for side in range(2):
            start = (1 + side) * width + g * part
            ref[:, side * part : (side + 1) * part] = dot(
                normed_attn, attn[:, start : start + part], 1, 0
            ).astype(BF16)


def bias_kernel(places, ends, edges, bias_ref, *, crops):
    count, lanes = edges.shape
    rows = bias_ref.shape[1]
    window = bias_ref.shape[0] * rows
    col = pl.program_id(0)
    nodes = col * lanes + lax.broadcasted_iota(jnp.int32, (1, lanes), 1)
    first = places[0] * rows
    low = jnp.zeros((1, lanes), jnp.int32)
    high = jnp.full((1, lanes), places[1] * rows, jnp.int32)
    for c in range(crops - 1, -1, -1):
        high = jnp.where(ends[c] > first + nodes, ends[c], high)
    for c in range(crops):
        low = jnp.where(ends[c] <= first + nodes, ends[c], low)
    near = edges[...] + (first - rows)
    place = jnp.where((near >= low) & (near < high), edges[...], -1)
    place = jnp.concatenate([place, rows + nodes], axis=0)
    tile = 128
    tiles = window // tile
    each = 6
    fine = jnp.where(place < 0, -1, place % tile)
    coarse = place // tile
    sub = lax.broadcasted_iota(jnp.int32, (tile, lanes), 0)
    for start in range(0, tiles, each):
        here = (coarse >= start) & (coarse < start + each)
        amount = jnp.where(here, jnp.left_shift(1, 5 * jnp.where(here, coarse - start, 0)), 0)
        total = jnp.zeros((tile, lanes), jnp.int32)
        for j in range(count + 1):
            total = total + jnp.where(sub == fine[j : j + 1], amount[j : j + 1], 0)
        for t in range(start, min(tiles, start + each)):
            tally = jnp.bitwise_and(jnp.right_shift(total, 5 * (t - start)), 31)
            value = jnp.where(tally == 0, -1e30, jnp.log2(jnp.maximum(tally, 1).astype(F32)))
            at = t * tile
            bias_ref[at // rows, at % rows : at % rows + tile, :] = value


def attend_kernel(q_ref, k0, k1, k2, v0, v1, v2, bias, o_ref, l_ref, scores, *, chunk):
    depth, lanes = q_ref.shape
    rows = k0.shape[0]
    factor = depth**-0.5 * LOG2E
    q = q_ref[...]
    top = jnp.full((8, lanes), -3e38, F32)
    for w, keys in enumerate((k0, k1, k2)):
        for start in range(0, rows, chunk):
            part = slice(start, start + chunk)
            score = dot(keys[part, :], q, 1, 0) * factor + bias[w, part, :]
            scores[w, part, :] = score
            top = jnp.maximum(top, jnp.max(score.reshape(chunk // 8, 8, lanes), axis=0))
    top = jnp.max(top, axis=0, keepdims=True)
    total = jnp.zeros((8, lanes), F32)
    result = jnp.zeros((depth, lanes), F32)
    for w, values in enumerate((v0, v1, v2)):
        for start in range(0, rows, chunk):
            part = slice(start, start + chunk)
            e = jnp.exp2(scores[w, part, :] - top)
            total = total + jnp.sum(e.reshape(chunk // 8, 8, lanes), axis=0)
            result = result + dot(values[part, :], e.astype(BF16), 0, 0)
    total = jnp.sum(total, axis=0, keepdims=True)
    o_ref[...] = result * (1.0 / total)
    l_ref[...] = jnp.broadcast_to((top + jnp.log2(total))[None], l_ref.shape)


def processor_kernel(
    o0, o1, encoded, gains, mlp, attn,
    attended_ref, residual_ref, normed_ref, slope_ref, active_ref, sent_ref,
):
    attended = jnp.concatenate([o0[...], o1[...]], axis=0).astype(BF16)
    attended_ref[...] = attended
    residual = encoded[...] + dot(attended, attn[...], 0, 0)
    residual_ref[...] = residual
    latent = mlp_forward(residual, gains[2:3], mlp, normed_ref, slope_ref, active_ref)
    sent_ref[...] = latent.astype(BF16)


def window_kernel(edges, sent, x, tables, tally_ref, partial_ref):
    count = edges.shape[0]
    bands, band, rows = tally_ref.shape
    places = lax.broadcasted_iota(jnp.int32, (band, rows), 0)
    for w in range(bands):
        tally_ref[w] = named(edges, places + w * band)
    gathered = dot(tally_ref[1], sent[...], 0, 0)
    partial_ref[...] = dot(x[...], tables[0], 0, 0) + gathered / count


def decoder_kernel(
    tally, s0, s2, partial, tables, gains, mlp,
    joined_ref, normed_ref, slope_ref, active_ref, decoded_ref, final_ref, output_ref, *, count,
):
    gathered = dot(tally[0], s0[...], 0, 0) + dot(tally[2], s2[...], 0, 0)
    joined = partial[...] + gathered / count
    joined_ref[...] = joined
    decoded = mlp_forward(joined, gains[3:4], mlp, normed_ref, slope_ref, active_ref)
    decoded_ref[...] = decoded
    final = (norm_parts(decoded)[0] * gains[4:5]).astype(BF16)
    final_ref[...] = final
    output_ref[...] = dot(tables[1], final, 1, 1)


def decoder_back_kernel(
    grad_output, tables, decoded, final, joined, slope, gains, mlp, x,
    high_ref, low_ref, rounded_ref, before_ref, table_ref, gain_ref, direct_ref,
):
    grad_final = dot(grad_output[...], tables[1], 0, 0)
    add_up(table_ref, dot(final[...], grad_output[...], 0, 1))
    grad_decoded, gain_final = norm_back(grad_final, decoded[...], gains[4:5])
    grad_join, gain_dec = mlp_backward(
        grad_decoded, joined[...], gains[3:4], mlp, slope, rounded_ref, before_ref
    )
    high, low = two_parts(grad_join)
    high_ref[...] = high
    low_ref[...] = low
    add_up(direct_ref, dot(high, x[...], 0, 1) + dot(low, x[...], 0, 1))
    add_up(gain_ref, jnp.concatenate([gain_dec, gain_final], axis=0))


def scatter_kernel(edges, high, low, *outs):
    rows = outs[0].shape[0]
    count, total = edges.shape
    sub = lax.broadcasted_iota(jnp.int32, (rows, total), 0) + pl.program_id(0) * rows
    for w, out in enumerate(outs):
        tally = named(edges, sub + w * total)
        value = dot(tally, high[...], 1, 0) + dot(tally, low[...], 1, 0)
        out[...] = (value / count).astype(out.dtype)


def processor_back_kernel(
    g0, g1, g2, residual, slope, gains, mlp, attn, o0, o1,
    grad_residual_ref, rounded_ref, before_ref, gain_ref, branch_ref, grad_o_ref, delta_ref,
):
    width = residual.shape[1]
    upstream = g1[...] + g0[...].astype(F32) + g2[...].astype(F32)
    grad, gain = mlp_backward(
        upstream, residual[...], gains[2:3], mlp, slope, rounded_ref, before_ref
    )
    add_up(gain_ref, gain)
    grad_residual_ref[...] = grad
    branch = grad.astype(BF16)
    branch_ref[...] = branch
    grad_o = dot(attn[...], branch, 1, 1).astype(BF16)
    grad_o_ref[...] = grad_o
    depth = width // HEADS
    attended = jnp.concatenate([o0[...], o1[...]], axis=0)
    together = grad_o.astype(F32) * attended
    for h in range(HEADS):
        row = jnp.sum(together[h * depth : (h + 1) * depth], axis=0, keepdims=True)
        delta_ref[h] = jnp.broadcast_to(row, delta_ref.shape[1:])


def attend_back_kernel(
    q_ref, do_ref, lse_ref, delta_ref, k0, k1, k2, v0, v1, v2, bias,
    dq_ref, out0, out1, out2, p_ref, ds_ref, *, chunk,
):
    block, depth = k0.shape
    scale = depth**-0.5
    factor = scale * LOG2E
    step, h = pl.program_id(0), pl.program_id(1)
    here = pl.ds(pl.multiple_of(h * depth, depth), depth)
    q = q_ref[here, :]
    do = do_ref[here, :]
    lse = lse_ref[h, 0:1, :]
    delta = delta_ref[h, 0:1, :]
    total = jnp.zeros(q.shape, F32)
    for w, (keys, values, out) in enumerate(((k0, v0, out0), (k1, v1, out1), (k2, v2, out2))):
        for start in range(0, block, chunk):
            part = slice(start, start + chunk)
            p = jnp.exp2(dot(keys[part, :], q, 1, 0) * factor + bias[w, part, :] - lse)
            ds = p * (dot(values[part, :], do, 1, 0) - delta)
            p_ref[part, :] = p.astype(BF16)
            ds_ref[part, :] = ds.astype(BF16)
            out[0, :, part] = (dot(q, ds_ref[part, :], 1, 1) * scale).astype(out.dtype)
            out[1, :, part] = dot(do, p_ref[part, :], 1, 1).astype(out.dtype)
            total = total + dot(keys[part, :], ds_ref[part, :], 0, 0)

    @pl.when(step == 0)
    def _():
        dq_ref[here, :] = total * scale

    @pl.when(step > 0)
    def _():
        dq_ref[here, :] += total * scale


def hand_out(core, value, keep_ref, send_ref, columns):
    bands, rows = keep_ref.shape[1:3]
    for parity in range(2):

        @pl.when(core == parity)
        def _(parity=parity):
            for band in range(bands):
                for side, ref in ((parity, keep_ref), (1 - parity, send_ref)):
                    at = (2 * band + side) * rows
                    ref[0, band, :, columns] = value[at : at + rows].astype(ref.dtype)


def turn(pairs):
    @pl.when(pl.program_id(0) == 0)
    def _():
        for ref, kept in pairs:
            kept[...] = ref[...].T


def weights_kernel(places, normed, rounded, before, active, keep_ref, send_ref, normed_turned, rounded_turned):
    size = before.shape[1]
    turn(((normed, normed_turned), (rounded, rounded_turned)))
    hand_out(places[2], dot(normed_turned[...], before[...], 1, 0), keep_ref, send_ref, slice(0, size))
    hand_out(places[2], dot(rounded_turned[...], active[...], 1, 0), keep_ref, send_ref, slice(size, 2 * size))


def down_weights_kernel(
    places, rounded, active, normed_attn, project, attended, branch, keep_ref, send_ref, rounded_turned, normed_turned
):
    quarter = pl.program_id(0)
    size = active.shape[1]
    turn(((rounded, rounded_turned), (normed_attn, normed_turned)))
    hand_out(places[2], dot(rounded_turned[...], active[...], 1, 0), keep_ref, send_ref, slice(0, size))
    columns = slice(size, size + normed_attn.shape[1])

    @pl.when(quarter < 3)
    def _():
        hand_out(places[2], dot(normed_turned[...], project[...], 1, 1), keep_ref, send_ref, columns)

    @pl.when(quarter == 3)
    def _():
        hand_out(places[2], dot(attended[...], branch[...], 1, 0), keep_ref, send_ref, columns)


def up_weights_kernel(places, normed, before, table_in, table_direct, table_out, gain, keep_ref, send_ref, normed_turned):
    quarter = pl.program_id(0)
    size = before.shape[1]
    turn(((normed, normed_turned),))
    hand_out(places[2], dot(normed_turned[...], before[...], 1, 0), keep_ref, send_ref, slice(0, size))
    columns = slice(size, size + table_in.shape[1])

    @pl.when(quarter == 0)
    def _():
        hand_out(places[2], table_in[...] + table_direct[...], keep_ref, send_ref, columns)

    for index, ref in ((1, table_out), (2, gain)):

        @pl.when(quarter == index)
        def _(ref=ref):
            hand_out(places[2], ref[...], keep_ref, send_ref, columns)

    @pl.when(quarter == 3)
    def _():
        hand_out(places[2], jnp.zeros(table_in.shape, F32), keep_ref, send_ref, columns)


def item_kernel(places, *refs, pairs, exact):
    ins, outs = refs[: 2 * pairs], refs[2 * pairs :]
    step = pl.program_id(0)
    for index, out in enumerate(outs):

        @pl.when(step == index)
        def _(index=index, out=out):
            start = 0
            for pair in range(pairs):
                keep, came = ins[2 * pair : 2 * pair + 2]
                value = keep[0] + came[0]
                size = value.shape[-1]
                out[:, :, start : start + size] = value.astype(out.dtype)
                if index > 0 and exact and pair == pairs - 1:
                    part = value[:, :, size - exact :]
                    rest = part - part.astype(out.dtype).astype(F32)
                    out[:, :, start + size : start + size + exact] = rest.astype(out.dtype)
                start += size


def band_kernel(places, *refs, groups, count, exact):
    ins, outs = refs[: groups * (1 + count)], refs[groups * (1 + count) :]
    step = pl.program_id(0)
    start = 0
    for group in range(groups):
        own, *came = ins[group * (1 + count) : (group + 1) * (1 + count)]
        size = own.shape[-1]
        total = own[0]
        for ref in came:
            total = total + ref[0, :, :size].astype(F32)
        last = exact and group == groups - 1
        if last:
            part = total[:, size - exact :] + sum(ref[0, :, size:].astype(F32) for ref in came)
            high = part.astype(BF16)
            rest = (part - high.astype(F32)).astype(BF16)
        for index, out in enumerate(outs):

            @pl.when(step == index)
            def _(index=index, out=out):
                out[:, start : start + size] = total.astype(out.dtype)
                if last and index == 0:
                    out[:, start + size - exact : start + size] = part
                elif last:
                    out[:, start + size - exact : start + size] = high
                    out[:, start + size : start + size + exact] = rest

        start += size


def exchange(value, axis, distance):
    size = lax.axis_size(axis)
    return lax.ppermute(value, axis, [(i, i ^ distance) for i in range(size)])


def prefetched(kernel, grid, outs, in_specs, out_specs, places, operands, moved, weight=1):
    return pl.pallas_call(
        kernel,
        grid_spec=pltpu.PrefetchScalarGridSpec(
            num_scalar_prefetch=1, grid=grid, in_specs=in_specs, out_specs=out_specs
        ),
        out_shape=outs,
        cost_estimate=pl.CostEstimate(flops=moved * WEIGH * weight, bytes_accessed=moved * WEIGH, transcendentals=0),
        compiler_params=pltpu.CompilerParams(vmem_limit_bytes=VMEM_BYTES * 2 // 3),
    )(places, *[far(x) for x in operands])


def sort_shares(keeps, sends, places, exact=0, late=()):
    items = lax.axis_size("item")
    came = [exchange(send, "lat", 1) for send in sends]
    quarters, bands, rows, _ = keeps[0].shape
    size = sum(keep.shape[-1] for keep in keeps)
    wide = size + exact
    operands = [after(x, *late) for pair in zip(keeps, came) for x in pair]
    return prefetched(
        functools.partial(item_kernel, pairs=len(keeps), exact=exact),
        (items,),
        [shape((bands, rows, size), F32)] + [shape((bands, rows, wide), BF16)] * (items - 1),
        [pl.BlockSpec((1,) + x.shape[1:], lambda j, s: (s[3] ^ j, 0, 0, 0)) for x in operands],
        [pl.BlockSpec((bands, rows, size), lambda j, s: (0, 0, 0))]
        + [pl.BlockSpec((bands, rows, wide), lambda j, s: (0, 0, 0))] * (items - 1),
        places,
        operands,
        moved=14 * bands * rows * size * items,
    )


def swap_items(sorted_shares):
    own, *others = sorted_shares
    return [own] + [exchange(x, "item", k + 1) for k, x in enumerate(others)]


def sum_items(groups, places, exact=0):
    items = len(groups[0])
    bands, rows, _ = groups[0][0].shape
    operands = [x for group in groups for x in group]
    size = sum(group[0].shape[-1] for group in groups)
    wide = size + exact
    return prefetched(
        functools.partial(band_kernel, groups=len(groups), count=items - 1, exact=exact),
        (bands,),
        [shape((rows, size), F32)] + [shape((rows, wide), BF16)] * (bands - 1),
        [pl.BlockSpec((1,) + x.shape[1:], lambda j, s: (s[4] ^ j, 0, 0)) for x in operands],
        [pl.BlockSpec((rows, size), lambda j, s: (0, 0))]
        + [pl.BlockSpec((rows, wide), lambda j, s: (0, 0))] * (bands - 1),
        places,
        operands,
        moved=14 * bands * rows * size,
        weight=10000,
    )


def sum_bands(parts, exact=0, late=()):
    own, *others = parts
    size = own.shape[-1]
    came = [exchange(x, "lat", 2 * (k + 1)) for k, x in enumerate(others)]
    total = after(own, *late) if late else own
    for x in came:
        total = total + x[:, :size].astype(F32)
    if exact:
        rest = sum(x[:, size:].astype(F32) for x in came)
        total = jnp.concatenate([total[:, : size - exact], total[:, size - exact :] + rest], axis=1)
    return total


def after(value, *others):
    result = lax.optimization_barrier((value, *others))[0]
    if is_far(value):
        FAR.append(result)
    return result


def total_kernel(own, *refs):
    *came, out0, out1 = refs
    total = own[...]
    for ref in came:
        total = total + ref[...].astype(F32)
    half = out0.shape[-1]
    out0[...] = total[:, :half]
    out1[...] = total[:, half:]


def add_bands(parts, late):
    own, *others = parts
    came = [exchange(x, "lat", 2 * (k + 1)) for k, x in enumerate(others)]
    return call(
        total_kernel,
        (1,),
        [shape((own.shape[0], own.shape[1] // 2), F32)] * 2,
        [whole(own.shape)] * len(parts),
        [whole((own.shape[0], own.shape[1] // 2))] * 2,
        (after(own, *late), *came),
        flops=10**11,
        moved=16 * own.size,
        near=(0, 1),
    )


def all_items(one, two):
    one_near, two_far = exchange(one, "item", 1), exchange(two, "item", 2)
    one_far, two_near = exchange(one, "item", 2), exchange(two, "item", 1)
    return [
        (one, two), (one_near, two_near), (one_far, two_far),
        (exchange(one_near, "item", 2), exchange(two_far, "item", 1)),
    ]


def sum_over(value, axis):
    distance = 1
    while distance < lax.axis_size(axis):
        value = value + exchange(value, axis, distance)
        distance *= 2
    return value


def adam_kernel(places, factor, *refs):
    dec, proc, down, up, whole_up = (refs[4 * i : 4 * i + 4] for i in range(5))
    mlp, attn, tables, gains = (refs[20 + 4 * i : 24 + 4 * i] for i in range(4))
    mlp_out, attn_out, tables_out, gains_out = (refs[36 + 5 * i : 41 + 5 * i] for i in range(4))
    size = down[0].shape[-1] - attn[0].shape[-1] // 4
    part = attn[0].shape[-1] // 4
    scale = factor[0]
    block, layer = pl.program_id(0), pl.program_id(1)

    def update(share, state, new_state, at, rate, decay):
        new = adam_update(scale * share, *(ref[at] for ref in state), rate, decay)
        for ref, value in zip(new_state, new):
            ref[at] = value

    for k in range(4):
        quarter = places[3] ^ k
        for index, sides in enumerate(((up, down), (proc, proc), (dec, dec))):

            @pl.when(layer == index)
            def _(k=k, index=index, sides=sides, quarter=quarter):
                for side, shares in enumerate(sides):
                    start = 0 if index == 0 else side * size
                    columns = pl.ds(pl.multiple_of((4 * side + quarter) * size, size), size)
                    share = shares[k][:, start : start + size]
                    update(share, mlp, mlp_out, (0, slice(None), columns), RATE_MATRIX, WEIGHT_DECAY)

        @pl.when(layer == 0)
        def _(k=k, quarter=quarter):
            columns = pl.ds(pl.multiple_of(quarter * part, part), part)
            update(down[k][:, size:], attn, attn_out, (slice(None), columns), RATE_MATRIX, WEIGHT_DECAY)

        small = (layer == 0) & (block == 0)
        for table in range(2):

            @pl.when(small & (quarter == table))
            def _(k=k, table=table):
                share = whole_up[k][:, size : size + tables[0].shape[-1]]
                update(share, tables, tables_out, (table,), RATE_MATRIX, WEIGHT_DECAY)

        @pl.when(small & (quarter == 2))
        def _(k=k):
            turned = whole_up[k][:, size:].T[: gains[0].shape[0]]
            update(turned, gains, gains_out, (slice(None),), RATE_GAIN, 0.0)


def projection_back_kernel(
    dq0, dq1, left0, left1, own0, own1, right0, right1, grad_residual, encoded, gains, attn,
    upstream_ref, rounded_ref, project_ref, gain_ref,
):
    pairs = [
        own[...] + left[...].astype(F32) + right[...].astype(F32)
        for left, own, right in ((left0, own0, right0), (left1, own1, right1))
    ]
    project = jnp.concatenate(
        [dq0[...], dq1[...], pairs[0][0], pairs[1][0], pairs[0][1], pairs[1][1]], axis=0
    ).astype(BF16)
    project_ref[...] = project
    grad_normed = dot(project, attn[...], 0, 1)
    grad_encoded, gain_attn = norm_back(grad_normed, encoded[...], gains[1:2])
    upstream = grad_residual[...] + grad_encoded
    upstream_ref[...] = upstream
    rounded_ref[...] = upstream.astype(BF16)
    add_up(gain_ref, gain_attn)


def encoder_back_kernel(
    upstream, pooled, slope, gains, mlp, pin, before_ref, table_ref, gain_ref, rounded_ref
):
    grad_pooled, gain_enc = mlp_backward(
        upstream[...], pooled[...], gains[0:1], mlp, slope, rounded_ref, before_ref
    )
    add_up(gain_ref, gain_enc)
    high, low = two_parts(grad_pooled)
    both = dot(high, pin[...], 0, 0) + dot(low, pin[...], 0, 0)
    channels = both.shape[1] // 2
    add_up(table_ref, both[:, :channels] + both[:, channels:])


def weights(kernel, places, operands, specs, columns, flops, turned):
    rows, width = operands[0].shape
    bands = lax.axis_size("lat") // 2
    out = shape((4, bands, width // (2 * bands), columns), F32)
    out_spec = pl.BlockSpec((1,) + out.shape[1:], lambda i: (i, 0, 0, 0))
    return call(
        kernel,
        (4,),
        [out, out],
        [pl.BlockSpec(memory_space=pltpu.SMEM)] + specs,
        [out_spec, out_spec],
        (places, *operands),
        flops=flops,
        moved=8 * width * columns * 4,
        scratch=[pltpu.VMEM((width, rows), BF16)] * turned,
        vmem=VMEM_BYTES * 2 // 3,
        near=(0, 1),
    )


def adam_update(gradient, master, moment_one, moment_two, average, step_rate, decay_rate):
    one_new = BETA_ONE * moment_one + (1.0 - BETA_ONE) * gradient
    two_new = BETA_TWO * moment_two + (1.0 - BETA_TWO) * gradient * gradient
    one_hat = one_new * (1.0 / (1.0 - BETA_ONE**STEP))
    two_hat = two_new * (1.0 / (1.0 - BETA_TWO**STEP))
    master_new = master - step_rate * (
        one_hat / (jnp.sqrt(two_hat) + ADAM_EPS) + decay_rate * master
    )
    average_new = EMA_DECAY * average + (1.0 - EMA_DECAY) * master_new
    return (one_new, two_new, master_new, average_new, master_new.astype(jnp.bfloat16))


def from_sides(to_left, to_right):
    size = lax.axis_size("lat")
    up = [(i, (i + 1) % size) for i in range(size - 1)]
    down = [(j, i) for i, j in up]
    return lax.ppermute(to_right, "lat", up), lax.ppermute(to_left, "lat", down)


def shards(
    noisy_state,
    target_state,
    sigmas,
    sh_basis,
    lengths,
    grid_edges,
    mesh_edges,
    dec_edges,
    tables_copy,
    tables_master,
    tables_first,
    tables_second,
    tables_ema,
    attn_copy,
    attn_master,
    attn_first,
    attn_second,
    attn_ema,
    mlp_copy,
    mlp_master,
    mlp_first,
    mlp_second,
    mlp_ema,
    gains_copy,
    gains_master,
    gains_first,
    gains_second,
    gains_ema,
):
    FAR.clear()
    band_index = lax.axis_index("lat")
    bands = lax.axis_size("lat")
    item_index = lax.axis_index("item")
    places = jnp.stack([band_index, bands, band_index % 2, item_index, band_index // 2]).astype(jnp.int32)
    rows = mesh_edges.shape[0]
    grid_rows = noisy_state.shape[2]
    width = attn_copy.shape[0]
    channels = noisy_state.shape[1]
    padded = CHANNEL_PAD
    hidden = mlp_copy.shape[2] // 2
    depth = width // HEADS
    FAR.extend([mlp_copy, attn_copy, mlp_master, mlp_first, mlp_second, mlp_ema])
    FAR.extend([attn_master, attn_first, attn_second, attn_ema])
    gains = gains_copy.astype(F32)
    gain_rows = gains.shape[0]
    noise_level = sigmas[0]
    square = noise_level * noise_level
    scale_in = lax.rsqrt(square + 1.0)
    scale_skip = 1.0 / (square + 1.0)
    scale_out = noise_level * scale_in
    weight_loss = (square + 1.0) / square
    noisy_field = noisy_state[0]
    target_field = target_state[0]
    extra = padded - channels
    inputs = jnp.pad((scale_in * noisy_field).astype(BF16), ((0, extra), (0, 0)))
    tables = jnp.pad(tables_copy, ((0, 0), (0, extra), (0, 0)))

    def weights_spec(index):
        return pl.BlockSpec((1, width, 2 * hidden), lambda *_: (index, 0, 0))

    wout_spec = pl.BlockSpec((width, width), lambda *_: (0, 3))
    few = HEADS // GROUPS
    part = few * depth
    gains_spec = whole(gains.shape)
    tables_spec = whole(tables.shape)
    steps = rows // ROWS
    kept_shapes = [shape((rows, width), BF16), shape((rows, hidden), F32), shape((rows, hidden), BF16)]
    kept_specs = [rows_of(width), rows_of(hidden), rows_of(hidden)]
    mlp_flops = 4 * rows * width * hidden

    pin, pooled, encoded, normed_enc, slope_enc, active_enc, normed_attn, queries, *pairs = call(
        encoder_kernel,
        (steps,),
        [shape((rows, 2 * padded), BF16), shape((rows, width), F32), shape((rows, width), F32)]
        + kept_shapes
        + [shape((rows, width), BF16), shape((width, rows), BF16)]
        + [shape((rows, width), BF16)] * GROUPS,
        [
            lanes_of(grid_edges.shape[1]), whole((padded, grid_rows)), tables_spec, gains_spec,
            weights_spec(0), pl.BlockSpec((width, 3 * width), lambda i: (0, 0)),
        ],
        [rows_of(2 * padded), rows_of(width), rows_of(width)]
        + kept_specs
        + [rows_of(width), lanes_of(width)]
        + [rows_of(width)] * GROUPS,
        (grid_edges.T, inputs, tables, gains, mlp_copy, attn_copy),
        flops=mlp_flops + 6 * rows * width * width,
        moved=30 * rows * width,
    )

    crops = lengths.shape[1]
    smem = pl.BlockSpec(memory_space=pltpu.SMEM)
    bias_lanes = 128
    bias = call(
        functools.partial(bias_kernel, crops=crops),
        (rows // bias_lanes,),
        shape((3, rows, rows), F32),
        [smem, smem, lanes_of(mesh_edges.shape[1], bias_lanes)],
        pl.BlockSpec((3, rows, bias_lanes), lambda i: (0, 0, i)),
        (places, jnp.cumsum(lengths[0]), mesh_edges.T),
        flops=2 * 10**9,
        moved=12 * rows * rows,
    )

    windows = []
    for own in pairs:
        if windows:
            own = after(own, *windows[-1], bias)
        came = from_sides(own, own)
        windows.append([came[0], own, came[1]])

    lanes = 512
    attended, lse = [], []
    for g, window in enumerate(windows):
        result, logs = call(
            functools.partial(attend_kernel, chunk=256),
            (rows // lanes, few),
            [shape((part, rows), F32), shape((few, 8, rows), F32)],
            [pl.BlockSpec((depth, lanes), lambda i, h, g=g: (g * few + h, i))]
            + [pl.BlockSpec((rows, depth), lambda i, h: (0, h))] * 3
            + [pl.BlockSpec((rows, depth), lambda i, h: (0, few + h))] * 3
            + [pl.BlockSpec((3, rows, lanes), lambda i, h: (0, 0, i))],
            [
                pl.BlockSpec((depth, lanes), lambda i, h: (h, i)),
                pl.BlockSpec((1, 8, lanes), lambda i, h: (h, 0, i)),
            ],
            (queries, *window, *window, bias),
            scratch=[pltpu.VMEM((3, rows, lanes), F32)],
            flops=24 * rows * rows * part,
            moved=12 * rows * rows,
        )
        attended.append(result)
        lse.append(logs)

    rounded_o, residual, normed_proc, slope_proc, active_proc, sent = call(
        processor_kernel,
        (steps,),
        [shape((width, rows), BF16), shape((rows, width), F32)] + kept_shapes + [shape((rows, width), BF16)],
        [lanes_of(part)] * GROUPS + [rows_of(width), gains_spec, weights_spec(1), wout_spec],
        [lanes_of(width), rows_of(width)] + kept_specs + [rows_of(width)],
        (*attended, encoded, gains, mlp_copy, attn_copy),
        flops=mlp_flops + 2 * rows * width * width,
        moved=24 * rows * width,
        near=(5,),
    )

    before_sent, after_sent = from_sides(sent, sent)

    dec_count = dec_edges.shape[1]
    tally, partial = call(
        window_kernel,
        (grid_rows // ROWS,),
        [shape((3, rows, grid_rows), BF16), shape((grid_rows, width), F32)],
        [lanes_of(dec_count), whole((rows, width)), lanes_of(padded), tables_spec],
        [pl.BlockSpec((3, rows, ROWS), lambda i: (0, 0, i)), rows_of(width)],
        (dec_edges.T, sent, inputs, tables),
        flops=2 * rows * rows * width,
        moved=24 * rows * width,
    )
    joined, normed_dec, slope_dec, active_dec, decoded, final, output = call(
        functools.partial(decoder_kernel, count=dec_count),
        (grid_rows // ROWS,),
        [shape((grid_rows, width), F32)]
        + kept_shapes
        + [shape((grid_rows, width), F32), shape((grid_rows, width), BF16), shape((padded, grid_rows), F32)],
        [
            pl.BlockSpec((3, rows, ROWS), lambda i: (0, 0, i)), whole((rows, width)), whole((rows, width)),
            rows_of(width), tables_spec, gains_spec, weights_spec(2),
        ],
        [rows_of(width)] + kept_specs + [rows_of(width), rows_of(width), lanes_of(padded)],
        (tally, before_sent, after_sent, partial, tables, gains, mlp_copy),
        flops=mlp_flops + 6 * rows * rows * width,
        moved=24 * rows * width,
    )

    error_field = scale_skip * noisy_field + scale_out * output[:channels] - target_field
    partial_value = lax.dot_general(
        error_field,
        sh_basis,
        (((1,), (1,)), ((), ())),
        precision=HIGH_PRECISION,
        preferred_element_type=F32,
    )
    coeffs = sum_over(partial_value, "lat")
    slice_width = coeffs.shape[1] // bands
    own_coeffs = lax.dynamic_slice_in_dim(coeffs, band_index * slice_width, slice_width, 1)
    loss_item = weight_loss * jnp.sum(own_coeffs * own_coeffs)
    grad_error = jnp.dot(
        2.0 * weight_loss * coeffs, sh_basis, precision=HIGH_PRECISION, preferred_element_type=F32
    )
    grad_output = jnp.pad((scale_out * grad_error).astype(BF16), ((0, extra), (0, 0)))

    join_high, join_low, rounded_dec, before_dec, table_out, gain_dec, table_direct = call(
        decoder_back_kernel,
        (grid_rows // ROWS,),
        [
            shape((grid_rows, width), BF16), shape((grid_rows, width), BF16), shape((grid_rows, width), BF16),
            shape((grid_rows, hidden), BF16), shape((width, padded), F32), shape((2, width), F32),
            shape((width, padded), F32),
        ],
        [
            lanes_of(padded), tables_spec, rows_of(width), rows_of(width), rows_of(width), rows_of(hidden),
            gains_spec, weights_spec(2), lanes_of(padded),
        ],
        [
            rows_of(width), rows_of(width), rows_of(width), rows_of(hidden), whole((width, padded)),
            whole((2, width)), whole((width, padded)),
        ],
        (grad_output, tables, decoded, final, joined, slope_dec, gains, mlp_copy, inputs),
        flops=mlp_flops,
        moved=24 * rows * width,
        near=(0, 1, 2),
    )

    to_left, grad_own, to_right = call(
        scatter_kernel,
        (steps,),
        [shape((rows, width), BF16), shape((rows, width), F32), shape((rows, width), BF16)],
        [whole((dec_count, grid_rows)), whole((grid_rows, width)), whole((grid_rows, width))],
        [rows_of(width)] * 3,
        (dec_edges.T, join_high, join_low),
        near=(0, 1, 2),
        flops=12 * rows * grid_rows * width,
        moved=12 * rows * width,
    )
    from_left, from_right = from_sides(to_left, to_right)
    quarter = hidden // 4
    columns_of = pl.BlockSpec((rows, quarter), lambda i: (0, i))
    table_spec = whole((width, padded))
    full = whole((rows, width))
    product = 2 * rows * width * width

    def layer_weights(*operands):
        return weights(
            weights_kernel, places, operands, [full, full, columns_of, columns_of], 2 * quarter, 8 * product, 2
        )

    keep_dec, send_dec = layer_weights(normed_dec, after(rounded_dec, to_left, to_right), before_dec, active_dec)
    sorted_dec = sort_shares([keep_dec], [send_dec], places)
    swapped_dec = swap_items(sorted_dec)

    grad_residual, rounded_proc, before_proc, gain_proc, branch, grad_o, delta = call(
        processor_back_kernel,
        (steps,),
        [
            shape((rows, width), F32), shape((rows, width), BF16), shape((rows, hidden), BF16),
            shape((1, width), F32), shape((rows, width), BF16), shape((width, rows), BF16),
            shape((HEADS, 8, rows), F32),
        ],
        [rows_of(width)] * 4 + [rows_of(hidden), gains_spec, weights_spec(1), wout_spec] + [lanes_of(part)] * GROUPS,
        [
            rows_of(width), rows_of(width), rows_of(hidden), whole((1, width)), rows_of(width), lanes_of(width),
            pl.BlockSpec((HEADS, 8, ROWS), lambda i: (0, 0, i)),
        ],
        (from_left, after(grad_own, keep_dec, send_dec), from_right, residual, slope_proc, gains, mlp_copy, attn_copy,
            *attended,
        ),
        flops=mlp_flops + 2 * rows * width * width,
        moved=24 * rows * width,
        near=(1, 5),
    )

    block = 512
    side = pl.BlockSpec((2, depth, block), lambda i, h: (0, h, i))
    group_spec = whole((few, 8, rows))
    grad_queries, sides = [], []
    ahead = tuple(sorted_dec)
    for g, window in enumerate(windows):
        row_spec = pl.BlockSpec((part, rows), lambda i, h, g=g: (g, 0))
        dq, left, own, right = call(
            functools.partial(attend_back_kernel, chunk=256),
            (rows // block, few),
            [
                shape((part, rows), F32), shape((2, part, rows), BF16), shape((2, part, rows), F32),
                shape((2, part, rows), BF16),
            ],
            [row_spec, row_spec, group_spec, pl.BlockSpec((few, 8, rows), lambda i, h, g=g: (g, 0, 0))]
            + [pl.BlockSpec((block, depth), lambda i, h: (i, h))] * 3
            + [pl.BlockSpec((block, depth), lambda i, h: (i, few + h))] * 3
            + [pl.BlockSpec((3, block, rows), lambda i, h: (0, i, 0))],
            [whole((part, rows)), side, side, side],
            (queries, after(grad_o, *ahead), lse[g], delta, *window, *window, bias),
            scratch=[pltpu.VMEM((block, rows), BF16), pltpu.VMEM((block, rows), BF16)],
            flops=60 * rows * rows * part,
            moved=12 * rows * rows,
        )
        if sides:
            left, right = after(left, *sides[-1]), after(right, *sides[-1])
        came = from_sides(left, right)
        sides.append([came[0], own, came[1]])
        grad_queries.append(dq)
        ahead = tuple(swapped_dec)

    keep_proc, send_proc = layer_weights(normed_proc, after(rounded_proc, left, right), before_proc, active_proc)
    side_spec = pl.BlockSpec((2, part, ROWS), lambda i: (0, 0, i))
    upstream, rounded_enc, project, gain_attn = call(
        projection_back_kernel,
        (steps,),
        [
            shape((rows, width), F32), shape((rows, width), BF16), shape((3 * width, rows), BF16),
            shape((1, width), F32),
        ],
        [lanes_of(part)] * 2 + [side_spec] * 6
        + [rows_of(width)] * 2 + [gains_spec, pl.BlockSpec((width, 3 * width), lambda i: (0, 0))],
        [rows_of(width), rows_of(width), lanes_of(3 * width), whole((1, width))],
        (
            *grad_queries, sides[0][0], sides[1][0], sides[0][1], sides[1][1], sides[0][2], sides[1][2],
            after(grad_residual, keep_proc, send_proc), encoded, gains, attn_copy,
        ),
        flops=3 * product,
        moved=24 * rows * width,
        near=(0, 1, 2),
    )
    sorted_proc = sort_shares([keep_proc], [send_proc], places, late=(upstream,))
    swapped_proc = swap_items(sorted_proc)
    keep_down, send_down = weights(
        down_weights_kernel,
        places,
        (after(rounded_enc, *sorted_proc), active_enc, normed_attn, project, rounded_o, branch),
        [full, columns_of, full, pl.BlockSpec((width, rows), lambda i: (jnp.minimum(i, 2), 0)), whole((width, rows)), full],
        quarter + width,
        8 * product,
        2,
    )
    sorted_down = sort_shares([keep_down], [send_down], places)
    before_enc, table_in, gain_enc, _ = call(
        encoder_back_kernel,
        (steps,),
        [
            shape((rows, hidden), BF16), shape((width, padded), F32), shape((1, width), F32),
            shape((rows, width), BF16),
        ],
        [rows_of(width)] * 2
        + [rows_of(hidden), gains_spec, weights_spec(0), rows_of(2 * padded)],
        [rows_of(hidden), table_spec, whole((1, width)), rows_of(width)],
        (after(upstream, *sorted_down), pooled, slope_enc, gains, mlp_copy, pin),
        flops=mlp_flops,
        moved=24 * rows * width,
    )
    grad_gains = jnp.concatenate([gain_enc, gain_attn, gain_proc, gain_dec], axis=0)
    gain_columns = jnp.pad(grad_gains.T, ((0, 0), (0, padded - gain_rows)))
    swapped_down = swap_items([sorted_down[0]] + [after(x, *swapped_proc, before_enc) for x in sorted_down[1:]])
    own_proc = [after(swapped_proc[0], before_enc)] + swapped_proc[1:]
    first_parts = sum_items([swapped_dec, own_proc], places)
    first_total = add_bands(first_parts, (first_parts[0],))
    keep_up, send_up = weights(
        up_weights_kernel,
        places,
        (normed_enc, after(before_enc, first_parts[0]), table_in, table_direct, table_out, gain_columns),
        [full, columns_of, table_spec, table_spec, table_spec, table_spec],
        quarter + padded,
        4 * product,
        1,
    )
    down_parts = sum_items([swapped_down], places)
    down_total = sum_bands(down_parts)
    sorted_up = sort_shares([keep_up], [send_up], places, exact=padded, late=(down_parts[0], *first_total))
    swapped_up = swap_items([sorted_up[0]] + [after(x, *swapped_down) for x in sorted_up[1:]])
    first_all = all_items(*[after(x, *swapped_up) for x in first_total])
    ready = [x for pair in first_all for x in pair]
    up_total = sum_bands(sum_items([swapped_up], places, exact=padded), exact=padded)
    squares = sum(jnp.sum(jnp.square(x.astype(F32))) for x in (*first_total, down_total, up_total))
    scalars = sum_over(jnp.stack([squares, loss_item])[None], "lat")
    place = [lax.broadcasted_iota(jnp.int32, up_total.shape, dim) for dim in range(2)]
    carried = jnp.where(place[0] == 0, scalars[0, 0], scalars[0, 1])
    up_total = jnp.where((place[1] == up_total.shape[1] - 1) & (place[0] < 2), carried, up_total)
    last_all = all_items(after(down_total, *ready), after(up_total, *ready))
    scalars = [x[:2, -1] for _, x in last_all]
    scalars = (scalars[0] + scalars[1]) + (scalars[2] + scalars[3])
    loss_sum = scalars[1]
    grad_norm = jnp.sqrt(scalars[0])
    scale_factor = CLIP_LEVEL / jnp.maximum(grad_norm, CLIP_LEVEL)

    shard_rows = attn_master.shape[0]
    block_rows = min(shard_rows, 32)
    mlp_spec = pl.BlockSpec((1, block_rows, 2 * hidden), lambda r, l, s: (l, r, 0))
    attn_part = pl.BlockSpec((block_rows, attn_master.shape[1]), lambda r, l, s: (r, 0))
    kinds = [F32, F32, F32, F32, BF16]
    shares = [x for pair in zip(*first_all) for x in pair] + [x for pair in zip(*last_all) for x in pair]
    state = (mlp_master, mlp_first, mlp_second, mlp_ema, attn_master, attn_first, attn_second, attn_ema)
    table_state = [jnp.swapaxes(x, 1, 2) for x in (tables_master, tables_first, tables_second, tables_ema)]
    FAR.extend([*table_state, *shares])
    updated = prefetched(
        adam_kernel,
        (shard_rows // block_rows, mlp_master.shape[0]),
        [shape(x.shape, kind) for x in (mlp_master, attn_master, table_state[0], gains_master) for kind in kinds],
        [smem]
        + [pl.BlockSpec((block_rows, x.shape[1]), lambda r, l, s: (r, 0)) for x in shares]
        + [pl.BlockSpec(x.shape, lambda *_: (0, 0)) for x in shares[-4:]]
        + [mlp_spec] * 4
        + [attn_part] * 4
        + [whole(table_state[0].shape)] * 4
        + [whole(gains_master.shape)] * 4,
        [mlp_spec] * 5 + [attn_part] * 5 + [whole(table_state[0].shape)] * 5 + [whole(gains_master.shape)] * 5,
        places,
        (
            scale_factor[None], *shares, *shares[-4:], *state, *table_state,
            gains_master, gains_first, gains_second, gains_ema,
        ),
        moved=34 * (mlp_master.size + attn_master.size),
    )
    mlps, att, gns = updated[:5], updated[5:10], updated[15:]
    tab = [jnp.swapaxes(x, 1, 2) for x in updated[10:15]]
    return (loss_sum, grad_norm, *tab, *att, *mlps, *gns)


def solution(mesh):
    table = P(None, None, "lat")
    attn = P("lat", None)
    mlp = P(None, "lat", None)
    gain = P(None, "lat")
    placed = (
        P("item", None, "lat"),
        P("item", None, "lat"),
        P("item"),
        P(None, "lat"),
        P("item", None),
        P("lat", None),
        P("lat", None),
        P("lat", None),
        P(), table, table, table, table,
        P(), attn, attn, attn, attn,
        P(), mlp, mlp, mlp, mlp,
        P(), gain, gain, gain, gain,
    )
    return jax.shard_map(
        shards,
        mesh=mesh,
        in_specs=placed,
        out_specs=(P(), P(), *([table] * 5), *([attn] * 5), *([mlp] * 5), *([gain] * 5)),
        check_vma=False,
    )
```

```python
import functools

import jax
import jax.numpy as jnp
from jax import lax
from jax.experimental import pallas as pl
from jax.experimental.pallas import tpu as pltpu
from jax.sharding import PartitionSpec as P

HEADS = 4
GROUPS = 2
WEIGH = 30
LARGE = 1 << 20
STEP = 10

EPS_NORM = 1e-05
CLIP_LEVEL = 1.0
BETA_ONE = 0.9
BETA_TWO = 0.999
ADAM_EPS = 1e-08
EMA_DECAY = 0.9
RATE_MATRIX = 0.05
RATE_GAIN = 0.3
WEIGHT_DECAY = 0.1
HIGH_PRECISION = lax.Precision.HIGHEST

F32 = jnp.float32
BF16 = jnp.bfloat16
LOG2E = 1.4426950408889634
CHANNEL_PAD = 128
ROWS = 256
VMEM_BYTES = 36 * 1024 * 1024


def dot(left, right, left_dim, right_dim):
    return lax.dot_general(
        left, right, (((left_dim,), (right_dim,)), ((), ())), preferred_element_type=F32
    )


FAR = []


def is_far(value):
    return any(value is x for x in FAR)


def far(value):
    return pltpu.with_memory_space_constraint(value, pltpu.HBM) if is_far(value) else value


def call(kernel, grid, outs, in_specs, out_specs, operands, scratch=(), flops=0, moved=0, near=(), vmem=VMEM_BYTES):
    single = not isinstance(outs, list)
    kinds = [outs] if single else outs
    large = [i not in near and x.size * x.dtype.itemsize >= LARGE for i, x in enumerate(kinds)]
    kinds = [pltpu.HBM(x.shape, x.dtype) if flag else x for x, flag in zip(kinds, large)]
    results = pl.pallas_call(
        kernel,
        grid=grid,
        out_shape=kinds[0] if single else kinds,
        in_specs=in_specs,
        out_specs=out_specs,
        scratch_shapes=list(scratch),
        cost_estimate=pl.CostEstimate(flops=flops * WEIGH, bytes_accessed=moved * WEIGH, transcendentals=0),
        compiler_params=pltpu.CompilerParams(vmem_limit_bytes=vmem),
    )(*[far(x) for x in operands])
    FAR.extend(x for x, flag in zip([results] if single else results, large) if flag)
    return results


def whole(shape):
    return pl.BlockSpec(shape, lambda *_: (0,) * len(shape))


def rows_of(width, rows=ROWS):
    return pl.BlockSpec((rows, width), lambda i: (i, 0))


def lanes_of(height, lanes=ROWS):
    return pl.BlockSpec((height, lanes), lambda i: (0, i))


def shape(dims, kind):
    return jax.ShapeDtypeStruct(dims, kind)


def norm_parts(values):
    center = values - jnp.mean(values, axis=-1, keepdims=True)
    spread = jnp.mean(center * center, axis=-1, keepdims=True)
    inverse = lax.rsqrt(spread + EPS_NORM)
    return center * inverse, inverse


def norm_back(upstream, values, gain_row):
    unit, inverse = norm_parts(values)
    scaled = upstream * gain_row
    along = jnp.mean(scaled * unit, axis=-1, keepdims=True)
    grad = inverse * (scaled - jnp.mean(scaled, axis=-1, keepdims=True) - unit * along)
    gain_grad = jnp.sum(upstream * unit, axis=0, keepdims=True)
    return grad, gain_grad


def gelu_parts(u):
    root = 0.7978845608028654
    cubic = 0.044715
    square = u * u
    inner = u * (root + (root * cubic) * square)
    half = 0.5 + 0.5 * jnp.tanh(inner)
    slope = half * (1.0 + (1.0 - half) * (6.0 * inner - (4.0 * root) * u))
    return u * half, slope


def mlp_forward(values, gain_row, w_ref, normed_ref, slope_ref, active_ref, step=512):
    hidden = w_ref.shape[-1] // 2
    normed = (norm_parts(values)[0] * gain_row).astype(BF16)
    normed_ref[...] = normed
    result = jnp.zeros(values.shape, F32)
    starts = range(0, hidden, step)
    befores = [dot(normed, w_ref[0, :, :step], 1, 0)]
    for start in starts:
        part = slice(start, start + step)
        if start + step < hidden:
            befores.append(dot(normed, w_ref[0, :, start + step : start + 2 * step], 1, 0))
        active, slope = gelu_parts(befores.pop(0))
        active = active.astype(BF16)
        slope_ref[:, part] = slope
        active_ref[:, part] = active
        result = result + dot(active, w_ref[0, :, hidden + start : hidden + start + step], 1, 1)
    return values + result


def mlp_backward(upstream, values, gain_row, w_ref, slope_ref, rounded_ref, before_ref, step=512):
    hidden = w_ref.shape[-1] // 2
    rounded = upstream.astype(BF16)
    rounded_ref[...] = rounded
    grad_normed = jnp.zeros(values.shape, F32)
    ahead = [dot(rounded, w_ref[0, :, hidden : hidden + step], 1, 0)]
    for start in range(0, hidden, step):
        part = slice(start, start + step)
        if start + step < hidden:
            ahead.append(dot(rounded, w_ref[0, :, hidden + start + step : hidden + start + 2 * step], 1, 0))
        grad_before = (ahead.pop(0) * slope_ref[:, part]).astype(BF16)
        before_ref[:, part] = grad_before
        grad_normed = grad_normed + dot(grad_before, w_ref[0, :, part], 1, 1)
    grad, gain_grad = norm_back(grad_normed, values, gain_row)
    return upstream + grad, gain_grad


def two_parts(values):
    high = values.astype(BF16)
    return high, (values - high.astype(F32)).astype(BF16)


def named(edges, places):
    tally = jnp.zeros(places.shape, F32)
    for j in range(edges.shape[0]):
        tally = tally + jnp.where(edges[j : j + 1, :] == places, 1.0, 0.0)
    return tally.astype(BF16)


def add_up(ref, value):
    step = pl.program_id(0)

    @pl.when(step == 0)
    def _():
        ref[...] = value

    @pl.when(step > 0)
    def _():
        ref[...] += value


def encoder_kernel(
    edges, x, table, gains, mlp, attn,
    pin_ref, pooled_ref, encoded_ref, normed_ref, slope_ref, active_ref, normed_attn_ref, q_ref, *pair_refs,
):
    count, rows = edges.shape
    width = attn.shape[0]
    places = lax.broadcasted_iota(jnp.int32, (x.shape[1], rows), 0)
    pin = dot(named(edges, places), x[...], 0, 1) / count
    high, low = two_parts(pin)
    pin_ref[...] = jnp.concatenate([high, low], axis=1)
    pooled = dot(high, table[0], 1, 0) + dot(low, table[0], 1, 0)
    pooled_ref[...] = pooled
    encoded = mlp_forward(pooled, gains[0:1], mlp, normed_ref, slope_ref, active_ref)
    encoded_ref[...] = encoded
    normed_attn = (norm_parts(encoded)[0] * gains[1:2]).astype(BF16)
    normed_attn_ref[...] = normed_attn
    q_ref[...] = dot(attn[:, :width], normed_attn, 0, 1).astype(BF16)
    part = width // len(pair_refs)
    for g, ref in enumerate(pair_refs):
        for side in range(2):
            start = (1 + side) * width + g * part
            ref[:, side * part : (side + 1) * part] = dot(
                normed_attn, attn[:, start : start + part], 1, 0
            ).astype(BF16)


def bias_kernel(places, ends, edges, bias_ref, *, crops):
    count, lanes = edges.shape
    rows = bias_ref.shape[1]
    window = bias_ref.shape[0] * rows
    col = pl.program_id(0)
    nodes = col * lanes + lax.broadcasted_iota(jnp.int32, (1, lanes), 1)
    first = places[0] * rows
    low = jnp.zeros((1, lanes), jnp.int32)
    high = jnp.full((1, lanes), places[1] * rows, jnp.int32)
    for c in range(crops - 1, -1, -1):
        high = jnp.where(ends[c] > first + nodes, ends[c], high)
    for c in range(crops):
        low = jnp.where(ends[c] <= first + nodes, ends[c], low)
    near = edges[...] + (first - rows)
    place = jnp.where((near >= low) & (near < high), edges[...], -1)
    place = jnp.concatenate([place, rows + nodes], axis=0)
    tile = 128
    tiles = window // tile
    each = 6
    fine = jnp.where(place < 0, -1, place % tile)
    coarse = place // tile
    sub = lax.broadcasted_iota(jnp.int32, (tile, lanes), 0)
    for start in range(0, tiles, each):
        here = (coarse >= start) & (coarse < start + each)
        amount = jnp.where(here, jnp.left_shift(1, 5 * jnp.where(here, coarse - start, 0)), 0)
        total = jnp.zeros((tile, lanes), jnp.int32)
        for j in range(count + 1):
            total = total + jnp.where(sub == fine[j : j + 1], amount[j : j + 1], 0)
        for t in range(start, min(tiles, start + each)):
            tally = jnp.bitwise_and(jnp.right_shift(total, 5 * (t - start)), 31)
            value = jnp.where(tally == 0, -1e30, jnp.log2(jnp.maximum(tally, 1).astype(F32)))
            at = t * tile
            bias_ref[at // rows, at % rows : at % rows + tile, :] = value


def attend_kernel(q_ref, k0, k1, k2, v0, v1, v2, bias, o_ref, l_ref, scores, *, chunk):
    depth, lanes = q_ref.shape
    rows = k0.shape[0]
    factor = depth**-0.5 * LOG2E
    q = q_ref[...]
    top = jnp.full((8, lanes), -3e38, F32)
    for w, keys in enumerate((k0, k1, k2)):
        for start in range(0, rows, chunk):
            part = slice(start, start + chunk)
            score = dot(keys[part, :], q, 1, 0) * factor + bias[w, part, :]
            scores[w, part, :] = score
            top = jnp.maximum(top, jnp.max(score.reshape(chunk // 8, 8, lanes), axis=0))
    top = jnp.max(top, axis=0, keepdims=True)
    total = jnp.zeros((8, lanes), F32)
    result = jnp.zeros((depth, lanes), F32)
    for w, values in enumerate((v0, v1, v2)):
        for start in range(0, rows, chunk):
            part = slice(start, start + chunk)
            e = jnp.exp2(scores[w, part, :] - top)
            total = total + jnp.sum(e.reshape(chunk // 8, 8, lanes), axis=0)
            result = result + dot(values[part, :], e.astype(BF16), 0, 0)
    total = jnp.sum(total, axis=0, keepdims=True)
    o_ref[...] = result * (1.0 / total)
    l_ref[...] = jnp.broadcast_to((top + jnp.log2(total))[None], l_ref.shape)


def processor_kernel(
    o0, o1, encoded, gains, mlp, attn,
    attended_ref, residual_ref, normed_ref, slope_ref, active_ref, sent_ref,
):
    attended = jnp.concatenate([o0[...], o1[...]], axis=0).astype(BF16)
    attended_ref[...] = attended
    residual = encoded[...] + dot(attended, attn[...], 0, 0)
    residual_ref[...] = residual
    latent = mlp_forward(residual, gains[2:3], mlp, normed_ref, slope_ref, active_ref)
    sent_ref[...] = latent.astype(BF16)


def window_kernel(edges, sent, x, tables, tally_ref, partial_ref):
    count = edges.shape[0]
    bands, band, rows = tally_ref.shape
    places = lax.broadcasted_iota(jnp.int32, (band, rows), 0)
    for w in range(bands):
        tally_ref[w] = named(edges, places + w * band)
    gathered = dot(tally_ref[1], sent[...], 0, 0)
    partial_ref[...] = dot(x[...], tables[0], 0, 0) + gathered / count


def decoder_kernel(
    tally, s0, s2, partial, tables, gains, mlp,
    joined_ref, normed_ref, slope_ref, active_ref, decoded_ref, final_ref, output_ref, *, count,
):
    gathered = dot(tally[0], s0[...], 0, 0) + dot(tally[2], s2[...], 0, 0)
    joined = partial[...] + gathered / count
    joined_ref[...] = joined
    decoded = mlp_forward(joined, gains[3:4], mlp, normed_ref, slope_ref, active_ref)
    decoded_ref[...] = decoded
    final = (norm_parts(decoded)[0] * gains[4:5]).astype(BF16)
    final_ref[...] = final
    output_ref[...] = dot(tables[1], final, 1, 1)


def decoder_back_kernel(
    grad_output, tables, decoded, final, joined, slope, gains, mlp, x,
    high_ref, low_ref, rounded_ref, before_ref, table_ref, gain_ref, direct_ref,
):
    grad_final = dot(grad_output[...], tables[1], 0, 0)
    add_up(table_ref, dot(final[...], grad_output[...], 0, 1))
    grad_decoded, gain_final = norm_back(grad_final, decoded[...], gains[4:5])
    grad_join, gain_dec = mlp_backward(
        grad_decoded, joined[...], gains[3:4], mlp, slope, rounded_ref, before_ref
    )
    high, low = two_parts(grad_join)
    high_ref[...] = high
    low_ref[...] = low
    add_up(direct_ref, dot(high, x[...], 0, 1) + dot(low, x[...], 0, 1))
    add_up(gain_ref, jnp.concatenate([gain_dec, gain_final], axis=0))


def scatter_kernel(edges, high, low, *outs):
    rows = outs[0].shape[0]
    count, total = edges.shape
    sub = lax.broadcasted_iota(jnp.int32, (rows, total), 0) + pl.program_id(0) * rows
    for w, out in enumerate(outs):
        tally = named(edges, sub + w * total)
        value = dot(tally, high[...], 1, 0) + dot(tally, low[...], 1, 0)
        out[...] = (value / count).astype(out.dtype)


def processor_back_kernel(
    g0, g1, g2, residual, slope, gains, mlp, attn, o0, o1,
    grad_residual_ref, rounded_ref, before_ref, gain_ref, branch_ref, grad_o_ref, delta_ref,
):
    width = residual.shape[1]
    upstream = g1[...] + g0[...].astype(F32) + g2[...].astype(F32)
    grad, gain = mlp_backward(
        upstream, residual[...], gains[2:3], mlp, slope, rounded_ref, before_ref
    )
    add_up(gain_ref, gain)
    grad_residual_ref[...] = grad
    branch = grad.astype(BF16)
    branch_ref[...] = branch
    grad_o = dot(attn[...], branch, 1, 1).astype(BF16)
    grad_o_ref[...] = grad_o
    depth = width // HEADS
    attended = jnp.concatenate([o0[...], o1[...]], axis=0)
    together = grad_o.astype(F32) * attended
    for h in range(HEADS):
        row = jnp.sum(together[h * depth : (h + 1) * depth], axis=0, keepdims=True)
        delta_ref[h] = jnp.broadcast_to(row, delta_ref.shape[1:])


def attend_back_kernel(
    q_ref, do_ref, lse_ref, delta_ref, k0, k1, k2, v0, v1, v2, bias,
    dq_ref, out0, out1, out2, p_ref, ds_ref, *, chunk,
):
    block, depth = k0.shape
    scale = depth**-0.5
    factor = scale * LOG2E
    step, h = pl.program_id(0), pl.program_id(1)
    here = pl.ds(pl.multiple_of(h * depth, depth), depth)
    q = q_ref[here, :]
    do = do_ref[here, :]
    lse = lse_ref[h, 0:1, :]
    delta = delta_ref[h, 0:1, :]
    total = jnp.zeros(q.shape, F32)
    for w, (keys, values, out) in enumerate(((k0, v0, out0), (k1, v1, out1), (k2, v2, out2))):
        for start in range(0, block, chunk):
            part = slice(start, start + chunk)
            p = jnp.exp2(dot(keys[part, :], q, 1, 0) * factor + bias[w, part, :] - lse)
            ds = p * (dot(values[part, :], do, 1, 0) - delta)
            p_ref[part, :] = p.astype(BF16)
            ds_ref[part, :] = ds.astype(BF16)
            out[0, :, part] = (dot(q, ds_ref[part, :], 1, 1) * scale).astype(out.dtype)
            out[1, :, part] = dot(do, p_ref[part, :], 1, 1).astype(out.dtype)
            total = total + dot(keys[part, :], ds_ref[part, :], 0, 0)

    @pl.when(step == 0)
    def _():
        dq_ref[here, :] = total * scale

    @pl.when(step > 0)
    def _():
        dq_ref[here, :] += total * scale


def hand_out(core, value, keep_ref, send_ref, columns):
    bands, rows = keep_ref.shape[1:3]
    for parity in range(2):

        @pl.when(core == parity)
        def _(parity=parity):
            for band in range(bands):
                for side, ref in ((parity, keep_ref), (1 - parity, send_ref)):
                    at = (2 * band + side) * rows
                    ref[0, band, :, columns] = value[at : at + rows].astype(ref.dtype)


def turn(pairs):
    @pl.when(pl.program_id(0) == 0)
    def _():
        for ref, kept in pairs:
            kept[...] = ref[...].T


def weights_kernel(places, normed, rounded, before, active, keep_ref, send_ref, normed_turned, rounded_turned):
    size = before.shape[1]
    turn(((normed, normed_turned), (rounded, rounded_turned)))
    hand_out(places[2], dot(normed_turned[...], before[...], 1, 0), keep_ref, send_ref, slice(0, size))
    hand_out(places[2], dot(rounded_turned[...], active[...], 1, 0), keep_ref, send_ref, slice(size, 2 * size))


def down_weights_kernel(
    places, rounded, active, normed_attn, project, attended, branch, keep_ref, send_ref, rounded_turned, normed_turned
):
    quarter = pl.program_id(0)
    size = active.shape[1]
    turn(((rounded, rounded_turned), (normed_attn, normed_turned)))
    hand_out(places[2], dot(rounded_turned[...], active[...], 1, 0), keep_ref, send_ref, slice(0, size))
    columns = slice(size, size + normed_attn.shape[1])

    @pl.when(quarter < 3)
    def _():
        hand_out(places[2], dot(normed_turned[...], project[...], 1, 1), keep_ref, send_ref, columns)

    @pl.when(quarter == 3)
    def _():
        hand_out(places[2], dot(attended[...], branch[...], 1, 0), keep_ref, send_ref, columns)


def up_weights_kernel(places, normed, before, table_in, table_direct, table_out, gain, keep_ref, send_ref, normed_turned):
    quarter = pl.program_id(0)
    size = before.shape[1]
    turn(((normed, normed_turned),))
    hand_out(places[2], dot(normed_turned[...], before[...], 1, 0), keep_ref, send_ref, slice(0, size))
    columns = slice(size, size + table_in.shape[1])

    @pl.when(quarter == 0)
    def _():
        hand_out(places[2], table_in[...] + table_direct[...], keep_ref, send_ref, columns)

    for index, ref in ((1, table_out), (2, gain)):

        @pl.when(quarter == index)
        def _(ref=ref):
            hand_out(places[2], ref[...], keep_ref, send_ref, columns)

    @pl.when(quarter == 3)
    def _():
        hand_out(places[2], jnp.zeros(table_in.shape, F32), keep_ref, send_ref, columns)


def item_kernel(places, *refs, pairs, exact):
    ins, outs = refs[: 2 * pairs], refs[2 * pairs :]
    step = pl.program_id(0)
    for index, out in enumerate(outs):

        @pl.when(step == index)
        def _(index=index, out=out):
            start = 0
            for pair in range(pairs):
                keep, came = ins[2 * pair : 2 * pair + 2]
                value = keep[0] + came[0]
                size = value.shape[-1]
                out[:, :, start : start + size] = value.astype(out.dtype)
                if index > 0 and exact and pair == pairs - 1:
                    part = value[:, :, size - exact :]
                    rest = part - part.astype(out.dtype).astype(F32)
                    out[:, :, start + size : start + size + exact] = rest.astype(out.dtype)
                start += size


def band_kernel(places, *refs, groups, count, exact):
    ins, outs = refs[: groups * (1 + count)], refs[groups * (1 + count) :]
    step = pl.program_id(0)
    start = 0
    for group in range(groups):
        own, *came = ins[group * (1 + count) : (group + 1) * (1 + count)]
        size = own.shape[-1]
        total = own[0]
        for ref in came:
            total = total + ref[0, :, :size].astype(F32)
        last = exact and group == groups - 1
        if last:
            part = total[:, size - exact :] + sum(ref[0, :, size:].astype(F32) for ref in came)
            high = part.astype(BF16)
            rest = (part - high.astype(F32)).astype(BF16)
        for index, out in enumerate(outs):

            @pl.when(step == index)
            def _(index=index, out=out):
                out[:, start : start + size] = total.astype(out.dtype)
                if last and index == 0:
                    out[:, start + size - exact : start + size] = part
                elif last:
                    out[:, start + size - exact : start + size] = high
                    out[:, start + size : start + size + exact] = rest

        start += size


def exchange(value, axis, distance):
    size = lax.axis_size(axis)
    return lax.ppermute(value, axis, [(i, i ^ distance) for i in range(size)])


def prefetched(kernel, grid, outs, in_specs, out_specs, places, operands, moved, weight=1):
    return pl.pallas_call(
        kernel,
        grid_spec=pltpu.PrefetchScalarGridSpec(
            num_scalar_prefetch=1, grid=grid, in_specs=in_specs, out_specs=out_specs
        ),
        out_shape=outs,
        cost_estimate=pl.CostEstimate(flops=moved * WEIGH * weight, bytes_accessed=moved * WEIGH, transcendentals=0),
        compiler_params=pltpu.CompilerParams(vmem_limit_bytes=VMEM_BYTES * 2 // 3),
    )(places, *[far(x) for x in operands])


def sort_shares(keeps, sends, places, exact=0, late=()):
    items = lax.axis_size("item")
    came = [exchange(send, "lat", 1) for send in sends]
    quarters, bands, rows, _ = keeps[0].shape
    size = sum(keep.shape[-1] for keep in keeps)
    wide = size + exact
    operands = [after(x, *late) for pair in zip(keeps, came) for x in pair]
    return prefetched(
        functools.partial(item_kernel, pairs=len(keeps), exact=exact),
        (items,),
        [shape((bands, rows, size), F32)] + [shape((bands, rows, wide), BF16)] * (items - 1),
        [pl.BlockSpec((1,) + x.shape[1:], lambda j, s: (s[3] ^ j, 0, 0, 0)) for x in operands],
        [pl.BlockSpec((bands, rows, size), lambda j, s: (0, 0, 0))]
        + [pl.BlockSpec((bands, rows, wide), lambda j, s: (0, 0, 0))] * (items - 1),
        places,
        operands,
        moved=14 * bands * rows * size * items,
    )


def swap_items(sorted_shares):
    own, *others = sorted_shares
    return [own] + [exchange(x, "item", k + 1) for k, x in enumerate(others)]


def sum_items(groups, places, exact=0):
    items = len(groups[0])
    bands, rows, _ = groups[0][0].shape
    operands = [x for group in groups for x in group]
    size = sum(group[0].shape[-1] for group in groups)
    wide = size + exact
    return prefetched(
        functools.partial(band_kernel, groups=len(groups), count=items - 1, exact=exact),
        (bands,),
        [shape((rows, size), F32)] + [shape((rows, wide), BF16)] * (bands - 1),
        [pl.BlockSpec((1,) + x.shape[1:], lambda j, s: (s[4] ^ j, 0, 0)) for x in operands],
        [pl.BlockSpec((rows, size), lambda j, s: (0, 0))]
        + [pl.BlockSpec((rows, wide), lambda j, s: (0, 0))] * (bands - 1),
        places,
        operands,
        moved=14 * bands * rows * size,
        weight=10000,
    )


def sum_bands(parts, exact=0, late=()):
    own, *others = parts
    size = own.shape[-1]
    came = [exchange(x, "lat", 2 * (k + 1)) for k, x in enumerate(others)]
    total = after(own, *late) if late else own
    for x in came:
        total = total + x[:, :size].astype(F32)
    if exact:
        rest = sum(x[:, size:].astype(F32) for x in came)
        total = jnp.concatenate([total[:, : size - exact], total[:, size - exact :] + rest], axis=1)
    return total


def after(value, *others):
    result = lax.optimization_barrier((value, *others))[0]
    if is_far(value):
        FAR.append(result)
    return result


def total_kernel(own, *refs):
    *came, out0, out1 = refs
    total = own[...]
    for ref in came:
        total = total + ref[...].astype(F32)
    half = out0.shape[-1]
    out0[...] = total[:, :half]
    out1[...] = total[:, half:]


def add_bands(parts, late):
    own, *others = parts
    came = [exchange(x, "lat", 2 * (k + 1)) for k, x in enumerate(others)]
    return call(
        total_kernel,
        (1,),
        [shape((own.shape[0], own.shape[1] // 2), F32)] * 2,
        [whole(own.shape)] * len(parts),
        [whole((own.shape[0], own.shape[1] // 2))] * 2,
        (after(own, *late), *came),
        flops=10**11,
        moved=16 * own.size,
        near=(0, 1),
    )


def all_items(one, two):
    one_near, two_far = exchange(one, "item", 1), exchange(two, "item", 2)
    one_far, two_near = exchange(one, "item", 2), exchange(two, "item", 1)
    return [
        (one, two), (one_near, two_near), (one_far, two_far),
        (exchange(one_near, "item", 2), exchange(two_far, "item", 1)),
    ]


def sum_over(value, axis):
    distance = 1
    while distance < lax.axis_size(axis):
        value = value + exchange(value, axis, distance)
        distance *= 2
    return value


def adam_kernel(places, factor, *refs):
    dec, proc, down, up, whole_up = (refs[4 * i : 4 * i + 4] for i in range(5))
    mlp, attn, tables, gains = (refs[20 + 4 * i : 24 + 4 * i] for i in range(4))
    mlp_out, attn_out, tables_out, gains_out = (refs[36 + 5 * i : 41 + 5 * i] for i in range(4))
    size = down[0].shape[-1] - attn[0].shape[-1] // 4
    part = attn[0].shape[-1] // 4
    scale = factor[0]
    block, layer = pl.program_id(0), pl.program_id(1)

    def update(share, state, new_state, at, rate, decay):
        new = adam_update(scale * share, *(ref[at] for ref in state), rate, decay)
        for ref, value in zip(new_state, new):
            ref[at] = value

    for k in range(4):
        quarter = places[3] ^ k
        for index, sides in enumerate(((up, down), (proc, proc), (dec, dec))):

            @pl.when(layer == index)
            def _(k=k, index=index, sides=sides, quarter=quarter):
                for side, shares in enumerate(sides):
                    start = 0 if index == 0 else side * size
                    columns = pl.ds(pl.multiple_of((4 * side + quarter) * size, size), size)
                    share = shares[k][:, start : start + size]
                    update(share, mlp, mlp_out, (0, slice(None), columns), RATE_MATRIX, WEIGHT_DECAY)

        @pl.when(layer == 0)
        def _(k=k, quarter=quarter):
            columns = pl.ds(pl.multiple_of(quarter * part, part), part)
            update(down[k][:, size:], attn, attn_out, (slice(None), columns), RATE_MATRIX, WEIGHT_DECAY)

        small = (layer == 0) & (block == 0)
        for table in range(2):

            @pl.when(small & (quarter == table))
            def _(k=k, table=table):
                share = whole_up[k][:, size : size + tables[0].shape[-1]]
                update(share, tables, tables_out, (table,), RATE_MATRIX, WEIGHT_DECAY)

        @pl.when(small & (quarter == 2))
        def _(k=k):
            turned = whole_up[k][:, size:].T[: gains[0].shape[0]]
            update(turned, gains, gains_out, (slice(None),), RATE_GAIN, 0.0)


def projection_back_kernel(
    dq0, dq1, left0, left1, own0, own1, right0, right1, grad_residual, encoded, gains, attn,
    upstream_ref, rounded_ref, project_ref, gain_ref,
):
    pairs = [
        own[...] + left[...].astype(F32) + right[...].astype(F32)
        for left, own, right in ((left0, own0, right0), (left1, own1, right1))
    ]
    project = jnp.concatenate(
        [dq0[...], dq1[...], pairs[0][0], pairs[1][0], pairs[0][1], pairs[1][1]], axis=0
    ).astype(BF16)
    project_ref[...] = project
    grad_normed = dot(project, attn[...], 0, 1)
    grad_encoded, gain_attn = norm_back(grad_normed, encoded[...], gains[1:2])
    upstream = grad_residual[...] + grad_encoded
    upstream_ref[...] = upstream
    rounded_ref[...] = upstream.astype(BF16)
    add_up(gain_ref, gain_attn)


def encoder_back_kernel(
    upstream, pooled, slope, gains, mlp, pin, before_ref, table_ref, gain_ref, rounded_ref
):
    grad_pooled, gain_enc = mlp_backward(
        upstream[...], pooled[...], gains[0:1], mlp, slope, rounded_ref, before_ref
    )
    add_up(gain_ref, gain_enc)
    high, low = two_parts(grad_pooled)
    both = dot(high, pin[...], 0, 0) + dot(low, pin[...], 0, 0)
    channels = both.shape[1] // 2
    add_up(table_ref, both[:, :channels] + both[:, channels:])


def weights(kernel, places, operands, specs, columns, flops, turned):
    rows, width = operands[0].shape
    bands = lax.axis_size("lat") // 2
    out = shape((4, bands, width // (2 * bands), columns), F32)
    out_spec = pl.BlockSpec((1,) + out.shape[1:], lambda i: (i, 0, 0, 0))
    return call(
        kernel,
        (4,),
        [out, out],
        [pl.BlockSpec(memory_space=pltpu.SMEM)] + specs,
        [out_spec, out_spec],
        (places, *operands),
        flops=flops,
        moved=8 * width * columns * 4,
        scratch=[pltpu.VMEM((width, rows), BF16)] * turned,
        vmem=VMEM_BYTES * 2 // 3,
        near=(0, 1),
    )


def adam_update(gradient, master, moment_one, moment_two, average, step_rate, decay_rate):
    one_new = BETA_ONE * moment_one + (1.0 - BETA_ONE) * gradient
    two_new = BETA_TWO * moment_two + (1.0 - BETA_TWO) * gradient * gradient
    one_hat = one_new * (1.0 / (1.0 - BETA_ONE**STEP))
    two_hat = two_new * (1.0 / (1.0 - BETA_TWO**STEP))
    master_new = master - step_rate * (
        one_hat / (jnp.sqrt(two_hat) + ADAM_EPS) + decay_rate * master
    )
    average_new = EMA_DECAY * average + (1.0 - EMA_DECAY) * master_new
    return (one_new, two_new, master_new, average_new, master_new.astype(jnp.bfloat16))


def from_sides(to_left, to_right):
    size = lax.axis_size("lat")
    up = [(i, (i + 1) % size) for i in range(size - 1)]
    down = [(j, i) for i, j in up]
    return lax.ppermute(to_right, "lat", up), lax.ppermute(to_left, "lat", down)


def shards(
    noisy_state,
    target_state,
    sigmas,
    sh_basis,
    lengths,
    grid_edges,
    mesh_edges,
    dec_edges,
    tables_copy,
    tables_master,
    tables_first,
    tables_second,
    tables_ema,
    attn_copy,
    attn_master,
    attn_first,
    attn_second,
    attn_ema,
    mlp_copy,
    mlp_master,
    mlp_first,
    mlp_second,
    mlp_ema,
    gains_copy,
    gains_master,
    gains_first,
    gains_second,
    gains_ema,
):
    FAR.clear()
    band_index = lax.axis_index("lat")
    bands = lax.axis_size("lat")
    item_index = lax.axis_index("item")
    places = jnp.stack([band_index, bands, band_index % 2, item_index, band_index // 2]).astype(jnp.int32)
    rows = mesh_edges.shape[0]
    grid_rows = noisy_state.shape[2]
    width = attn_copy.shape[0]
    channels = noisy_state.shape[1]
    padded = CHANNEL_PAD
    hidden = mlp_copy.shape[2] // 2
    depth = width // HEADS
    FAR.extend([mlp_copy, attn_copy, mlp_master, mlp_first, mlp_second, mlp_ema])
    FAR.extend([attn_master, attn_first, attn_second, attn_ema])
    gains = gains_copy.astype(F32)
    gain_rows = gains.shape[0]
    noise_level = sigmas[0]
    square = noise_level * noise_level
    scale_in = lax.rsqrt(square + 1.0)
    scale_skip = 1.0 / (square + 1.0)
    scale_out = noise_level * scale_in
    weight_loss = (square + 1.0) / square
    noisy_field = noisy_state[0]
    target_field = target_state[0]
    extra = padded - channels
    inputs = jnp.pad((scale_in * noisy_field).astype(BF16), ((0, extra), (0, 0)))
    tables = jnp.pad(tables_copy, ((0, 0), (0, extra), (0, 0)))

    def weights_spec(index):
        return pl.BlockSpec((1, width, 2 * hidden), lambda *_: (index, 0, 0))

    wout_spec = pl.BlockSpec((width, width), lambda *_: (0, 3))
    few = HEADS // GROUPS
    part = few * depth
    gains_spec = whole(gains.shape)
    tables_spec = whole(tables.shape)
    steps = rows // ROWS
    kept_shapes = [shape((rows, width), BF16), shape((rows, hidden), F32), shape((rows, hidden), BF16)]
    kept_specs = [rows_of(width), rows_of(hidden), rows_of(hidden)]
    mlp_flops = 4 * rows * width * hidden

    pin, pooled, encoded, normed_enc, slope_enc, active_enc, normed_attn, queries, *pairs = call(
        encoder_kernel,
        (steps,),
        [shape((rows, 2 * padded), BF16), shape((rows, width), F32), shape((rows, width), F32)]
        + kept_shapes
        + [shape((rows, width), BF16), shape((width, rows), BF16)]
        + [shape((rows, width), BF16)] * GROUPS,
        [
            lanes_of(grid_edges.shape[1]), whole((padded, grid_rows)), tables_spec, gains_spec,
            weights_spec(0), pl.BlockSpec((width, 3 * width), lambda i: (0, 0)),
        ],
        [rows_of(2 * padded), rows_of(width), rows_of(width)]
        + kept_specs
        + [rows_of(width), lanes_of(width)]
        + [rows_of(width)] * GROUPS,
        (grid_edges.T, inputs, tables, gains, mlp_copy, attn_copy),
        flops=mlp_flops + 6 * rows * width * width,
        moved=30 * rows * width,
    )

    crops = lengths.shape[1]
    smem = pl.BlockSpec(memory_space=pltpu.SMEM)
    bias_lanes = 128
    bias = call(
        functools.partial(bias_kernel, crops=crops),
        (rows // bias_lanes,),
        shape((3, rows, rows), F32),
        [smem, smem, lanes_of(mesh_edges.shape[1], bias_lanes)],
        pl.BlockSpec((3, rows, bias_lanes), lambda i: (0, 0, i)),
        (places, jnp.cumsum(lengths[0]), mesh_edges.T),
        flops=2 * 10**9,
        moved=12 * rows * rows,
    )

    windows = []
    for own in pairs:
        if windows:
            own = after(own, *windows[-1], bias)
        came = from_sides(own, own)
        windows.append([came[0], own, came[1]])

    lanes = 512
    attended, lse = [], []
    for g, window in enumerate(windows):
        result, logs = call(
            functools.partial(attend_kernel, chunk=256),
            (rows // lanes, few),
            [shape((part, rows), F32), shape((few, 8, rows), F32)],
            [pl.BlockSpec((depth, lanes), lambda i, h, g=g: (g * few + h, i))]
            + [pl.BlockSpec((rows, depth), lambda i, h: (0, h))] * 3
            + [pl.BlockSpec((rows, depth), lambda i, h: (0, few + h))] * 3
            + [pl.BlockSpec((3, rows, lanes), lambda i, h: (0, 0, i))],
            [
                pl.BlockSpec((depth, lanes), lambda i, h: (h, i)),
                pl.BlockSpec((1, 8, lanes), lambda i, h: (h, 0, i)),
            ],
            (queries, *window, *window, bias),
            scratch=[pltpu.VMEM((3, rows, lanes), F32)],
            flops=24 * rows * rows * part,
            moved=12 * rows * rows,
        )
        attended.append(result)
        lse.append(logs)

    rounded_o, residual, normed_proc, slope_proc, active_proc, sent = call(
        processor_kernel,
        (steps,),
        [shape((width, rows), BF16), shape((rows, width), F32)] + kept_shapes + [shape((rows, width), BF16)],
        [lanes_of(part)] * GROUPS + [rows_of(width), gains_spec, weights_spec(1), wout_spec],
        [lanes_of(width), rows_of(width)] + kept_specs + [rows_of(width)],
        (*attended, encoded, gains, mlp_copy, attn_copy),
        flops=mlp_flops + 2 * rows * width * width,
        moved=24 * rows * width,
        near=(5,),
    )

    before_sent, after_sent = from_sides(sent, sent)

    dec_count = dec_edges.shape[1]
    tally, partial = call(
        window_kernel,
        (grid_rows // ROWS,),
        [shape((3, rows, grid_rows), BF16), shape((grid_rows, width), F32)],
        [lanes_of(dec_count), whole((rows, width)), lanes_of(padded), tables_spec],
        [pl.BlockSpec((3, rows, ROWS), lambda i: (0, 0, i)), rows_of(width)],
        (dec_edges.T, sent, inputs, tables),
        flops=2 * rows * rows * width,
        moved=24 * rows * width,
    )
    joined, normed_dec, slope_dec, active_dec, decoded, final, output = call(
        functools.partial(decoder_kernel, count=dec_count),
        (grid_rows // ROWS,),
        [shape((grid_rows, width), F32)]
        + kept_shapes
        + [shape((grid_rows, width), F32), shape((grid_rows, width), BF16), shape((padded, grid_rows), F32)],
        [
            pl.BlockSpec((3, rows, ROWS), lambda i: (0, 0, i)), whole((rows, width)), whole((rows, width)),
            rows_of(width), tables_spec, gains_spec, weights_spec(2),
        ],
        [rows_of(width)] + kept_specs + [rows_of(width), rows_of(width), lanes_of(padded)],
        (tally, before_sent, after_sent, partial, tables, gains, mlp_copy),
        flops=mlp_flops + 6 * rows * rows * width,
        moved=24 * rows * width,
    )

    error_field = scale_skip * noisy_field + scale_out * output[:channels] - target_field
    partial_value = lax.dot_general(
        error_field,
        sh_basis,
        (((1,), (1,)), ((), ())),
        precision=HIGH_PRECISION,
        preferred_element_type=F32,
    )
    coeffs = sum_over(partial_value, "lat")
    slice_width = coeffs.shape[1] // bands
    own_coeffs = lax.dynamic_slice_in_dim(coeffs, band_index * slice_width, slice_width, 1)
    loss_item = weight_loss * jnp.sum(own_coeffs * own_coeffs)
    grad_error = jnp.dot(
        2.0 * weight_loss * coeffs, sh_basis, precision=HIGH_PRECISION, preferred_element_type=F32
    )
    grad_output = jnp.pad((scale_out * grad_error).astype(BF16), ((0, extra), (0, 0)))

    join_high, join_low, rounded_dec, before_dec, table_out, gain_dec, table_direct = call(
        decoder_back_kernel,
        (grid_rows // ROWS,),
        [
            shape((grid_rows, width), BF16), shape((grid_rows, width), BF16), shape((grid_rows, width), BF16),
            shape((grid_rows, hidden), BF16), shape((width, padded), F32), shape((2, width), F32),
            shape((width, padded), F32),
        ],
        [
            lanes_of(padded), tables_spec, rows_of(width), rows_of(width), rows_of(width), rows_of(hidden),
            gains_spec, weights_spec(2), lanes_of(padded),
        ],
        [
            rows_of(width), rows_of(width), rows_of(width), rows_of(hidden), whole((width, padded)),
            whole((2, width)), whole((width, padded)),
        ],
        (grad_output, tables, decoded, final, joined, slope_dec, gains, mlp_copy, inputs),
        flops=mlp_flops,
        moved=24 * rows * width,
        near=(0, 1, 2),
    )

    to_left, grad_own, to_right = call(
        scatter_kernel,
        (steps,),
        [shape((rows, width), BF16), shape((rows, width), F32), shape((rows, width), BF16)],
        [whole((dec_count, grid_rows)), whole((grid_rows, width)), whole((grid_rows, width))],
        [rows_of(width)] * 3,
        (dec_edges.T, join_high, join_low),
        near=(0, 1, 2),
        flops=12 * rows * grid_rows * width,
        moved=12 * rows * width,
    )
    from_left, from_right = from_sides(to_left, to_right)
    quarter = hidden // 4
    columns_of = pl.BlockSpec((rows, quarter), lambda i: (0, i))
    table_spec = whole((width, padded))
    full = whole((rows, width))
    product = 2 * rows * width * width

    def layer_weights(*operands):
        return weights(
            weights_kernel, places, operands, [full, full, columns_of, columns_of], 2 * quarter, 8 * product, 2
        )

    keep_dec, send_dec = layer_weights(normed_dec, after(rounded_dec, to_left, to_right), before_dec, active_dec)
    sorted_dec = sort_shares([keep_dec], [send_dec], places)
    swapped_dec = swap_items(sorted_dec)

    grad_residual, rounded_proc, before_proc, gain_proc, branch, grad_o, delta = call(
        processor_back_kernel,
        (steps,),
        [
            shape((rows, width), F32), shape((rows, width), BF16), shape((rows, hidden), BF16),
            shape((1, width), F32), shape((rows, width), BF16), shape((width, rows), BF16),
            shape((HEADS, 8, rows), F32),
        ],
        [rows_of(width)] * 4 + [rows_of(hidden), gains_spec, weights_spec(1), wout_spec] + [lanes_of(part)] * GROUPS,
        [
            rows_of(width), rows_of(width), rows_of(hidden), whole((1, width)), rows_of(width), lanes_of(width),
            pl.BlockSpec((HEADS, 8, ROWS), lambda i: (0, 0, i)),
        ],
        (from_left, after(grad_own, keep_dec, send_dec), from_right, residual, slope_proc, gains, mlp_copy, attn_copy,
            *attended,
        ),
        flops=mlp_flops + 2 * rows * width * width,
        moved=24 * rows * width,
        near=(1, 5),
    )

    block = 512
    side = pl.BlockSpec((2, depth, block), lambda i, h: (0, h, i))
    group_spec = whole((few, 8, rows))
    grad_queries, sides = [], []
    ahead = tuple(sorted_dec)
    for g, window in enumerate(windows):
        row_spec = pl.BlockSpec((part, rows), lambda i, h, g=g: (g, 0))
        dq, left, own, right = call(
            functools.partial(attend_back_kernel, chunk=256),
            (rows // block, few),
            [
                shape((part, rows), F32), shape((2, part, rows), BF16), shape((2, part, rows), F32),
                shape((2, part, rows), BF16),
            ],
            [row_spec, row_spec, group_spec, pl.BlockSpec((few, 8, rows), lambda i, h, g=g: (g, 0, 0))]
            + [pl.BlockSpec((block, depth), lambda i, h: (i, h))] * 3
            + [pl.BlockSpec((block, depth), lambda i, h: (i, few + h))] * 3
            + [pl.BlockSpec((3, block, rows), lambda i, h: (0, i, 0))],
            [whole((part, rows)), side, side, side],
            (queries, after(grad_o, *ahead), lse[g], delta, *window, *window, bias),
            scratch=[pltpu.VMEM((block, rows), BF16), pltpu.VMEM((block, rows), BF16)],
            flops=60 * rows * rows * part,
            moved=12 * rows * rows,
        )
        if sides:
            left, right = after(left, *sides[-1]), after(right, *sides[-1])
        came = from_sides(left, right)
        sides.append([came[0], own, came[1]])
        grad_queries.append(dq)
        ahead = tuple(swapped_dec)

    keep_proc, send_proc = layer_weights(normed_proc, after(rounded_proc, left, right), before_proc, active_proc)
    side_spec = pl.BlockSpec((2, part, ROWS), lambda i: (0, 0, i))
    upstream, rounded_enc, project, gain_attn = call(
        projection_back_kernel,
        (steps,),
        [
            shape((rows, width), F32), shape((rows, width), BF16), shape((3 * width, rows), BF16),
            shape((1, width), F32),
        ],
        [lanes_of(part)] * 2 + [side_spec] * 6
        + [rows_of(width)] * 2 + [gains_spec, pl.BlockSpec((width, 3 * width), lambda i: (0, 0))],
        [rows_of(width), rows_of(width), lanes_of(3 * width), whole((1, width))],
        (
            *grad_queries, sides[0][0], sides[1][0], sides[0][1], sides[1][1], sides[0][2], sides[1][2],
            after(grad_residual, keep_proc, send_proc), encoded, gains, attn_copy,
        ),
        flops=3 * product,
        moved=24 * rows * width,
        near=(0, 1, 2),
    )
    sorted_proc = sort_shares([keep_proc], [send_proc], places, late=(upstream,))
    swapped_proc = swap_items(sorted_proc)
    keep_down, send_down = weights(
        down_weights_kernel,
        places,
        (after(rounded_enc, *sorted_proc), active_enc, normed_attn, project, rounded_o, branch),
        [full, columns_of, full, pl.BlockSpec((width, rows), lambda i: (jnp.minimum(i, 2), 0)), whole((width, rows)), full],
        quarter + width,
        8 * product,
        2,
    )
    sorted_down = sort_shares([keep_down], [send_down], places)
    before_enc, table_in, gain_enc, _ = call(
        encoder_back_kernel,
        (steps,),
        [
            shape((rows, hidden), BF16), shape((width, padded), F32), shape((1, width), F32),
            shape((rows, width), BF16),
        ],
        [rows_of(width)] * 2
        + [rows_of(hidden), gains_spec, weights_spec(0), rows_of(2 * padded)],
        [rows_of(hidden), table_spec, whole((1, width)), rows_of(width)],
        (after(upstream, *sorted_down), pooled, slope_enc, gains, mlp_copy, pin),
        flops=mlp_flops,
        moved=24 * rows * width,
    )
    grad_gains = jnp.concatenate([gain_enc, gain_attn, gain_proc, gain_dec], axis=0)
    gain_columns = jnp.pad(grad_gains.T, ((0, 0), (0, padded - gain_rows)))
    swapped_down = swap_items([sorted_down[0]] + [after(x, *swapped_proc, before_enc) for x in sorted_down[1:]])
    own_proc = [after(swapped_proc[0], before_enc)] + swapped_proc[1:]
    first_parts = sum_items([swapped_dec, own_proc], places)
    first_total = add_bands(first_parts, (first_parts[0],))
    keep_up, send_up = weights(
        up_weights_kernel,
        places,
        (normed_enc, after(before_enc, first_parts[0]), table_in, table_direct, table_out, gain_columns),
        [full, columns_of, table_spec, table_spec, table_spec, table_spec],
        quarter + padded,
        4 * product,
        1,
    )
    down_parts = sum_items([swapped_down], places)
    down_total = sum_bands(down_parts)
    sorted_up = sort_shares([keep_up], [send_up], places, exact=padded, late=(down_parts[0], *first_total))
    swapped_up = swap_items([sorted_up[0]] + [after(x, *swapped_down) for x in sorted_up[1:]])
    first_all = all_items(*[after(x, sorted_up[0]) for x in first_total])
    ready = [x for pair in first_all for x in pair]
    up_total = sum_bands(sum_items([swapped_up], places, exact=padded), exact=padded)
    squares = sum(jnp.sum(jnp.square(x.astype(F32))) for x in (*first_total, down_total, up_total))
    scalars = sum_over(jnp.stack([squares, loss_item])[None], "lat")
    place = [lax.broadcasted_iota(jnp.int32, up_total.shape, dim) for dim in range(2)]
    carried = jnp.where(place[0] == 0, scalars[0, 0], scalars[0, 1])
    up_total = jnp.where((place[1] == up_total.shape[1] - 1) & (place[0] < 2), carried, up_total)
    last_all = all_items(after(down_total, *ready), after(up_total, *ready))
    scalars = [x[:2, -1] for _, x in last_all]
    scalars = (scalars[0] + scalars[1]) + (scalars[2] + scalars[3])
    loss_sum = scalars[1]
    grad_norm = jnp.sqrt(scalars[0])
    scale_factor = CLIP_LEVEL / jnp.maximum(grad_norm, CLIP_LEVEL)

    shard_rows = attn_master.shape[0]
    block_rows = min(shard_rows, 32)
    mlp_spec = pl.BlockSpec((1, block_rows, 2 * hidden), lambda r, l, s: (l, r, 0))
    attn_part = pl.BlockSpec((block_rows, attn_master.shape[1]), lambda r, l, s: (r, 0))
    kinds = [F32, F32, F32, F32, BF16]
    shares = [x for pair in zip(*first_all) for x in pair] + [x for pair in zip(*last_all) for x in pair]
    state = (mlp_master, mlp_first, mlp_second, mlp_ema, attn_master, attn_first, attn_second, attn_ema)
    table_state = [jnp.swapaxes(x, 1, 2) for x in (tables_master, tables_first, tables_second, tables_ema)]
    FAR.extend([*table_state, *shares])
    updated = prefetched(
        adam_kernel,
        (shard_rows // block_rows, mlp_master.shape[0]),
        [shape(x.shape, kind) for x in (mlp_master, attn_master, table_state[0], gains_master) for kind in kinds],
        [smem]
        + [pl.BlockSpec((block_rows, x.shape[1]), lambda r, l, s: (r, 0)) for x in shares]
        + [pl.BlockSpec(x.shape, lambda *_: (0, 0)) for x in shares[-4:]]
        + [mlp_spec] * 4
        + [attn_part] * 4
        + [whole(table_state[0].shape)] * 4
        + [whole(gains_master.shape)] * 4,
        [mlp_spec] * 5 + [attn_part] * 5 + [whole(table_state[0].shape)] * 5 + [whole(gains_master.shape)] * 5,
        places,
        (
            scale_factor[None], *shares, *shares[-4:], *state, *table_state,
            gains_master, gains_first, gains_second, gains_ema,
        ),
        moved=34 * (mlp_master.size + attn_master.size),
    )
    mlps, att, gns = updated[:5], updated[5:10], updated[15:]
    tab = [jnp.swapaxes(x, 1, 2) for x in updated[10:15]]
    return (loss_sum, grad_norm, *tab, *att, *mlps, *gns)


def solution(mesh):
    table = P(None, None, "lat")
    attn = P("lat", None)
    mlp = P(None, "lat", None)
    gain = P(None, "lat")
    placed = (
        P("item", None, "lat"),
        P("item", None, "lat"),
        P("item"),
        P(None, "lat"),
        P("item", None),
        P("lat", None),
        P("lat", None),
        P("lat", None),
        P(), table, table, table, table,
        P(), attn, attn, attn, attn,
        P(), mlp, mlp, mlp, mlp,
        P(), gain, gain, gain, gain,
    )
    return jax.shard_map(
        shards,
        mesh=mesh,
        in_specs=placed,
        out_specs=(P(), P(), *([table] * 5), *([attn] * 5), *([mlp] * 5), *([gain] * 5)),
        check_vma=False,
    )
```

```python
import functools

import jax
import jax.numpy as jnp
from jax import lax
from jax.experimental import pallas as pl
from jax.experimental.pallas import tpu as pltpu
from jax.sharding import PartitionSpec as P

HEADS = 4
GROUPS = 2
WEIGH = 30
LARGE = 1 << 20
STEP = 10

EPS_NORM = 1e-05
CLIP_LEVEL = 1.0
BETA_ONE = 0.9
BETA_TWO = 0.999
ADAM_EPS = 1e-08
EMA_DECAY = 0.9
RATE_MATRIX = 0.05
RATE_GAIN = 0.3
WEIGHT_DECAY = 0.1
HIGH_PRECISION = lax.Precision.HIGHEST

F32 = jnp.float32
BF16 = jnp.bfloat16
LOG2E = 1.4426950408889634
CHANNEL_PAD = 128
ROWS = 256
VMEM_BYTES = 36 * 1024 * 1024


def dot(left, right, left_dim, right_dim):
    return lax.dot_general(
        left, right, (((left_dim,), (right_dim,)), ((), ())), preferred_element_type=F32
    )


FAR = []


def is_far(value):
    return any(value is x for x in FAR)


def far(value):
    return pltpu.with_memory_space_constraint(value, pltpu.HBM) if is_far(value) else value


def call(kernel, grid, outs, in_specs, out_specs, operands, scratch=(), flops=0, moved=0, near=(), vmem=VMEM_BYTES):
    single = not isinstance(outs, list)
    kinds = [outs] if single else outs
    large = [i not in near and x.size * x.dtype.itemsize >= LARGE for i, x in enumerate(kinds)]
    kinds = [pltpu.HBM(x.shape, x.dtype) if flag else x for x, flag in zip(kinds, large)]
    results = pl.pallas_call(
        kernel,
        grid=grid,
        out_shape=kinds[0] if single else kinds,
        in_specs=in_specs,
        out_specs=out_specs,
        scratch_shapes=list(scratch),
        cost_estimate=pl.CostEstimate(flops=flops * WEIGH, bytes_accessed=moved * WEIGH, transcendentals=0),
        compiler_params=pltpu.CompilerParams(vmem_limit_bytes=vmem),
    )(*[far(x) for x in operands])
    FAR.extend(x for x, flag in zip([results] if single else results, large) if flag)
    return results


def whole(shape):
    return pl.BlockSpec(shape, lambda *_: (0,) * len(shape))


def rows_of(width, rows=ROWS):
    return pl.BlockSpec((rows, width), lambda i: (i, 0))


def lanes_of(height, lanes=ROWS):
    return pl.BlockSpec((height, lanes), lambda i: (0, i))


def shape(dims, kind):
    return jax.ShapeDtypeStruct(dims, kind)


def norm_parts(values):
    center = values - jnp.mean(values, axis=-1, keepdims=True)
    spread = jnp.mean(center * center, axis=-1, keepdims=True)
    inverse = lax.rsqrt(spread + EPS_NORM)
    return center * inverse, inverse


def norm_back(upstream, values, gain_row):
    unit, inverse = norm_parts(values)
    scaled = upstream * gain_row
    along = jnp.mean(scaled * unit, axis=-1, keepdims=True)
    grad = inverse * (scaled - jnp.mean(scaled, axis=-1, keepdims=True) - unit * along)
    gain_grad = jnp.sum(upstream * unit, axis=0, keepdims=True)
    return grad, gain_grad


def gelu_parts(u):
    root = 0.7978845608028654
    cubic = 0.044715
    square = u * u
    inner = u * (root + (root * cubic) * square)
    half = 0.5 + 0.5 * jnp.tanh(inner)
    slope = half * (1.0 + (1.0 - half) * (6.0 * inner - (4.0 * root) * u))
    return u * half, slope


def mlp_forward(values, gain_row, w_ref, normed_ref, slope_ref, active_ref, step=512):
    hidden = w_ref.shape[-1] // 2
    normed = (norm_parts(values)[0] * gain_row).astype(BF16)
    normed_ref[...] = normed
    result = jnp.zeros(values.shape, F32)
    starts = range(0, hidden, step)
    befores = [dot(normed, w_ref[0, :, :step], 1, 0)]
    for start in starts:
        part = slice(start, start + step)
        if start + step < hidden:
            befores.append(dot(normed, w_ref[0, :, start + step : start + 2 * step], 1, 0))
        active, slope = gelu_parts(befores.pop(0))
        active = active.astype(BF16)
        slope_ref[:, part] = slope
        active_ref[:, part] = active
        result = result + dot(active, w_ref[0, :, hidden + start : hidden + start + step], 1, 1)
    return values + result


def mlp_backward(upstream, values, gain_row, w_ref, slope_ref, rounded_ref, before_ref, step=512):
    hidden = w_ref.shape[-1] // 2
    rounded = upstream.astype(BF16)
    rounded_ref[...] = rounded
    grad_normed = jnp.zeros(values.shape, F32)
    ahead = [dot(rounded, w_ref[0, :, hidden : hidden + step], 1, 0)]
    for start in range(0, hidden, step):
        part = slice(start, start + step)
        if start + step < hidden:
            ahead.append(dot(rounded, w_ref[0, :, hidden + start + step : hidden + start + 2 * step], 1, 0))
        grad_before = (ahead.pop(0) * slope_ref[:, part]).astype(BF16)
        before_ref[:, part] = grad_before
        grad_normed = grad_normed + dot(grad_before, w_ref[0, :, part], 1, 1)
    grad, gain_grad = norm_back(grad_normed, values, gain_row)
    return upstream + grad, gain_grad


def two_parts(values):
    high = values.astype(BF16)
    return high, (values - high.astype(F32)).astype(BF16)


def named(edges, places):
    tally = jnp.zeros(places.shape, F32)
    for j in range(edges.shape[0]):
        tally = tally + jnp.where(edges[j : j + 1, :] == places, 1.0, 0.0)
    return tally.astype(BF16)


def add_up(ref, value):
    step = pl.program_id(0)

    @pl.when(step == 0)
    def _():
        ref[...] = value

    @pl.when(step > 0)
    def _():
        ref[...] += value


def encoder_kernel(
    edges, x, table, gains, mlp, attn,
    pin_ref, pooled_ref, encoded_ref, normed_ref, slope_ref, active_ref, normed_attn_ref, q_ref, *pair_refs,
):
    count, rows = edges.shape
    width = attn.shape[0]
    places = lax.broadcasted_iota(jnp.int32, (x.shape[1], rows), 0)
    pin = dot(named(edges, places), x[...], 0, 1) / count
    high, low = two_parts(pin)
    pin_ref[...] = jnp.concatenate([high, low], axis=1)
    pooled = dot(high, table[0], 1, 0) + dot(low, table[0], 1, 0)
    pooled_ref[...] = pooled
    encoded = mlp_forward(pooled, gains[0:1], mlp, normed_ref, slope_ref, active_ref)
    encoded_ref[...] = encoded
    normed_attn = (norm_parts(encoded)[0] * gains[1:2]).astype(BF16)
    normed_attn_ref[...] = normed_attn
    q_ref[...] = dot(attn[:, :width], normed_attn, 0, 1).astype(BF16)
    part = width // len(pair_refs)
    for g, ref in enumerate(pair_refs):
        for side in range(2):
            start = (1 + side) * width + g * part
            ref[:, side * part : (side + 1) * part] = dot(
                normed_attn, attn[:, start : start + part], 1, 0
            ).astype(BF16)


def bias_kernel(places, ends, edges, bias_ref, *, crops):
    count, lanes = edges.shape
    rows = bias_ref.shape[1]
    window = bias_ref.shape[0] * rows
    col = pl.program_id(0)
    nodes = col * lanes + lax.broadcasted_iota(jnp.int32, (1, lanes), 1)
    first = places[0] * rows
    low = jnp.zeros((1, lanes), jnp.int32)
    high = jnp.full((1, lanes), places[1] * rows, jnp.int32)
    for c in range(crops - 1, -1, -1):
        high = jnp.where(ends[c] > first + nodes, ends[c], high)
    for c in range(crops):
        low = jnp.where(ends[c] <= first + nodes, ends[c], low)
    near = edges[...] + (first - rows)
    place = jnp.where((near >= low) & (near < high), edges[...], -1)
    place = jnp.concatenate([place, rows + nodes], axis=0)
    tile = 128
    tiles = window // tile
    each = 6
    fine = jnp.where(place < 0, -1, place % tile)
    coarse = place // tile
    sub = lax.broadcasted_iota(jnp.int32, (tile, lanes), 0)
    for start in range(0, tiles, each):
        here = (coarse >= start) & (coarse < start + each)
        amount = jnp.where(here, jnp.left_shift(1, 5 * jnp.where(here, coarse - start, 0)), 0)
        total = jnp.zeros((tile, lanes), jnp.int32)
        for j in range(count + 1):
            total = total + jnp.where(sub == fine[j : j + 1], amount[j : j + 1], 0)
        for t in range(start, min(tiles, start + each)):
            tally = jnp.bitwise_and(jnp.right_shift(total, 5 * (t - start)), 31)
            value = jnp.where(tally == 0, -1e30, jnp.log2(jnp.maximum(tally, 1).astype(F32)))
            at = t * tile
            bias_ref[at // rows, at % rows : at % rows + tile, :] = value


def attend_kernel(q_ref, k0, k1, k2, v0, v1, v2, bias, o_ref, l_ref, scores, *, chunk):
    depth, lanes = q_ref.shape
    rows = k0.shape[0]
    factor = depth**-0.5 * LOG2E
    q = q_ref[...]
    top = jnp.full((8, lanes), -3e38, F32)
    for w, keys in enumerate((k0, k1, k2)):
        for start in range(0, rows, chunk):
            part = slice(start, start + chunk)
            score = dot(keys[part, :], q, 1, 0) * factor + bias[w, part, :]
            scores[w, part, :] = score
            top = jnp.maximum(top, jnp.max(score.reshape(chunk // 8, 8, lanes), axis=0))
    top = jnp.max(top, axis=0, keepdims=True)
    total = jnp.zeros((8, lanes), F32)
    result = jnp.zeros((depth, lanes), F32)
    for w, values in enumerate((v0, v1, v2)):
        for start in range(0, rows, chunk):
            part = slice(start, start + chunk)
            e = jnp.exp2(scores[w, part, :] - top)
            total = total + jnp.sum(e.reshape(chunk // 8, 8, lanes), axis=0)
            result = result + dot(values[part, :], e.astype(BF16), 0, 0)
    total = jnp.sum(total, axis=0, keepdims=True)
    o_ref[...] = result * (1.0 / total)
    l_ref[...] = jnp.broadcast_to((top + jnp.log2(total))[None], l_ref.shape)


def processor_kernel(
    o0, o1, encoded, gains, mlp, attn,
    attended_ref, residual_ref, normed_ref, slope_ref, active_ref, sent_ref,
):
    attended = jnp.concatenate([o0[...], o1[...]], axis=0).astype(BF16)
    attended_ref[...] = attended
    residual = encoded[...] + dot(attended, attn[...], 0, 0)
    residual_ref[...] = residual
    latent = mlp_forward(residual, gains[2:3], mlp, normed_ref, slope_ref, active_ref)
    sent_ref[...] = latent.astype(BF16)


def window_kernel(edges, sent, x, tables, tally_ref, partial_ref):
    count = edges.shape[0]
    bands, band, rows = tally_ref.shape
    places = lax.broadcasted_iota(jnp.int32, (band, rows), 0)
    for w in range(bands):
        tally_ref[w] = named(edges, places + w * band)
    gathered = dot(tally_ref[1], sent[...], 0, 0)
    partial_ref[...] = dot(x[...], tables[0], 0, 0) + gathered / count


def decoder_kernel(
    tally, s0, s2, partial, tables, gains, mlp,
    joined_ref, normed_ref, slope_ref, active_ref, decoded_ref, final_ref, output_ref, *, count,
):
    gathered = dot(tally[0], s0[...], 0, 0) + dot(tally[2], s2[...], 0, 0)
    joined = partial[...] + gathered / count
    joined_ref[...] = joined
    decoded = mlp_forward(joined, gains[3:4], mlp, normed_ref, slope_ref, active_ref)
    decoded_ref[...] = decoded
    final = (norm_parts(decoded)[0] * gains[4:5]).astype(BF16)
    final_ref[...] = final
    output_ref[...] = dot(tables[1], final, 1, 1)


def decoder_back_kernel(
    grad_output, tables, decoded, final, joined, slope, gains, mlp, x,
    high_ref, low_ref, rounded_ref, before_ref, table_ref, gain_ref, direct_ref,
):
    grad_final = dot(grad_output[...], tables[1], 0, 0)
    add_up(table_ref, dot(final[...], grad_output[...], 0, 1))
    grad_decoded, gain_final = norm_back(grad_final, decoded[...], gains[4:5])
    grad_join, gain_dec = mlp_backward(
        grad_decoded, joined[...], gains[3:4], mlp, slope, rounded_ref, before_ref
    )
    high, low = two_parts(grad_join)
    high_ref[...] = high
    low_ref[...] = low
    add_up(direct_ref, dot(high, x[...], 0, 1) + dot(low, x[...], 0, 1))
    add_up(gain_ref, jnp.concatenate([gain_dec, gain_final], axis=0))


def scatter_kernel(edges, high, low, *outs):
    rows = outs[0].shape[0]
    count, total = edges.shape
    sub = lax.broadcasted_iota(jnp.int32, (rows, total), 0) + pl.program_id(0) * rows
    for w, out in enumerate(outs):
        tally = named(edges, sub + w * total)
        value = dot(tally, high[...], 1, 0) + dot(tally, low[...], 1, 0)
        out[...] = (value / count).astype(out.dtype)


def processor_back_kernel(
    g0, g1, g2, residual, slope, gains, mlp, attn, o0, o1,
    grad_residual_ref, rounded_ref, before_ref, gain_ref, branch_ref, grad_o_ref, delta_ref,
):
    width = residual.shape[1]
    upstream = g1[...] + g0[...].astype(F32) + g2[...].astype(F32)
    grad, gain = mlp_backward(
        upstream, residual[...], gains[2:3], mlp, slope, rounded_ref, before_ref
    )
    add_up(gain_ref, gain)
    grad_residual_ref[...] = grad
    branch = grad.astype(BF16)
    branch_ref[...] = branch
    grad_o = dot(attn[...], branch, 1, 1).astype(BF16)
    grad_o_ref[...] = grad_o
    depth = width // HEADS
    attended = jnp.concatenate([o0[...], o1[...]], axis=0)
    together = grad_o.astype(F32) * attended
    for h in range(HEADS):
        row = jnp.sum(together[h * depth : (h + 1) * depth], axis=0, keepdims=True)
        delta_ref[h] = jnp.broadcast_to(row, delta_ref.shape[1:])


def attend_back_kernel(
    q_ref, do_ref, lse_ref, delta_ref, k0, k1, k2, v0, v1, v2, bias,
    dq_ref, out0, out1, out2, p_ref, ds_ref, *, chunk,
):
    block, depth = k0.shape
    scale = depth**-0.5
    factor = scale * LOG2E
    step, h = pl.program_id(0), pl.program_id(1)
    here = pl.ds(pl.multiple_of(h * depth, depth), depth)
    q = q_ref[here, :]
    do = do_ref[here, :]
    lse = lse_ref[h, 0:1, :]
    delta = delta_ref[h, 0:1, :]
    total = jnp.zeros(q.shape, F32)
    for w, (keys, values, out) in enumerate(((k0, v0, out0), (k1, v1, out1), (k2, v2, out2))):
        for start in range(0, block, chunk):
            part = slice(start, start + chunk)
            p = jnp.exp2(dot(keys[part, :], q, 1, 0) * factor + bias[w, part, :] - lse)
            ds = p * (dot(values[part, :], do, 1, 0) - delta)
            p_ref[part, :] = p.astype(BF16)
            ds_ref[part, :] = ds.astype(BF16)
            out[0, :, part] = (dot(q, ds_ref[part, :], 1, 1) * scale).astype(out.dtype)
            out[1, :, part] = dot(do, p_ref[part, :], 1, 1).astype(out.dtype)
            total = total + dot(keys[part, :], ds_ref[part, :], 0, 0)

    @pl.when(step == 0)
    def _():
        dq_ref[here, :] = total * scale

    @pl.when(step > 0)
    def _():
        dq_ref[here, :] += total * scale


def hand_out(core, value, keep_ref, send_ref, columns):
    bands, rows = keep_ref.shape[1:3]
    for parity in range(2):

        @pl.when(core == parity)
        def _(parity=parity):
            for band in range(bands):
                for side, ref in ((parity, keep_ref), (1 - parity, send_ref)):
                    at = (2 * band + side) * rows
                    ref[0, band, :, columns] = value[at : at + rows].astype(ref.dtype)


def turn(pairs):
    @pl.when(pl.program_id(0) == 0)
    def _():
        for ref, kept in pairs:
            kept[...] = ref[...].T


def weights_kernel(places, normed, rounded, before, active, keep_ref, send_ref, normed_turned, rounded_turned):
    size = before.shape[1]
    turn(((normed, normed_turned), (rounded, rounded_turned)))
    hand_out(places[2], dot(normed_turned[...], before[...], 1, 0), keep_ref, send_ref, slice(0, size))
    hand_out(places[2], dot(rounded_turned[...], active[...], 1, 0), keep_ref, send_ref, slice(size, 2 * size))


def down_weights_kernel(
    places, rounded, active, normed_attn, project, attended, branch, keep_ref, send_ref, rounded_turned, normed_turned
):
    quarter = pl.program_id(0)
    size = active.shape[1]
    turn(((rounded, rounded_turned), (normed_attn, normed_turned)))
    hand_out(places[2], dot(rounded_turned[...], active[...], 1, 0), keep_ref, send_ref, slice(0, size))
    columns = slice(size, size + normed_attn.shape[1])

    @pl.when(quarter < 3)
    def _():
        hand_out(places[2], dot(normed_turned[...], project[...], 1, 1), keep_ref, send_ref, columns)

    @pl.when(quarter == 3)
    def _():
        hand_out(places[2], dot(attended[...], branch[...], 1, 0), keep_ref, send_ref, columns)


def up_weights_kernel(places, normed, before, table_in, table_direct, table_out, gain, keep_ref, send_ref, normed_turned):
    quarter = pl.program_id(0)
    size = before.shape[1]
    turn(((normed, normed_turned),))
    hand_out(places[2], dot(normed_turned[...], before[...], 1, 0), keep_ref, send_ref, slice(0, size))
    columns = slice(size, size + table_in.shape[1])

    @pl.when(quarter == 0)
    def _():
        hand_out(places[2], table_in[...] + table_direct[...], keep_ref, send_ref, columns)

    for index, ref in ((1, table_out), (2, gain)):

        @pl.when(quarter == index)
        def _(ref=ref):
            hand_out(places[2], ref[...], keep_ref, send_ref, columns)

    @pl.when(quarter == 3)
    def _():
        hand_out(places[2], jnp.zeros(table_in.shape, F32), keep_ref, send_ref, columns)


def item_kernel(places, *refs, pairs, exact):
    ins, outs = refs[: 2 * pairs], refs[2 * pairs :]
    step = pl.program_id(0)
    for index, out in enumerate(outs):

        @pl.when(step == index)
        def _(index=index, out=out):
            start = 0
            for pair in range(pairs):
                keep, came = ins[2 * pair : 2 * pair + 2]
                value = keep[0] + came[0]
                size = value.shape[-1]
                out[:, :, start : start + size] = value.astype(out.dtype)
                if index > 0 and exact and pair == pairs - 1:
                    part = value[:, :, size - exact :]
                    rest = part - part.astype(out.dtype).astype(F32)
                    out[:, :, start + size : start + size + exact] = rest.astype(out.dtype)
                start += size


def band_kernel(places, *refs, groups, count, exact):
    ins, outs = refs[: groups * (1 + count)], refs[groups * (1 + count) :]
    step = pl.program_id(0)
    start = 0
    for group in range(groups):
        own, *came = ins[group * (1 + count) : (group + 1) * (1 + count)]
        size = own.shape[-1]
        total = own[0]
        for ref in came:
            total = total + ref[0, :, :size].astype(F32)
        last = exact and group == groups - 1
        if last:
            part = total[:, size - exact :] + sum(ref[0, :, size:].astype(F32) for ref in came)
            high = part.astype(BF16)
            rest = (part - high.astype(F32)).astype(BF16)
        for index, out in enumerate(outs):

            @pl.when(step == index)
            def _(index=index, out=out):
                out[:, start : start + size] = total.astype(out.dtype)
                if last and index == 0:
                    out[:, start + size - exact : start + size] = part
                elif last:
                    out[:, start + size - exact : start + size] = high
                    out[:, start + size : start + size + exact] = rest

        start += size


def exchange(value, axis, distance):
    size = lax.axis_size(axis)
    return lax.ppermute(value, axis, [(i, i ^ distance) for i in range(size)])


def prefetched(kernel, grid, outs, in_specs, out_specs, places, operands, moved, weight=1):
    return pl.pallas_call(
        kernel,
        grid_spec=pltpu.PrefetchScalarGridSpec(
            num_scalar_prefetch=1, grid=grid, in_specs=in_specs, out_specs=out_specs
        ),
        out_shape=outs,
        cost_estimate=pl.CostEstimate(flops=moved * WEIGH * weight, bytes_accessed=moved * WEIGH, transcendentals=0),
        compiler_params=pltpu.CompilerParams(vmem_limit_bytes=VMEM_BYTES * 2 // 3),
    )(places, *[far(x) for x in operands])


def sort_shares(keeps, sends, places, exact=0, late=()):
    items = lax.axis_size("item")
    came = [exchange(send, "lat", 1) for send in sends]
    quarters, bands, rows, _ = keeps[0].shape
    size = sum(keep.shape[-1] for keep in keeps)
    wide = size + exact
    operands = [after(x, *late) for pair in zip(keeps, came) for x in pair]
    return prefetched(
        functools.partial(item_kernel, pairs=len(keeps), exact=exact),
        (items,),
        [shape((bands, rows, size), F32)] + [shape((bands, rows, wide), BF16)] * (items - 1),
        [pl.BlockSpec((1,) + x.shape[1:], lambda j, s: (s[3] ^ j, 0, 0, 0)) for x in operands],
        [pl.BlockSpec((bands, rows, size), lambda j, s: (0, 0, 0))]
        + [pl.BlockSpec((bands, rows, wide), lambda j, s: (0, 0, 0))] * (items - 1),
        places,
        operands,
        moved=14 * bands * rows * size * items,
    )


def swap_items(sorted_shares):
    own, *others = sorted_shares
    return [own] + [exchange(x, "item", k + 1) for k, x in enumerate(others)]


def sum_items(groups, places, exact=0):
    items = len(groups[0])
    bands, rows, _ = groups[0][0].shape
    operands = [x for group in groups for x in group]
    size = sum(group[0].shape[-1] for group in groups)
    wide = size + exact
    return prefetched(
        functools.partial(band_kernel, groups=len(groups), count=items - 1, exact=exact),
        (bands,),
        [shape((rows, size), F32)] + [shape((rows, wide), BF16)] * (bands - 1),
        [pl.BlockSpec((1,) + x.shape[1:], lambda j, s: (s[4] ^ j, 0, 0)) for x in operands],
        [pl.BlockSpec((rows, size), lambda j, s: (0, 0))]
        + [pl.BlockSpec((rows, wide), lambda j, s: (0, 0))] * (bands - 1),
        places,
        operands,
        moved=14 * bands * rows * size,
        weight=10000,
    )


def sum_bands(parts, exact=0, late=()):
    own, *others = parts
    size = own.shape[-1]
    came = [exchange(x, "lat", 2 * (k + 1)) for k, x in enumerate(others)]
    total = after(own, *late) if late else own
    for x in came:
        total = total + x[:, :size].astype(F32)
    if exact:
        rest = sum(x[:, size:].astype(F32) for x in came)
        total = jnp.concatenate([total[:, : size - exact], total[:, size - exact :] + rest], axis=1)
    return total


def after(value, *others):
    result = lax.optimization_barrier((value, *others))[0]
    if is_far(value):
        FAR.append(result)
    return result


def total_kernel(own, *refs):
    *came, out0, out1 = refs
    total = own[...]
    for ref in came:
        total = total + ref[...].astype(F32)
    half = out0.shape[-1]
    out0[...] = total[:, :half]
    out1[...] = total[:, half:]


def add_bands(parts, late):
    own, *others = parts
    came = [exchange(x, "lat", 2 * (k + 1)) for k, x in enumerate(others)]
    return call(
        total_kernel,
        (1,),
        [shape((own.shape[0], own.shape[1] // 2), F32)] * 2,
        [whole(own.shape)] * len(parts),
        [whole((own.shape[0], own.shape[1] // 2))] * 2,
        (after(own, *late), *came),
        flops=10**11,
        moved=16 * own.size,
        near=(0, 1),
    )


def all_items(one, two):
    one_near, two_far = exchange(one, "item", 1), exchange(two, "item", 2)
    one_far, two_near = exchange(one, "item", 2), exchange(two, "item", 1)
    return [
        (one, two), (one_near, two_near), (one_far, two_far),
        (exchange(one_near, "item", 2), exchange(two_far, "item", 1)),
    ]


def sum_over(value, axis):
    distance = 1
    while distance < lax.axis_size(axis):
        value = value + exchange(value, axis, distance)
        distance *= 2
    return value


def adam_kernel(places, factor, *refs):
    dec, proc, down, up, whole_up = (refs[4 * i : 4 * i + 4] for i in range(5))
    mlp, attn, tables, gains = (refs[20 + 4 * i : 24 + 4 * i] for i in range(4))
    mlp_out, attn_out, tables_out, gains_out = (refs[36 + 5 * i : 41 + 5 * i] for i in range(4))
    size = down[0].shape[-1] - attn[0].shape[-1] // 4
    part = attn[0].shape[-1] // 4
    scale = factor[0]
    block, layer = pl.program_id(0), pl.program_id(1)

    def update(share, state, new_state, at, rate, decay):
        new = adam_update(scale * share, *(ref[at] for ref in state), rate, decay)
        for ref, value in zip(new_state, new):
            ref[at] = value

    for k in range(4):
        quarter = places[3] ^ k
        for index, sides in enumerate(((up, down), (proc, proc), (dec, dec))):

            @pl.when(layer == index)
            def _(k=k, index=index, sides=sides, quarter=quarter):
                for side, shares in enumerate(sides):
                    start = 0 if index == 0 else side * size
                    columns = pl.ds(pl.multiple_of((4 * side + quarter) * size, size), size)
                    share = shares[k][:, start : start + size]
                    update(share, mlp, mlp_out, (0, slice(None), columns), RATE_MATRIX, WEIGHT_DECAY)

        @pl.when(layer == 0)
        def _(k=k, quarter=quarter):
            columns = pl.ds(pl.multiple_of(quarter * part, part), part)
            update(down[k][:, size:], attn, attn_out, (slice(None), columns), RATE_MATRIX, WEIGHT_DECAY)

        small = (layer == 0) & (block == 0)
        for table in range(2):

            @pl.when(small & (quarter == table))
            def _(k=k, table=table):
                share = whole_up[k][:, size : size + tables[0].shape[-1]]
                update(share, tables, tables_out, (table,), RATE_MATRIX, WEIGHT_DECAY)

        @pl.when(small & (quarter == 2))
        def _(k=k):
            turned = whole_up[k][:, size:].T[: gains[0].shape[0]]
            update(turned, gains, gains_out, (slice(None),), RATE_GAIN, 0.0)


def projection_back_kernel(
    dq0, dq1, left0, left1, own0, own1, right0, right1, grad_residual, encoded, gains, attn,
    upstream_ref, rounded_ref, project_ref, gain_ref,
):
    pairs = [
        own[...] + left[...].astype(F32) + right[...].astype(F32)
        for left, own, right in ((left0, own0, right0), (left1, own1, right1))
    ]
    project = jnp.concatenate(
        [dq0[...], dq1[...], pairs[0][0], pairs[1][0], pairs[0][1], pairs[1][1]], axis=0
    ).astype(BF16)
    project_ref[...] = project
    grad_normed = dot(project, attn[...], 0, 1)
    grad_encoded, gain_attn = norm_back(grad_normed, encoded[...], gains[1:2])
    upstream = grad_residual[...] + grad_encoded
    upstream_ref[...] = upstream
    rounded_ref[...] = upstream.astype(BF16)
    add_up(gain_ref, gain_attn)


def encoder_back_kernel(
    upstream, pooled, slope, gains, mlp, pin, before_ref, table_ref, gain_ref, rounded_ref
):
    grad_pooled, gain_enc = mlp_backward(
        upstream[...], pooled[...], gains[0:1], mlp, slope, rounded_ref, before_ref
    )
    add_up(gain_ref, gain_enc)
    high, low = two_parts(grad_pooled)
    both = dot(high, pin[...], 0, 0) + dot(low, pin[...], 0, 0)
    channels = both.shape[1] // 2
    add_up(table_ref, both[:, :channels] + both[:, channels:])


def weights(kernel, places, operands, specs, columns, flops, turned):
    rows, width = operands[0].shape
    bands = lax.axis_size("lat") // 2
    out = shape((4, bands, width // (2 * bands), columns), F32)
    out_spec = pl.BlockSpec((1,) + out.shape[1:], lambda i: (i, 0, 0, 0))
    return call(
        kernel,
        (4,),
        [out, out],
        [pl.BlockSpec(memory_space=pltpu.SMEM)] + specs,
        [out_spec, out_spec],
        (places, *operands),
        flops=flops,
        moved=8 * width * columns * 4,
        scratch=[pltpu.VMEM((width, rows), BF16)] * turned,
        vmem=VMEM_BYTES * 2 // 3,
        near=(0, 1),
    )


def adam_update(gradient, master, moment_one, moment_two, average, step_rate, decay_rate):
    one_new = BETA_ONE * moment_one + (1.0 - BETA_ONE) * gradient
    two_new = BETA_TWO * moment_two + (1.0 - BETA_TWO) * gradient * gradient
    one_hat = one_new * (1.0 / (1.0 - BETA_ONE**STEP))
    two_hat = two_new * (1.0 / (1.0 - BETA_TWO**STEP))
    master_new = master - step_rate * (
        one_hat / (jnp.sqrt(two_hat) + ADAM_EPS) + decay_rate * master
    )
    average_new = EMA_DECAY * average + (1.0 - EMA_DECAY) * master_new
    return (one_new, two_new, master_new, average_new, master_new.astype(jnp.bfloat16))


def from_sides(to_left, to_right):
    size = lax.axis_size("lat")
    up = [(i, (i + 1) % size) for i in range(size - 1)]
    down = [(j, i) for i, j in up]
    return lax.ppermute(to_right, "lat", up), lax.ppermute(to_left, "lat", down)


def shards(
    noisy_state,
    target_state,
    sigmas,
    sh_basis,
    lengths,
    grid_edges,
    mesh_edges,
    dec_edges,
    tables_copy,
    tables_master,
    tables_first,
    tables_second,
    tables_ema,
    attn_copy,
    attn_master,
    attn_first,
    attn_second,
    attn_ema,
    mlp_copy,
    mlp_master,
    mlp_first,
    mlp_second,
    mlp_ema,
    gains_copy,
    gains_master,
    gains_first,
    gains_second,
    gains_ema,
):
    FAR.clear()
    band_index = lax.axis_index("lat")
    bands = lax.axis_size("lat")
    item_index = lax.axis_index("item")
    places = jnp.stack([band_index, bands, band_index % 2, item_index, band_index // 2]).astype(jnp.int32)
    rows = mesh_edges.shape[0]
    grid_rows = noisy_state.shape[2]
    width = attn_copy.shape[0]
    channels = noisy_state.shape[1]
    padded = CHANNEL_PAD
    hidden = mlp_copy.shape[2] // 2
    depth = width // HEADS
    FAR.extend([mlp_copy, attn_copy, mlp_master, mlp_first, mlp_second, mlp_ema])
    FAR.extend([attn_master, attn_first, attn_second, attn_ema])
    gains = gains_copy.astype(F32)
    gain_rows = gains.shape[0]
    noise_level = sigmas[0]
    square = noise_level * noise_level
    scale_in = lax.rsqrt(square + 1.0)
    scale_skip = 1.0 / (square + 1.0)
    scale_out = noise_level * scale_in
    weight_loss = (square + 1.0) / square
    noisy_field = noisy_state[0]
    target_field = target_state[0]
    extra = padded - channels
    inputs = jnp.pad((scale_in * noisy_field).astype(BF16), ((0, extra), (0, 0)))
    tables = jnp.pad(tables_copy, ((0, 0), (0, extra), (0, 0)))

    def weights_spec(index):
        return pl.BlockSpec((1, width, 2 * hidden), lambda *_: (index, 0, 0))

    wout_spec = pl.BlockSpec((width, width), lambda *_: (0, 3))
    few = HEADS // GROUPS
    part = few * depth
    gains_spec = whole(gains.shape)
    tables_spec = whole(tables.shape)
    steps = rows // ROWS
    kept_shapes = [shape((rows, width), BF16), shape((rows, hidden), F32), shape((rows, hidden), BF16)]
    kept_specs = [rows_of(width), rows_of(hidden), rows_of(hidden)]
    mlp_flops = 4 * rows * width * hidden

    pin, pooled, encoded, normed_enc, slope_enc, active_enc, normed_attn, queries, *pairs = call(
        encoder_kernel,
        (steps,),
        [shape((rows, 2 * padded), BF16), shape((rows, width), F32), shape((rows, width), F32)]
        + kept_shapes
        + [shape((rows, width), BF16), shape((width, rows), BF16)]
        + [shape((rows, width), BF16)] * GROUPS,
        [
            lanes_of(grid_edges.shape[1]), whole((padded, grid_rows)), tables_spec, gains_spec,
            weights_spec(0), pl.BlockSpec((width, 3 * width), lambda i: (0, 0)),
        ],
        [rows_of(2 * padded), rows_of(width), rows_of(width)]
        + kept_specs
        + [rows_of(width), lanes_of(width)]
        + [rows_of(width)] * GROUPS,
        (grid_edges.T, inputs, tables, gains, mlp_copy, attn_copy),
        flops=mlp_flops + 6 * rows * width * width,
        moved=30 * rows * width,
    )

    crops = lengths.shape[1]
    smem = pl.BlockSpec(memory_space=pltpu.SMEM)
    bias_lanes = 128
    bias = call(
        functools.partial(bias_kernel, crops=crops),
        (rows // bias_lanes,),
        shape((3, rows, rows), F32),
        [smem, smem, lanes_of(mesh_edges.shape[1], bias_lanes)],
        pl.BlockSpec((3, rows, bias_lanes), lambda i: (0, 0, i)),
        (places, jnp.cumsum(lengths[0]), mesh_edges.T),
        flops=2 * 10**9,
        moved=12 * rows * rows,
    )

    windows = []
    for own in pairs:
        if windows:
            own = after(own, *windows[-1], bias)
        came = from_sides(own, own)
        windows.append([came[0], own, came[1]])

    lanes = 512
    attended, lse = [], []
    for g, window in enumerate(windows):
        result, logs = call(
            functools.partial(attend_kernel, chunk=256),
            (rows // lanes, few),
            [shape((part, rows), F32), shape((few, 8, rows), F32)],
            [pl.BlockSpec((depth, lanes), lambda i, h, g=g: (g * few + h, i))]
            + [pl.BlockSpec((rows, depth), lambda i, h: (0, h))] * 3
            + [pl.BlockSpec((rows, depth), lambda i, h: (0, few + h))] * 3
            + [pl.BlockSpec((3, rows, lanes), lambda i, h: (0, 0, i))],
            [
                pl.BlockSpec((depth, lanes), lambda i, h: (h, i)),
                pl.BlockSpec((1, 8, lanes), lambda i, h: (h, 0, i)),
            ],
            (queries, *window, *window, bias),
            scratch=[pltpu.VMEM((3, rows, lanes), F32)],
            flops=24 * rows * rows * part,
            moved=12 * rows * rows,
        )
        attended.append(result)
        lse.append(logs)

    rounded_o, residual, normed_proc, slope_proc, active_proc, sent = call(
        processor_kernel,
        (steps,),
        [shape((width, rows), BF16), shape((rows, width), F32)] + kept_shapes + [shape((rows, width), BF16)],
        [lanes_of(part)] * GROUPS + [rows_of(width), gains_spec, weights_spec(1), wout_spec],
        [lanes_of(width), rows_of(width)] + kept_specs + [rows_of(width)],
        (*attended, encoded, gains, mlp_copy, attn_copy),
        flops=mlp_flops + 2 * rows * width * width,
        moved=24 * rows * width,
        near=(5,),
    )

    before_sent, after_sent = from_sides(sent, sent)

    dec_count = dec_edges.shape[1]
    tally, partial = call(
        window_kernel,
        (grid_rows // ROWS,),
        [shape((3, rows, grid_rows), BF16), shape((grid_rows, width), F32)],
        [lanes_of(dec_count), whole((rows, width)), lanes_of(padded), tables_spec],
        [pl.BlockSpec((3, rows, ROWS), lambda i: (0, 0, i)), rows_of(width)],
        (dec_edges.T, sent, inputs, tables),
        flops=2 * rows * rows * width,
        moved=24 * rows * width,
    )
    joined, normed_dec, slope_dec, active_dec, decoded, final, output = call(
        functools.partial(decoder_kernel, count=dec_count),
        (grid_rows // ROWS,),
        [shape((grid_rows, width), F32)]
        + kept_shapes
        + [shape((grid_rows, width), F32), shape((grid_rows, width), BF16), shape((padded, grid_rows), F32)],
        [
            pl.BlockSpec((3, rows, ROWS), lambda i: (0, 0, i)), whole((rows, width)), whole((rows, width)),
            rows_of(width), tables_spec, gains_spec, weights_spec(2),
        ],
        [rows_of(width)] + kept_specs + [rows_of(width), rows_of(width), lanes_of(padded)],
        (tally, before_sent, after_sent, partial, tables, gains, mlp_copy),
        flops=mlp_flops + 6 * rows * rows * width,
        moved=24 * rows * width,
    )

    error_field = scale_skip * noisy_field + scale_out * output[:channels] - target_field
    partial_value = lax.dot_general(
        error_field,
        sh_basis,
        (((1,), (1,)), ((), ())),
        precision=HIGH_PRECISION,
        preferred_element_type=F32,
    )
    coeffs = sum_over(partial_value, "lat")
    slice_width = coeffs.shape[1] // bands
    own_coeffs = lax.dynamic_slice_in_dim(coeffs, band_index * slice_width, slice_width, 1)
    loss_item = weight_loss * jnp.sum(own_coeffs * own_coeffs)
    grad_error = jnp.dot(
        2.0 * weight_loss * coeffs, sh_basis, precision=HIGH_PRECISION, preferred_element_type=F32
    )
    grad_output = jnp.pad((scale_out * grad_error).astype(BF16), ((0, extra), (0, 0)))

    join_high, join_low, rounded_dec, before_dec, table_out, gain_dec, table_direct = call(
        decoder_back_kernel,
        (grid_rows // ROWS,),
        [
            shape((grid_rows, width), BF16), shape((grid_rows, width), BF16), shape((grid_rows, width), BF16),
            shape((grid_rows, hidden), BF16), shape((width, padded), F32), shape((2, width), F32),
            shape((width, padded), F32),
        ],
        [
            lanes_of(padded), tables_spec, rows_of(width), rows_of(width), rows_of(width), rows_of(hidden),
            gains_spec, weights_spec(2), lanes_of(padded),
        ],
        [
            rows_of(width), rows_of(width), rows_of(width), rows_of(hidden), whole((width, padded)),
            whole((2, width)), whole((width, padded)),
        ],
        (grad_output, tables, decoded, final, joined, slope_dec, gains, mlp_copy, inputs),
        flops=mlp_flops,
        moved=24 * rows * width,
        near=(0, 1, 2),
    )

    to_left, grad_own, to_right = call(
        scatter_kernel,
        (steps,),
        [shape((rows, width), BF16), shape((rows, width), F32), shape((rows, width), BF16)],
        [whole((dec_count, grid_rows)), whole((grid_rows, width)), whole((grid_rows, width))],
        [rows_of(width)] * 3,
        (dec_edges.T, join_high, join_low),
        near=(0, 1, 2),
        flops=12 * rows * grid_rows * width,
        moved=12 * rows * width,
    )
    from_left, from_right = from_sides(to_left, to_right)
    quarter = hidden // 4
    columns_of = pl.BlockSpec((rows, quarter), lambda i: (0, i))
    table_spec = whole((width, padded))
    full = whole((rows, width))
    product = 2 * rows * width * width

    def layer_weights(*operands):
        return weights(
            weights_kernel, places, operands, [full, full, columns_of, columns_of], 2 * quarter, 8 * product, 2
        )

    keep_dec, send_dec = layer_weights(normed_dec, after(rounded_dec, to_left, to_right), before_dec, active_dec)
    sorted_dec = sort_shares([keep_dec], [send_dec], places)
    swapped_dec = swap_items(sorted_dec)

    grad_residual, rounded_proc, before_proc, gain_proc, branch, grad_o, delta = call(
        processor_back_kernel,
        (steps,),
        [
            shape((rows, width), F32), shape((rows, width), BF16), shape((rows, hidden), BF16),
            shape((1, width), F32), shape((rows, width), BF16), shape((width, rows), BF16),
            shape((HEADS, 8, rows), F32),
        ],
        [rows_of(width)] * 4 + [rows_of(hidden), gains_spec, weights_spec(1), wout_spec] + [lanes_of(part)] * GROUPS,
        [
            rows_of(width), rows_of(width), rows_of(hidden), whole((1, width)), rows_of(width), lanes_of(width),
            pl.BlockSpec((HEADS, 8, ROWS), lambda i: (0, 0, i)),
        ],
        (from_left, after(grad_own, keep_dec, send_dec), from_right, residual, slope_proc, gains, mlp_copy, attn_copy,
            *attended,
        ),
        flops=mlp_flops + 2 * rows * width * width,
        moved=24 * rows * width,
        near=(1, 5),
    )

    block = 512
    side = pl.BlockSpec((2, depth, block), lambda i, h: (0, h, i))
    group_spec = whole((few, 8, rows))
    grad_queries, sides = [], []
    ahead = tuple(sorted_dec)
    for g, window in enumerate(windows):
        row_spec = pl.BlockSpec((part, rows), lambda i, h, g=g: (g, 0))
        dq, left, own, right = call(
            functools.partial(attend_back_kernel, chunk=256),
            (rows // block, few),
            [
                shape((part, rows), F32), shape((2, part, rows), BF16), shape((2, part, rows), F32),
                shape((2, part, rows), BF16),
            ],
            [row_spec, row_spec, group_spec, pl.BlockSpec((few, 8, rows), lambda i, h, g=g: (g, 0, 0))]
            + [pl.BlockSpec((block, depth), lambda i, h: (i, h))] * 3
            + [pl.BlockSpec((block, depth), lambda i, h: (i, few + h))] * 3
            + [pl.BlockSpec((3, block, rows), lambda i, h: (0, i, 0))],
            [whole((part, rows)), side, side, side],
            (queries, after(grad_o, *ahead), lse[g], delta, *window, *window, bias),
            scratch=[pltpu.VMEM((block, rows), BF16), pltpu.VMEM((block, rows), BF16)],
            flops=60 * rows * rows * part,
            moved=12 * rows * rows,
        )
        if sides:
            left, right = after(left, *sides[-1]), after(right, *sides[-1])
        came = from_sides(left, right)
        sides.append([came[0], own, came[1]])
        grad_queries.append(dq)
        ahead = tuple(swapped_dec)

    keep_proc, send_proc = layer_weights(normed_proc, after(rounded_proc, left, right), before_proc, active_proc)
    side_spec = pl.BlockSpec((2, part, ROWS), lambda i: (0, 0, i))
    upstream, rounded_enc, project, gain_attn = call(
        projection_back_kernel,
        (steps,),
        [
            shape((rows, width), F32), shape((rows, width), BF16), shape((3 * width, rows), BF16),
            shape((1, width), F32),
        ],
        [lanes_of(part)] * 2 + [side_spec] * 6
        + [rows_of(width)] * 2 + [gains_spec, pl.BlockSpec((width, 3 * width), lambda i: (0, 0))],
        [rows_of(width), rows_of(width), lanes_of(3 * width), whole((1, width))],
        (
            *grad_queries, sides[0][0], sides[1][0], sides[0][1], sides[1][1], sides[0][2], sides[1][2],
            after(grad_residual, keep_proc, send_proc), encoded, gains, attn_copy,
        ),
        flops=3 * product,
        moved=24 * rows * width,
        near=(0, 1, 2),
    )
    sorted_proc = sort_shares([keep_proc], [send_proc], places, late=(upstream,))
    swapped_proc = swap_items(sorted_proc)
    keep_down, send_down = weights(
        down_weights_kernel,
        places,
        (after(rounded_enc, *sorted_proc), active_enc, normed_attn, project, rounded_o, branch),
        [full, columns_of, full, pl.BlockSpec((width, rows), lambda i: (jnp.minimum(i, 2), 0)), whole((width, rows)), full],
        quarter + width,
        8 * product,
        2,
    )
    sorted_down = sort_shares([keep_down], [send_down], places)
    before_enc, table_in, gain_enc, _ = call(
        encoder_back_kernel,
        (steps,),
        [
            shape((rows, hidden), BF16), shape((width, padded), F32), shape((1, width), F32),
            shape((rows, width), BF16),
        ],
        [rows_of(width)] * 2
        + [rows_of(hidden), gains_spec, weights_spec(0), rows_of(2 * padded)],
        [rows_of(hidden), table_spec, whole((1, width)), rows_of(width)],
        (after(upstream, *sorted_down), pooled, slope_enc, gains, mlp_copy, pin),
        flops=mlp_flops,
        moved=24 * rows * width,
    )
    grad_gains = jnp.concatenate([gain_enc, gain_attn, gain_proc, gain_dec], axis=0)
    gain_columns = jnp.pad(grad_gains.T, ((0, 0), (0, padded - gain_rows)))
    swapped_down = swap_items([sorted_down[0]] + [after(x, *swapped_proc, before_enc) for x in sorted_down[1:]])
    own_proc = [after(swapped_proc[0], before_enc)] + swapped_proc[1:]
    first_parts = sum_items([swapped_dec, own_proc], places)
    first_total = add_bands(first_parts, (first_parts[0],))
    keep_up, send_up = weights(
        up_weights_kernel,
        places,
        (normed_enc, after(before_enc, first_parts[0]), table_in, table_direct, table_out, gain_columns),
        [full, columns_of, table_spec, table_spec, table_spec, table_spec],
        quarter + padded,
        4 * product,
        1,
    )
    down_parts = sum_items([swapped_down], places)
    down_total = sum_bands(down_parts)
    sorted_up = sort_shares([keep_up], [send_up], places, exact=padded, late=(down_parts[0], *first_total))
    swapped_up = swap_items([sorted_up[0]] + [after(x, *swapped_down) for x in sorted_up[1:]])
    first_all = all_items(*[after(x, sorted_up[0]) for x in first_total])
    ready = [x for pair in first_all[:3] for x in pair]
    up_total = sum_bands(sum_items([swapped_up], places, exact=padded), exact=padded)
    squares = sum(jnp.sum(jnp.square(x.astype(F32))) for x in (*first_total, down_total, up_total))
    scalars = sum_over(jnp.stack([squares, loss_item])[None], "lat")
    place = [lax.broadcasted_iota(jnp.int32, up_total.shape, dim) for dim in range(2)]
    carried = jnp.where(place[0] == 0, scalars[0, 0], scalars[0, 1])
    up_total = jnp.where((place[1] == up_total.shape[1] - 1) & (place[0] < 2), carried, up_total)
    last_all = all_items(after(down_total, *ready), after(up_total, *ready))
    scalars = [x[:2, -1] for _, x in last_all]
    scalars = (scalars[0] + scalars[1]) + (scalars[2] + scalars[3])
    loss_sum = scalars[1]
    grad_norm = jnp.sqrt(scalars[0])
    scale_factor = CLIP_LEVEL / jnp.maximum(grad_norm, CLIP_LEVEL)

    shard_rows = attn_master.shape[0]
    block_rows = min(shard_rows, 32)
    mlp_spec = pl.BlockSpec((1, block_rows, 2 * hidden), lambda r, l, s: (l, r, 0))
    attn_part = pl.BlockSpec((block_rows, attn_master.shape[1]), lambda r, l, s: (r, 0))
    kinds = [F32, F32, F32, F32, BF16]
    shares = [x for pair in zip(*first_all) for x in pair] + [x for pair in zip(*last_all) for x in pair]
    state = (mlp_master, mlp_first, mlp_second, mlp_ema, attn_master, attn_first, attn_second, attn_ema)
    table_state = [jnp.swapaxes(x, 1, 2) for x in (tables_master, tables_first, tables_second, tables_ema)]
    FAR.extend([*table_state, *shares])
    updated = prefetched(
        adam_kernel,
        (shard_rows // block_rows, mlp_master.shape[0]),
        [shape(x.shape, kind) for x in (mlp_master, attn_master, table_state[0], gains_master) for kind in kinds],
        [smem]
        + [pl.BlockSpec((block_rows, x.shape[1]), lambda r, l, s: (r, 0)) for x in shares]
        + [pl.BlockSpec(x.shape, lambda *_: (0, 0)) for x in shares[-4:]]
        + [mlp_spec] * 4
        + [attn_part] * 4
        + [whole(table_state[0].shape)] * 4
        + [whole(gains_master.shape)] * 4,
        [mlp_spec] * 5 + [attn_part] * 5 + [whole(table_state[0].shape)] * 5 + [whole(gains_master.shape)] * 5,
        places,
        (
            scale_factor[None], *shares, *shares[-4:], *state, *table_state,
            gains_master, gains_first, gains_second, gains_ema,
        ),
        moved=34 * (mlp_master.size + attn_master.size),
    )
    mlps, att, gns = updated[:5], updated[5:10], updated[15:]
    tab = [jnp.swapaxes(x, 1, 2) for x in updated[10:15]]
    return (loss_sum, grad_norm, *tab, *att, *mlps, *gns)


def solution(mesh):
    table = P(None, None, "lat")
    attn = P("lat", None)
    mlp = P(None, "lat", None)
    gain = P(None, "lat")
    placed = (
        P("item", None, "lat"),
        P("item", None, "lat"),
        P("item"),
        P(None, "lat"),
        P("item", None),
        P("lat", None),
        P("lat", None),
        P("lat", None),
        P(), table, table, table, table,
        P(), attn, attn, attn, attn,
        P(), mlp, mlp, mlp, mlp,
        P(), gain, gain, gain, gain,
    )
    return jax.shard_map(
        shards,
        mesh=mesh,
        in_specs=placed,
        out_specs=(P(), P(), *([table] * 5), *([attn] * 5), *([mlp] * 5), *([gain] * 5)),
        check_vma=False,
    )
```
